32 devices in a mesh: gy: 4 (over y, x), gz: 8 (over z, core).
Axes of the slice: x: 2, y: 2, z: 4, core: 2. Of those that a mesh axis runs over, the one named last changes fastest.
Arguments:
- density: float32 [32, 96, 1024], P(None, 'gy', 'gz'), may hold values from 1 to 2
- momentum: float32 [3, 32, 96, 1024], P(None, None, 'gy', 'gz'), may hold values from -0.5 to 0.5
- energy: float32 [32, 96, 1024], P(None, 'gy', 'gz'), may hold values from 3 to 5
Outputs:
- density_out: float32 [32, 96, 1024], P(None, 'gy', 'gz')
- momentum_out: float32 [3, 32, 96, 1024], P(None, None, 'gy', 'gz')
- energy_out: float32 [32, 96, 1024], P(None, 'gy', 'gz')
The draws below stay inside these ranges and needn't reach their ends.
All inputs are finite; a program needn't handle non-finite values.
Results may differ from the reference program's by a relative error of at most 0.0003.
Values sent between devices are 32-bit elements; how exact they have to be, the bound alone decides.
No kernel may reach another device: no remote copies, remote signals or barrier semaphores. Data moves between devices by JAX's collectives and lax.ppermute only.
A program may use at most 64 MiB of HBM per device.

```python
import jax
import jax.numpy as jnp
from jax import lax

NX = 32
NY = 96
NZ = 1024


def block_scale(key, dims, shards, low, top_value):
    level, own = 1.0, jax.random.fold_in(key, 6)
    for axis_at, parts in shards:
        draws = jnp.exp(jax.random.uniform(jax.random.fold_in(own, axis_at), (parts,), jnp.float32, low / len(shards), top_value / len(shards)))
        level = level * jnp.repeat(draws, dims[axis_at] // parts).reshape([-1 if axis == axis_at else 1 for axis in range(len(dims))])
    return level


def setup_inputs(seed: int = 0) -> dict:
    key_of = jax.random.split(jax.random.key(seed), 4)
    return {
        "density": jnp.clip(1.0 + 1.0 * jax.random.uniform(key_of[0], (NX, NY, NZ), jnp.float32) ** block_scale(key_of[0], (NX, NY, NZ), ((1, 4), (2, 8)), -0.2, 0.2), 1.0, 2.0),
        "momentum": jnp.clip(jax.random.uniform(key_of[1], (3, NX, NY, NZ), jnp.float32, -0.5, 0.5) * block_scale(key_of[1], (3, NX, NY, NZ), ((2, 4), (3, 8)), -0.4, 0.0), -0.5, 0.5),
        "energy": jnp.clip(3.0 + 2.0 * jax.random.uniform(key_of[2], (NX, NY, NZ), jnp.float32) ** block_scale(key_of[2], (NX, NY, NZ), ((1, 4), (2, 8)), -0.2, 0.2), 3.0, 5.0),
    }


adiabatic = 1.4
courant = 0.15

def window(array, start, stop, spatial):
    return lax.slice_in_dim(array, start, stop, axis=spatial)

def limited(first, second):
    signum = jnp.sign(first)
    return signum * jnp.maximum(0.0, jnp.minimum(jnp.abs(first), 2.0 * signum * second))

def primitives(fields):
    density = fields[0]
    velocity = fields[1:4] / density
    kinetic = 0.5 * lax.optimization_barrier(jnp.sum(fields[1:4] * velocity, axis=0))
    pressure = (adiabatic - 1.0) * (fields[4] - kinetic)
    return jnp.concatenate([density[None], velocity, pressure[None]], axis=0)

def physical(prims, normal):
    density = prims[0]
    velocity = prims[1:4]
    pressure = prims[4]
    normal_speed = velocity[normal]
    energy = pressure / (adiabatic - 1.0) + 0.5 * density * lax.optimization_barrier(jnp.sum(velocity * velocity, axis=0))
    momentum = density * velocity
    conserved = jnp.concatenate([density[None], momentum, energy[None]], axis=0)
    carried = [momentum[normal]]
    for component in range(3):
        term = momentum[component] * normal_speed
        if component == normal:
            term = term + pressure
        carried.append(term)
    carried.append((energy + pressure) * normal_speed)
    sound_speed = jnp.sqrt(adiabatic * pressure / density)
    return (conserved, jnp.stack(carried, axis=0), normal_speed, sound_speed)

def advance(padded, spatial, normal):
    length = padded.shape[spatial] - 6
    prims = primitives(padded)
    behind = window(prims, 0, length + 4, spatial)
    middle = window(prims, 1, length + 5, spatial)
    forward = window(prims, 2, length + 6, spatial)
    central = 0.5 * (forward - behind)
    signum = jnp.sign(central)
    bounded = jnp.minimum(jnp.minimum(jnp.abs(central), 2.0 * signum * (middle - behind)), 2.0 * signum * (forward - middle))
    slopes = signum * jnp.maximum(0.0, bounded)
    lower_cell = window(prims, 1, length + 4, spatial)
    upper_cell = window(prims, 2, length + 5, spatial)
    edges = 0.5 * (lower_cell + upper_cell) - (window(slopes, 1, length + 4, spatial) - window(slopes, 0, length + 3, spatial)) / 6.0
    edges = jnp.clip(edges, jnp.minimum(lower_cell, upper_cell), jnp.maximum(lower_cell, upper_cell))
    centre = window(prims, 2, length + 4, spatial)
    downward = centre - window(edges, 0, length + 2, spatial)
    upward = window(edges, 1, length + 3, spatial) - centre
    left_faces = centre - limited(downward, upward)
    right_faces = centre + limited(upward, downward)
    left_state = window(right_faces, 0, length + 1, spatial)
    right_state = window(left_faces, 1, length + 2, spatial)
    held_left, carried_left, speed_left, sound_left = physical(left_state, normal)
    held_right, carried_right, speed_right, sound_right = physical(right_state, normal)
    slowest = jnp.minimum(jnp.minimum(speed_left - sound_left, speed_right - sound_right), 0.0)
    fastest = jnp.maximum(jnp.maximum(speed_left + sound_left, speed_right + sound_right), 0.0)
    fluxes = (fastest * carried_left - slowest * carried_right + slowest * fastest * (held_right - held_left)) / (fastest - slowest)
    interior = window(padded, 3, length + 3, spatial)
    return interior - courant * (window(fluxes, 1, length + 1, spatial) - window(fluxes, 0, length, spatial))

def periodic(fields, spatial):
    count = fields.shape[spatial]
    return jnp.concatenate([window(fields, count - 3, count, spatial), fields, window(fields, 0, 3, spatial)], axis=spatial)

def reference(density, momentum, energy):
    fields = jnp.concatenate([density[None], momentum, energy[None]], axis=0)
    planes = lax.map(lambda section: advance(periodic(section, 1), 1, 0), jnp.moveaxis(fields, 2, 0))
    fields = jnp.moveaxis(planes, 0, 2)
    planes = lax.map(lambda section: advance(periodic(section, 1), 1, 1), jnp.moveaxis(fields, 1, 0))
    fields = jnp.moveaxis(planes, 0, 1)
    planes = lax.map(lambda section: advance(periodic(section, 2), 2, 2), jnp.moveaxis(fields, 2, 0))
    fields = jnp.moveaxis(planes, 0, 2)
    return (fields[0], fields[1:4], fields[4])
```

```python
import jax
import jax.numpy as jnp
from jax import lax
from jax.sharding import PartitionSpec as P

adiabatic = 1.4
courant = 0.15


def window(array, start, stop, spatial):
    return lax.slice_in_dim(array, start, stop, axis=spatial)


def limited(first, second):
    signum = jnp.sign(first)
    return signum * jnp.maximum(0.0, jnp.minimum(jnp.abs(first), 2.0 * signum * second))


def primitives(fields):
    density = fields[0]
    velocity = fields[1:4] / density
    kinetic = 0.5 * jnp.sum(fields[1:4] * velocity, axis=0)
    pressure = (adiabatic - 1.0) * (fields[4] - kinetic)
    return jnp.concatenate([density[None], velocity, pressure[None]], axis=0)


def physical(prims, normal):
    density = prims[0]
    velocity = prims[1:4]
    pressure = prims[4]
    normal_speed = velocity[normal]
    energy = pressure / (adiabatic - 1.0) + 0.5 * density * jnp.sum(velocity * velocity, axis=0)
    momentum = density * velocity
    conserved = jnp.concatenate([density[None], momentum, energy[None]], axis=0)
    carried = [momentum[normal]]
    for component in range(3):
        term = momentum[component] * normal_speed
        if component == normal:
            term = term + pressure
        carried.append(term)
    carried.append((energy + pressure) * normal_speed)
    sound_speed = jnp.sqrt(adiabatic * pressure / density)
    return (conserved, jnp.stack(carried, axis=0), normal_speed, sound_speed)


def advance(padded, spatial, normal):
    length = padded.shape[spatial] - 6
    prims = primitives(padded)
    behind = window(prims, 0, length + 4, spatial)
    middle = window(prims, 1, length + 5, spatial)
    forward = window(prims, 2, length + 6, spatial)
    central = 0.5 * (forward - behind)
    signum = jnp.sign(central)
    bounded = jnp.minimum(
        jnp.minimum(jnp.abs(central), 2.0 * signum * (middle - behind)),
        2.0 * signum * (forward - middle),
    )
    slopes = signum * jnp.maximum(0.0, bounded)
    lower_cell = window(prims, 1, length + 4, spatial)
    upper_cell = window(prims, 2, length + 5, spatial)
    edges = (
        0.5 * (lower_cell + upper_cell)
        - (window(slopes, 1, length + 4, spatial) - window(slopes, 0, length + 3, spatial)) / 6.0
    )
    edges = jnp.clip(
        edges, jnp.minimum(lower_cell, upper_cell), jnp.maximum(lower_cell, upper_cell)
    )
    centre = window(prims, 2, length + 4, spatial)
    downward = centre - window(edges, 0, length + 2, spatial)
    upward = window(edges, 1, length + 3, spatial) - centre
    left_faces = centre - limited(downward, upward)
    right_faces = centre + limited(upward, downward)
    left_state = window(right_faces, 0, length + 1, spatial)
    right_state = window(left_faces, 1, length + 2, spatial)
    held_left, carried_left, speed_left, sound_left = physical(left_state, normal)
    held_right, carried_right, speed_right, sound_right = physical(right_state, normal)
    slowest = jnp.minimum(jnp.minimum(speed_left - sound_left, speed_right - sound_right), 0.0)
    fastest = jnp.maximum(jnp.maximum(speed_left + sound_left, speed_right + sound_right), 0.0)
    fluxes = (
        fastest * carried_left
        - slowest * carried_right
        + slowest * fastest * (held_right - held_left)
    ) / (fastest - slowest)
    interior = window(padded, 3, length + 3, spatial)
    return interior - courant * (
        window(fluxes, 1, length + 1, spatial) - window(fluxes, 0, length, spatial)
    )


def periodic(fields, spatial):
    count = fields.shape[spatial]
    return jnp.concatenate(
        [window(fields, count - 3, count, spatial), fields, window(fields, 0, 3, spatial)],
        axis=spatial,
    )


def halo(fields, axis, spatial):
    ranks = lax.axis_size(axis)
    count = fields.shape[spatial]
    up = [(rank, (rank + 1) % ranks) for rank in range(ranks)]
    down = [((rank + 1) % ranks, rank) for rank in range(ranks)]
    before = lax.ppermute(window(fields, count - 3, count, spatial), axis, up)
    after = lax.ppermute(window(fields, 0, 3, spatial), axis, down)
    return jnp.concatenate([before, fields, after], axis=spatial)


def body(density, momentum, energy):
    fields = jnp.concatenate([density[None], momentum, energy[None]], axis=0)
    fields = advance(periodic(fields, 1), 1, 0)
    fields = advance(halo(fields, "gy", 2), 2, 1)
    fields = advance(halo(fields, "gz", 3), 3, 2)
    return (fields[0], fields[1:4], fields[4])


def solution(mesh):
    return jax.shard_map(
        body,
        mesh=mesh,
        in_specs=(P(None, "gy", "gz"), P(None, None, "gy", "gz"), P(None, "gy", "gz")),
        out_specs=(P(None, "gy", "gz"), P(None, None, "gy", "gz"), P(None, "gy", "gz")),
        check_vma=False,
    )
```

```python
import functools

import jax
import jax.numpy as jnp
from jax import lax
from jax.experimental import pallas as pl
from jax.experimental.pallas import tpu as pltpu
from jax.sharding import PartitionSpec as P

adiabatic = 1.4
courant = 0.15
halo = 3
group = 8


def primitives(fields):
    density, mx, my, mz, energy = fields
    inverse = pl.reciprocal(density, approx=True)
    vx, vy, vz = mx * inverse, my * inverse, mz * inverse
    doubled = mx * vx + my * vy + mz * vz
    pressure = (adiabatic - 1.0) * energy - (0.5 * (adiabatic - 1.0)) * doubled
    return [density, vx, vy, vz, pressure]


def half_slope(ahead, behind):
    top = jnp.maximum(jnp.minimum(ahead, behind), 0.0)
    bottom = jnp.minimum(jnp.maximum(ahead, behind), 0.0)
    return jnp.maximum(jnp.minimum(0.25 * (ahead + behind), top), bottom)


def face_offset(ahead, slope, slope_next):
    offset = 0.5 * ahead - (1.0 / 3.0) * (slope_next - slope)
    return jnp.minimum(jnp.maximum(offset, jnp.minimum(ahead, 0.0)), jnp.maximum(ahead, 0.0))


def limited(first, second):
    doubled = second + second
    return jnp.maximum(jnp.minimum(first, jnp.maximum(doubled, 0.0)), jnp.minimum(doubled, 0.0))


def hll(left, right, normal):
    dl, pl_, ul = left[0], left[4], left[1 + normal]
    dr, pr, ur = right[0], right[4], right[1 + normal]
    tl = adiabatic * pl_
    tr = adiabatic * pr
    al = tl * lax.rsqrt(tl * dl)
    ar = tr * lax.rsqrt(tr * dr)
    slowest = jnp.minimum(jnp.minimum(ul - al, ur - ar), 0.0)
    fastest = jnp.maximum(jnp.maximum(ul + al, ur + ar), 0.0)
    cl = fastest * (courant * pl.reciprocal(fastest - slowest, approx=True))
    cr = courant - cl
    wl = cl * (ul - slowest)
    wr = cr * (ur - fastest)
    ml = wl * dl
    mr = wr * dr
    ql = cl * pl_
    qr = cr * pr
    gl = [ml * left[1 + k] for k in range(3)]
    gr = [mr * right[1 + k] for k in range(3)]
    kinetic = (
        gl[0] * left[1] + gl[1] * left[2] + gl[2] * left[3]
        + gr[0] * right[1] + gr[1] * right[2] + gr[2] * right[3]
    )
    flux = [ml + mr] + [gl[k] + gr[k] for k in range(3)]
    flux[1 + normal] = flux[1 + normal] + (ql + qr)
    inner = (1.0 / (adiabatic - 1.0)) * (wl * pl_ + wr * pr)
    flux.append(0.5 * kinetic + inner + (ql * ul + qr * ur))
    return flux


class Line:
    def __init__(self, load, normal, period=None):
        self.load, self.normal, self.period = load, normal, period
        self.known = {}

    def once(self, name, index, make):
        if self.period is not None:
            index = index % self.period
        if (name, index) not in self.known:
            self.known[(name, index)] = make(index)
        return self.known[(name, index)]

    def prims(self, i):
        return self.once("q", i, lambda i: primitives(self.load(i)))

    def diff(self, i):
        return self.once("d", i, lambda i: [b - a for a, b in zip(self.prims(i), self.prims(i + 1))])

    def slope(self, i):
        return self.once("s", i, lambda i: [half_slope(a, b) for a, b in zip(self.diff(i), self.diff(i - 1))])

    def up(self, i):
        return self.once("u", i, lambda i: [face_offset(d, s, t) for d, s, t in zip(self.diff(i), self.slope(i), self.slope(i + 1))])

    def down(self, i):
        return self.once("w", i, lambda i: [d - u for d, u in zip(self.diff(i - 1), self.up(i - 1))])

    def low(self, i):
        return self.once("l", i, lambda i: [q - limited(w, u) for q, w, u in zip(self.prims(i), self.down(i), self.up(i))])

    def high(self, i):
        return self.once("h", i, lambda i: [q + limited(u, w) for q, w, u in zip(self.prims(i), self.down(i), self.up(i))])

    def flux(self, i):
        return self.once("f", i, lambda i: hll(self.high(i), self.low(i + 1), self.normal))

    def swept(self, i):
        before, after = self.flux(i - 1), self.flux(i)
        return [u - (b - a) for u, a, b in zip(self.load(i), before, after)]


def rolled(fields, ahead, behind, normal):
    states = primitives(fields)
    low, high = [], []
    for q in states:
        d = ahead(q) - q
        s = half_slope(d, behind(d))
        u = face_offset(d, s, ahead(s))
        w = behind(d - u)
        low.append(ahead(q - limited(w, u)))
        high.append(q + limited(u, w))
    return hll(high, low, normal)


def shifts(axis, size):
    return (lambda a: pltpu.roll(a, size - 1, axis), lambda a: pltpu.roll(a, 1, axis))


def x_kernel(density, momentum, energy, out):
    nx, ny, _ = density.shape
    sources = [density, momentum.at[0], momentum.at[1], momentum.at[2], energy]

    @pl.loop(0, ny // 8)
    def _(tile):
        rows = pl.ds(pl.multiple_of(tile * 8, 8), 8)
        line = Line(lambda i: [s[i, rows, :] for s in sources], 0, nx)
        for i in range(nx):
            for f, value in enumerate(line.swept(i)):
                out[f, i, rows, :] = value


def y_kernel(nx, ny, own, before, after, out, edges, ghost):
    lanes = own.shape[-1]
    cells = nx * ny
    ahead, behind = shifts(0, nx)
    for side, source in enumerate((before, after)):

        @pl.loop(0, halo)
        def _(row):
            fields = [source[f, row] for f in range(5)]
            flux = rolled(fields, ahead, behind, 0)
            for f in range(5):
                ghost[f, side * halo + row] = fields[f] - (flux[f] - behind(flux[f]))

    @pl.loop(0, nx // 8)
    def _(tile):
        some = pl.ds(pl.multiple_of(tile * 8, 8), 8)

        def load(i):
            if i < 0:
                return [ghost[f, i + halo, some, :] for f in range(5)]
            if i >= ny:
                return [ghost[f, i - ny + halo, some, :] for f in range(5)]
            return [own[f, pl.ds(tile * (8 * ny) + i, 8, stride=ny), :] for f in range(5)]

        line = Line(load, 1)
        for i in range(ny):
            for f, value in enumerate(line.swept(i)):
                out[f, pl.ds(tile * (8 * ny) + i, 8, stride=ny), :] = value

    pack(nx, ny, lanes, out, edges)


def pack(nx, ny, lanes, source, edges):
    parts = nx * group // lanes
    place = lax.broadcasted_iota(jnp.int32, (ny, lanes), 1) // group

    @pl.loop(0, 5)
    def _(f):
        for j in range(parts):
            packed = None
            for k in range(nx // parts):
                x = k * parts + j
                moved = pltpu.roll(source[f, pl.ds(x * ny, ny), :], k * group + halo, 1)
                packed = moved if packed is None else jnp.where(place == k, moved, packed)
            edges[f, j] = packed


def z_kernel(nx, ny, own, left, right, density, momentum, energy, near, seam):
    lanes = own.shape[-1]
    wide = 2 * group
    parts = nx * group // lanes
    where = lax.broadcasted_iota(jnp.int32, (ny, lanes), 1)
    offset, place = where % wide, where // wide
    ahead, behind = shifts(1, lanes)
    slots = lanes // wide

    @pl.loop(0, 5)
    def _(f):
        for j in range(parts):
            for odd in range(2):
                low, high = left[f, j], right[f, j]
                if odd:
                    low = pltpu.roll(low, lanes - group, 1)
                high = pltpu.roll(high, lanes + 10 - odd * group if odd * group > 10 else 10 - odd * group, 1)
                packed = jnp.where(offset < halo, low, high)
                for k in range(slots):
                    line = own[f, pl.ds(((2 * k + odd) * parts + j) * ny, ny), :]
                    first = pltpu.roll(line, (k * wide + 3) % lanes, 1)
                    last = pltpu.roll(line, (k * wide + 13) % lanes, 1)
                    packed = jnp.where((place == k) & (offset >= 3) & (offset < 8), first, packed)
                    packed = jnp.where((place == k) & (offset >= 8) & (offset < 13), last, packed)
                near[f, j * 2 + odd] = packed

    @pl.loop(0, 2 * parts)
    def _(m):
        flux = rolled([near[f, m] for f in range(5)], ahead, behind, 2)
        for f in range(5):
            seam[f, m] = flux[f]

    outs = [density, momentum.at[0], momentum.at[1], momentum.at[2], energy]
    for k in range(slots):

        @pl.loop(0, 2 * parts)
        def _(m):
            j, odd = m // 2, m % 2
            x = (2 * k + odd) * parts + j
            fields = [own[f, pl.ds(pl.multiple_of(x * ny, 8), ny), :] for f in range(5)]
            flux = rolled(fields, ahead, behind, 2)
            for f in range(5):
                joint = seam[f, m]
                first = pltpu.roll(joint, (lanes - k * wide - 3) % lanes, 1)
                last = pltpu.roll(joint, (lanes + 115 - k * wide) % lanes, 1)
                here = jnp.where(where < 2, first, flux[f])
                here = jnp.where(where >= lanes - 3, last, here)
                prior = behind(jnp.where(where == lanes - 1, first, here))
                outs[f][x] = fields[f] - (here - prior)


def call(kernel, shapes, scratch, arguments):
    whole = pl.BlockSpec(memory_space=pltpu.VMEM)
    return pl.pallas_call(
        kernel,
        out_shape=[jax.ShapeDtypeStruct(shape, jnp.float32) for shape in shapes],
        in_specs=[whole] * len(arguments),
        out_specs=[whole] * len(shapes),
        scratch_shapes=[pltpu.VMEM(shape, jnp.float32) for shape in scratch],
        compiler_params=pltpu.CompilerParams(vmem_limit_bytes=24 * 2**20),
    )(*arguments)


def both_ways(axis, upward, downward):
    ranks = lax.axis_size(axis)
    up = [(rank, (rank + 1) % ranks) for rank in range(ranks)]
    down = [((rank + 1) % ranks, rank) for rank in range(ranks)]
    return lax.ppermute(upward, axis, up), lax.ppermute(downward, axis, down)


def body(density, momentum, energy):
    nx, ny, nz = density.shape
    whole = (nx, ny, nz)

    def rows(start):
        parts = [
            lax.slice_in_dim(density, start, start + halo, axis=1)[None],
            lax.slice_in_dim(momentum, start, start + halo, axis=2),
            lax.slice_in_dim(energy, start, start + halo, axis=1)[None],
        ]
        return jnp.swapaxes(jnp.concatenate(parts, axis=0), 1, 2)

    before, after = both_ways("gy", rows(ny - halo), rows(0))
    (swept,) = call(x_kernel, [(5, *whole)], [], [density, momentum, energy])
    swept, edges = call(
        functools.partial(y_kernel, nx, ny),
        [(5, nx * ny, nz), (5, nx * group // nz, ny, nz)],
        [(5, 2 * halo, nx, nz)],
        [swept.reshape(5, nx * ny, nz), before, after],
    )
    left, right = both_ways("gz", edges, edges)
    packed = (5, 2 * nx * group // nz, ny, nz)
    return tuple(
        call(
            functools.partial(z_kernel, nx, ny),
            [whole, (3, *whole), whole],
            [packed, packed],
            [swept, left, right],
        )
    )


def solution(mesh):
    return jax.shard_map(
        body,
        mesh=mesh,
        in_specs=(P(None, "gy", "gz"), P(None, None, "gy", "gz"), P(None, "gy", "gz")),
        out_specs=(P(None, "gy", "gz"), P(None, None, "gy", "gz"), P(None, "gy", "gz")),
        check_vma=False,
    )
```

```python
import functools

import jax
import jax.numpy as jnp
from jax import lax
from jax.experimental import pallas as pl
from jax.experimental.pallas import tpu as pltpu
from jax.sharding import PartitionSpec as P

adiabatic = 1.4
courant = 0.15
halo = 3
group = 8


def primitives(fields):
    density, mx, my, mz, energy = fields
    inverse = pl.reciprocal(density, approx=True)
    vx, vy, vz = mx * inverse, my * inverse, mz * inverse
    doubled = mx * vx + my * vy + mz * vz
    pressure = (adiabatic - 1.0) * energy - (0.5 * (adiabatic - 1.0)) * doubled
    return [density, vx, vy, vz, pressure]


def half_slope(ahead, behind):
    top = jnp.maximum(jnp.minimum(ahead, behind), 0.0)
    bottom = jnp.minimum(jnp.maximum(ahead, behind), 0.0)
    return jnp.maximum(jnp.minimum(0.25 * (ahead + behind), top), bottom)


def face_offset(ahead, slope, slope_next):
    offset = 0.5 * ahead - (1.0 / 3.0) * (slope_next - slope)
    return jnp.minimum(jnp.maximum(offset, jnp.minimum(ahead, 0.0)), jnp.maximum(ahead, 0.0))


def limited(first, second):
    doubled = second + second
    return jnp.maximum(jnp.minimum(first, jnp.maximum(doubled, 0.0)), jnp.minimum(doubled, 0.0))


def hll(left, right, normal):
    dl, pl_, ul = left[0], left[4], left[1 + normal]
    dr, pr, ur = right[0], right[4], right[1 + normal]
    tl = adiabatic * pl_
    tr = adiabatic * pr
    al = tl * lax.rsqrt(tl * dl)
    ar = tr * lax.rsqrt(tr * dr)
    slowest = jnp.minimum(jnp.minimum(ul - al, ur - ar), 0.0)
    fastest = jnp.maximum(jnp.maximum(ul + al, ur + ar), 0.0)
    cl = fastest * (courant * pl.reciprocal(fastest - slowest, approx=True))
    cr = courant - cl
    wl = cl * (ul - slowest)
    wr = cr * (ur - fastest)
    ml = wl * dl
    mr = wr * dr
    ql = cl * pl_
    qr = cr * pr
    gl = [ml * left[1 + k] for k in range(3)]
    gr = [mr * right[1 + k] for k in range(3)]
    kinetic = (
        gl[0] * left[1] + gl[1] * left[2] + gl[2] * left[3]
        + gr[0] * right[1] + gr[1] * right[2] + gr[2] * right[3]
    )
    flux = [ml + mr] + [gl[k] + gr[k] for k in range(3)]
    flux[1 + normal] = flux[1 + normal] + (ql + qr)
    inner = (1.0 / (adiabatic - 1.0)) * (wl * pl_ + wr * pr)
    flux.append(0.5 * kinetic + inner + (ql * ul + qr * ur))
    return flux


class Line:
    def __init__(self, load, normal, period=None):
        self.load, self.normal, self.period = load, normal, period
        self.known = {}

    def once(self, name, index, make):
        if self.period is not None:
            index = index % self.period
        if (name, index) not in self.known:
            self.known[(name, index)] = make(index)
        return self.known[(name, index)]

    def prims(self, i):
        return self.once("q", i, lambda i: primitives(self.load(i)))

    def diff(self, i):
        return self.once("d", i, lambda i: [b - a for a, b in zip(self.prims(i), self.prims(i + 1))])

    def slope(self, i):
        return self.once("s", i, lambda i: [half_slope(a, b) for a, b in zip(self.diff(i), self.diff(i - 1))])

    def up(self, i):
        return self.once("u", i, lambda i: [face_offset(d, s, t) for d, s, t in zip(self.diff(i), self.slope(i), self.slope(i + 1))])

    def down(self, i):
        return self.once("w", i, lambda i: [d - u for d, u in zip(self.diff(i - 1), self.up(i - 1))])

    def low(self, i):
        return self.once("l", i, lambda i: [q - limited(w, u) for q, w, u in zip(self.prims(i), self.down(i), self.up(i))])

    def high(self, i):
        return self.once("h", i, lambda i: [q + limited(u, w) for q, w, u in zip(self.prims(i), self.down(i), self.up(i))])

    def flux(self, i):
        return self.once("f", i, lambda i: hll(self.high(i), self.low(i + 1), self.normal))

    def swept(self, i):
        before, after = self.flux(i - 1), self.flux(i)
        return [u - (b - a) for u, a, b in zip(self.load(i), before, after)]


def rolled(fields, ahead, behind, normal):
    states = primitives(fields)
    low, high = [], []
    for q in states:
        d = ahead(q) - q
        s = half_slope(d, behind(d))
        u = face_offset(d, s, ahead(s))
        w = behind(d - u)
        low.append(ahead(q - limited(w, u)))
        high.append(q + limited(u, w))
    return hll(high, low, normal)


def shifts(axis, size):
    return (lambda a: pltpu.roll(a, size - 1, axis), lambda a: pltpu.roll(a, 1, axis))


def x_kernel(density, momentum, energy, out):
    nx, ny, _ = density.shape
    sources = [density, momentum.at[0], momentum.at[1], momentum.at[2], energy]

    @pl.loop(0, ny // 8)
    def _(tile):
        rows = pl.ds(pl.multiple_of(tile * 8, 8), 8)
        line = Line(lambda i: [s[i, rows, :] for s in sources], 0, nx)
        for i in range(nx):
            for f, value in enumerate(line.swept(i)):
                out[f, i, rows, :] = value


def y_kernel(nx, ny, own, before, after, out, edges, ghost):
    lanes = own.shape[-1]
    cells = nx * ny
    ahead, behind = shifts(0, nx)
    for side, source in enumerate((before, after)):

        @pl.loop(0, halo)
        def _(row):
            fields = [source[f, row] for f in range(5)]
            flux = rolled(fields, ahead, behind, 0)
            for f in range(5):
                ghost[f, side * halo + row] = fields[f] - (flux[f] - behind(flux[f]))

    @pl.loop(0, nx // 8)
    def _(tile):
        some = pl.ds(pl.multiple_of(tile * 8, 8), 8)

        def load(i):
            if i < 0:
                return [ghost[f, i + halo, some, :] for f in range(5)]
            if i >= ny:
                return [ghost[f, i - ny + halo, some, :] for f in range(5)]
            return [own[f, pl.ds(tile * (8 * ny) + i, 8, stride=ny), :] for f in range(5)]

        line = Line(load, 1)
        for i in range(ny):
            for f, value in enumerate(line.swept(i)):
                out[f, pl.ds(tile * (8 * ny) + i, 8, stride=ny), :] = value

    pack(nx, ny, lanes, out, edges)


def pack(nx, ny, lanes, source, edges):
    parts = nx * group // lanes
    place = lax.broadcasted_iota(jnp.int32, (ny, lanes), 1) // group

    @pl.loop(0, 5)
    def _(f):
        for j in range(parts):
            packed = None
            for k in range(nx // parts):
                x = k * parts + j
                moved = pltpu.roll(source[f, pl.ds(x * ny, ny), :], k * group + halo, 1)
                packed = moved if packed is None else jnp.where(place == k, moved, packed)
            edges[f, j] = packed


def z_kernel(nx, ny, own, left, right, density, momentum, energy, near, seam):
    lanes = own.shape[-1]
    wide = 2 * group
    parts = nx * group // lanes
    where = lax.broadcasted_iota(jnp.int32, (ny, lanes), 1)
    offset, place = where % wide, where // wide
    ahead, behind = shifts(1, lanes)
    slots = lanes // wide

    @pl.loop(0, 5)
    def _(f):
        for j in range(parts):
            for odd in range(2):
                low, high = left[f, j], right[f, j]
                if odd:
                    low = pltpu.roll(low, lanes - group, 1)
                high = pltpu.roll(high, lanes + 10 - odd * group if odd * group > 10 else 10 - odd * group, 1)
                packed = jnp.where(offset < halo, low, high)
                for k in range(slots):
                    line = own[f, pl.ds(((2 * k + odd) * parts + j) * ny, ny), :]
                    first = pltpu.roll(line, (k * wide + 3) % lanes, 1)
                    last = pltpu.roll(line, (k * wide + 13) % lanes, 1)
                    packed = jnp.where((place == k) & (offset >= 3) & (offset < 8), first, packed)
                    packed = jnp.where((place == k) & (offset >= 8) & (offset < 13), last, packed)
                near[f, j * 2 + odd] = packed

    @pl.loop(0, 2 * parts)
    def _(m):
        flux = rolled([near[f, m] for f in range(5)], ahead, behind, 2)
        for f in range(5):
            seam[f, m] = flux[f]

    outs = [density, momentum.at[0], momentum.at[1], momentum.at[2], energy]
    @pl.loop(0, 2 * parts)
    def _(m):
        j, odd = m // 2, m % 2
        for k in range(slots):
            x = (2 * k + odd) * parts + j
            fields = [own[f, pl.ds(pl.multiple_of(x * ny, 8), ny), :] for f in range(5)]
            flux = rolled(fields, ahead, behind, 2)
            for f in range(5):
                joint = seam[f, m]
                first = pltpu.roll(joint, (lanes - k * wide - 3) % lanes, 1)
                last = pltpu.roll(joint, (lanes + 115 - k * wide) % lanes, 1)
                here = jnp.where(where < 2, first, flux[f])
                here = jnp.where(where >= lanes - 3, last, here)
                prior = behind(jnp.where(where == lanes - 1, first, here))
                outs[f][x] = fields[f] - (here - prior)


def call(kernel, shapes, scratch, arguments):
    whole = pl.BlockSpec(memory_space=pltpu.VMEM)
    return pl.pallas_call(
        kernel,
        out_shape=[jax.ShapeDtypeStruct(shape, jnp.float32) for shape in shapes],
        in_specs=[whole] * len(arguments),
        out_specs=[whole] * len(shapes),
        scratch_shapes=[pltpu.VMEM(shape, jnp.float32) for shape in scratch],
        compiler_params=pltpu.CompilerParams(vmem_limit_bytes=24 * 2**20),
    )(*arguments)


def both_ways(axis, upward, downward):
    ranks = lax.axis_size(axis)
    up = [(rank, (rank + 1) % ranks) for rank in range(ranks)]
    down = [((rank + 1) % ranks, rank) for rank in range(ranks)]
    return lax.ppermute(upward, axis, up), lax.ppermute(downward, axis, down)


def body(density, momentum, energy):
    nx, ny, nz = density.shape
    whole = (nx, ny, nz)

    def rows(start):
        parts = [
            lax.slice_in_dim(density, start, start + halo, axis=1)[None],
            lax.slice_in_dim(momentum, start, start + halo, axis=2),
            lax.slice_in_dim(energy, start, start + halo, axis=1)[None],
        ]
        return jnp.swapaxes(jnp.concatenate(parts, axis=0), 1, 2)

    before, after = both_ways("gy", rows(ny - halo), rows(0))
    (swept,) = call(x_kernel, [(5, *whole)], [], [density, momentum, energy])
    swept, edges = call(
        functools.partial(y_kernel, nx, ny),
        [(5, nx * ny, nz), (5, nx * group // nz, ny, nz)],
        [(5, 2 * halo, nx, nz)],
        [swept.reshape(5, nx * ny, nz), before, after],
    )
    left, right = both_ways("gz", edges, edges)
    packed = (5, 2 * nx * group // nz, ny, nz)
    return tuple(
        call(
            functools.partial(z_kernel, nx, ny),
            [whole, (3, *whole), whole],
            [packed, packed],
            [swept, left, right],
        )
    )


def solution(mesh):
    return jax.shard_map(
        body,
        mesh=mesh,
        in_specs=(P(None, "gy", "gz"), P(None, None, "gy", "gz"), P(None, "gy", "gz")),
        out_specs=(P(None, "gy", "gz"), P(None, None, "gy", "gz"), P(None, "gy", "gz")),
        check_vma=False,
    )
```

```python
import functools

import jax
import jax.numpy as jnp
from jax import lax
from jax.experimental import pallas as pl
from jax.experimental.pallas import tpu as pltpu
from jax.sharding import PartitionSpec as P

adiabatic = 1.4
courant = 0.15
halo = 3
quarters = 4


def primitives(fields):
    density, mx, my, mz, energy = fields
    inverse = pl.reciprocal(density, approx=True)
    vx, vy, vz = mx * inverse, my * inverse, mz * inverse
    doubled = mx * vx + my * vy + mz * vz
    pressure = (adiabatic - 1.0) * energy - (0.5 * (adiabatic - 1.0)) * doubled
    return [density, vx, vy, vz, pressure]


def half_slope(ahead, behind):
    top = jnp.maximum(jnp.minimum(ahead, behind), 0.0)
    bottom = jnp.minimum(jnp.maximum(ahead, behind), 0.0)
    return jnp.maximum(jnp.minimum(0.25 * (ahead + behind), top), bottom)


def face_offset(ahead, slope, slope_next):
    offset = 0.5 * ahead - (1.0 / 3.0) * (slope_next - slope)
    return jnp.minimum(jnp.maximum(offset, jnp.minimum(ahead, 0.0)), jnp.maximum(ahead, 0.0))


def limited(first, second):
    doubled = second + second
    return jnp.maximum(jnp.minimum(first, jnp.maximum(doubled, 0.0)), jnp.minimum(doubled, 0.0))


def hll(left, right, normal):
    dl, pl_, ul = left[0], left[4], left[1 + normal]
    dr, pr, ur = right[0], right[4], right[1 + normal]
    tl = adiabatic * pl_
    tr = adiabatic * pr
    al = tl * lax.rsqrt(tl * dl)
    ar = tr * lax.rsqrt(tr * dr)
    slowest = jnp.minimum(jnp.minimum(ul - al, ur - ar), 0.0)
    fastest = jnp.maximum(jnp.maximum(ul + al, ur + ar), 0.0)
    cl = fastest * (courant * pl.reciprocal(fastest - slowest, approx=True))
    cr = courant - cl
    wl = cl * (ul - slowest)
    wr = cr * (ur - fastest)
    ml = wl * dl
    mr = wr * dr
    ql = cl * pl_
    qr = cr * pr
    gl = [ml * left[1 + k] for k in range(3)]
    gr = [mr * right[1 + k] for k in range(3)]
    kinetic = (
        gl[0] * left[1] + gl[1] * left[2] + gl[2] * left[3]
        + gr[0] * right[1] + gr[1] * right[2] + gr[2] * right[3]
    )
    flux = [ml + mr] + [gl[k] + gr[k] for k in range(3)]
    flux[1 + normal] = flux[1 + normal] + (ql + qr)
    inner = (1.0 / (adiabatic - 1.0)) * (wl * pl_ + wr * pr)
    flux.append(0.5 * kinetic + inner + (ql * ul + qr * ur))
    return flux


class Line:
    def __init__(self, load, normal, period=None):
        self.load, self.normal, self.period = load, normal, period
        self.known = {}

    def once(self, name, index, make):
        if self.period is not None:
            index = index % self.period
        if (name, index) not in self.known:
            self.known[(name, index)] = make(index)
        return self.known[(name, index)]

    def prims(self, i):
        return self.once("q", i, lambda i: primitives(self.load(i)))

    def diff(self, i):
        return self.once("d", i, lambda i: [b - a for a, b in zip(self.prims(i), self.prims(i + 1))])

    def slope(self, i):
        return self.once("s", i, lambda i: [half_slope(a, b) for a, b in zip(self.diff(i), self.diff(i - 1))])

    def up(self, i):
        return self.once("u", i, lambda i: [face_offset(d, s, t) for d, s, t in zip(self.diff(i), self.slope(i), self.slope(i + 1))])

    def down(self, i):
        return self.once("w", i, lambda i: [d - u for d, u in zip(self.diff(i - 1), self.up(i - 1))])

    def low(self, i):
        return self.once("l", i, lambda i: [q - limited(w, u) for q, w, u in zip(self.prims(i), self.down(i), self.up(i))])

    def high(self, i):
        return self.once("h", i, lambda i: [q + limited(u, w) for q, w, u in zip(self.prims(i), self.down(i), self.up(i))])

    def flux(self, i):
        return self.once("f", i, lambda i: hll(self.high(i), self.low(i + 1), self.normal))

    def swept(self, i):
        before, after = self.flux(i - 1), self.flux(i)
        return [u - (b - a) for u, a, b in zip(self.load(i), before, after)]


def rolled(fields, ahead, behind, normal):
    states = primitives(fields)
    low, high = [], []
    for q in states:
        d = ahead(q) - q
        s = half_slope(d, behind(d))
        u = face_offset(d, s, ahead(s))
        w = behind(d - u)
        low.append(ahead(q - limited(w, u)))
        high.append(q + limited(u, w))
    return hll(high, low, normal)


def shifts(axis, size):
    return (lambda a: pltpu.roll(a, size - 1, axis), lambda a: pltpu.roll(a, 1, axis))


def row(index):
    return pl.ds(index, 8)


def fields_of(density, momentum, energy):
    return [density, momentum.at[0], momentum.at[1], momentum.at[2], energy]


def rows_kernel(density, bottom_density, momentum, bottom_momentum, energy, bottom_energy, first, last):
    tops = fields_of(density, momentum, energy)
    bottoms = fields_of(bottom_density, bottom_momentum, bottom_energy)
    nx, _, nz = density.shape
    for f in range(5):
        for r in range(halo):
            first[f, r] = tops[f].reshape(nx * 8, nz)[pl.ds(r, nx, stride=8), :]
            last[f, r] = bottoms[f].reshape(nx * 8, nz)[pl.ds(8 - halo + r, nx, stride=8), :]


def turn_in(source, turned, count):
    lanes = source.shape[-1]
    span = lanes // quarters

    @pl.loop(0, 5)
    def _(f):
        for b in range(count):
            block = source[f, pl.ds(b * lanes, lanes), :].T
            for q in range(quarters):
                turned[f, pl.ds(q * count + b, span, stride=quarters * count), :] = block[q * span : (q + 1) * span]


def turn_out(turned, count, store):
    lanes = turned.shape[-1]
    span = lanes // quarters
    for f in range(5):
        for b in range(count):
            parts = [turned[f, pl.ds(q * count + b, span, stride=quarters * count), :] for q in range(quarters)]
            store(f, b, jnp.concatenate(parts, axis=0).T)


def ends(turned, count, upward, downward):
    span = turned.shape[1] // (quarters * count)
    for f in range(5):
        for k in range(halo):
            upward[f, k] = turned[f, row((span - halo + k + 1) * quarters * count - 8), :]
            downward[f, k] = turned[f, row(k * quarters * count), :]


def z_sweep(own, left, right, swept, count):
    width = quarters * count
    span = own.shape[1] // width
    place = lax.broadcasted_iota(jnp.int32, (8, own.shape[-1]), 0)
    for start in range(0, width, 8):

        def load(i):
            if 0 <= i < span:
                return [own[f, row(i * width + start), :] for f in range(5)]
            if i < 0:
                fields = [own[f, row((i + span) * width + start - count), :] for f in range(5)]
                if start == 0:
                    fields = [jnp.where(place < count, pltpu.roll(left[f, i + halo], count, 0), a) for f, a in enumerate(fields)]
                return fields
            fields = [own[f, row((i - span) * width + start + count), :] for f in range(5)]
            if start + 8 == width:
                fields = [jnp.where(place >= 8 - count, pltpu.roll(right[f, i - span], 8 - count, 0), a) for f, a in enumerate(fields)]
            return fields

        line = Line(load, 2)
        for i in range(span):
            for f, value in enumerate(line.swept(i)):
                swept[f, row(i * width + start), :] = value


def inner_kernel(density, momentum, energy, turned, upward, downward, rim, joint, held, inner):
    nx, ny, lanes = density.shape
    deep = lanes // nx
    sources = fields_of(density, momentum, energy)

    @pl.loop(0, ny // 8)
    def _(tile):
        start = pl.multiple_of(tile * 8, 8)
        line = Line(lambda i: [s[i, pl.ds(start, 8), :] for s in sources], 0, nx)
        for i in range(nx):
            for f, value in enumerate(line.swept(i)):
                held[f, pl.ds(pl.multiple_of(i * ny + start, 8), 8), :] = value

    @pl.loop(0, nx // 8)
    def _(tile):
        some = pl.ds(pl.multiple_of(tile * 8, 8), 8)
        line = Line(lambda i: [held[f, pl.ds(tile * (8 * ny) + i, 8, stride=ny), :] for f in range(5)], 1)
        for i in range(deep, ny - deep):
            for f, value in enumerate(line.swept(i)):
                inner[f, pl.ds(pl.multiple_of((i - deep) * nx + tile * 8, 8), 8), :] = value
        for f in range(5):
            joint[f, 0, some, :] = line.flux(deep - 1)[f]
            joint[f, 1, some, :] = line.flux(ny - deep - 1)[f]
        kept = deep + halo - 1
        for r in range(kept):
            for f, (a, b) in enumerate(zip(line.load(r), line.load(ny - kept + r))):
                rim[f, r, some, :] = a
                rim[f, kept + r, some, :] = b

    count = ny // deep - 2
    turn_in(inner, turned, count)
    ends(turned, count, upward, downward)


def edge_kernel(before, after, rim, joint, turned, upward, downward, ghost, outer):
    _, kept, nx, lanes = rim.shape
    kept = kept // 2
    deep = lanes // nx
    ahead, behind = shifts(0, nx)
    for side, source in enumerate((before, after)):

        @pl.loop(0, halo)
        def _(r):
            fields = [source[f, r] for f in range(5)]
            flux = rolled(fields, ahead, behind, 0)
            for f in range(5):
                ghost[f, side * halo + r] = fields[f] - (flux[f] - behind(flux[f]))

    @pl.loop(0, nx // 8)
    def _(tile):
        some = pl.ds(pl.multiple_of(tile * 8, 8), 8)
        for side in range(2):

            def load(i):
                if side == 0:
                    source, at = (ghost, i + halo) if i < 0 else (rim, i)
                else:
                    source, at = (ghost, i - deep + halo) if i >= deep else (rim, i + kept + kept - deep)
                return [source[f, at, some, :] for f in range(5)]

            line = Line(load, 1)
            known = deep - 1 if side == 0 else -1
            line.known[("f", known)] = [joint[f, side, some, :] for f in range(5)]
            for i in range(deep):
                for f, value in enumerate(line.swept(i)):
                    outer[f, pl.ds(pl.multiple_of((side * deep + i) * nx + tile * 8, 8), 8), :] = value

    turn_in(outer, turned, 2)
    ends(turned, 2, upward, downward)


def inner_z_kernel(count, own, left, right, out, swept):
    lanes = own.shape[-1]
    z_sweep(own, left, right, swept, count)

    def store(f, b, block):
        out[f, pl.ds(b * lanes, lanes), :] = block

    turn_out(swept, count, store)


def edge_z_kernel(ny, own, left, right, inner, density, momentum, energy, swept):
    lanes = own.shape[-1]
    nx = density.shape[0] // ny
    deep = lanes // nx
    outs = fields_of(density, momentum, energy)
    z_sweep(own, left, right, swept, 2)
    for f in range(5):
        for i in range(deep, ny - deep):
            outs[f][pl.ds(i, nx, stride=ny), :] = inner[f, pl.ds((i - deep) * nx, nx), :]

    def store(f, b, block):
        for r in range(deep):
            outs[f][pl.ds(b * (ny - deep) + r, nx, stride=ny), :] = block[r * nx : (r + 1) * nx]

    turn_out(swept, 2, store)


def call(kernel, shapes, scratch, arguments, in_specs=None):
    whole = pl.BlockSpec(memory_space=pltpu.VMEM)
    return pl.pallas_call(
        kernel,
        out_shape=[jax.ShapeDtypeStruct(shape, jnp.float32) for shape in shapes],
        in_specs=[whole] * len(arguments) if in_specs is None else in_specs,
        out_specs=[whole] * len(shapes),
        scratch_shapes=[pltpu.VMEM(shape, jnp.float32) for shape in scratch],
        compiler_params=pltpu.CompilerParams(vmem_limit_bytes=24 * 2**20),
    )(*arguments)


def both_ways(axis, upward, downward):
    ranks = lax.axis_size(axis)
    up = [(rank, (rank + 1) % ranks) for rank in range(ranks)]
    down = [((rank + 1) % ranks, rank) for rank in range(ranks)]
    return lax.ppermute(upward, axis, up), lax.ppermute(downward, axis, down)


def y_rows(density, momentum, energy):
    nx, ny, nz = density.shape
    plain = [pl.BlockSpec((nx, 8, nz), lambda _, at=at: (0, at, 0)) for at in (0, ny // 8 - 1)]
    vector = [pl.BlockSpec((3, nx, 8, nz), lambda _, at=at: (0, 0, at, 0)) for at in (0, ny // 8 - 1)]
    shape = (5, halo, nx, nz)
    return pl.pallas_call(
        rows_kernel,
        grid=(1,),
        out_shape=[jax.ShapeDtypeStruct(shape, jnp.float32)] * 2,
        in_specs=plain + vector + plain,
        out_specs=[pl.BlockSpec(shape, lambda _: (0, 0, 0, 0))] * 2,
        compiler_params=pltpu.CompilerParams(vmem_limit_bytes=16 * 2**20),
    )(density, density, momentum, momentum, energy, energy)


def body(density, momentum, energy):
    nx, ny, nz = density.shape
    deep = nz // nx
    count = ny // deep - 2
    kept = deep + halo - 1
    end = (5, halo, 8, nz)

    first, last = y_rows(density, momentum, energy)
    before, after = both_ways("gy", last, first)
    turned, upward, downward, rim, joint = call(
        inner_kernel,
        [(5, count * nz, nz), end, end, (5, 2 * kept, nx, nz), (5, 2, nx, nz)],
        [(5, nx * ny, nz), (5, count * nz, nz)],
        [density, momentum, energy],
    )
    left, right = both_ways("gz", upward, downward)
    (inner,) = call(
        functools.partial(inner_z_kernel, count),
        [(5, count * nz, nz)],
        [(5, count * nz, nz)],
        [turned, left, right],
    )
    turned, upward, downward = call(
        edge_kernel,
        [(5, 2 * nz, nz), end, end],
        [(5, 2 * halo, nx, nz), (5, 2 * nz, nz)],
        [before, after, rim, joint],
    )
    left, right = both_ways("gz", upward, downward)
    cells = nx * ny
    outs = call(
        functools.partial(edge_z_kernel, ny),
        [(cells, nz), (3, cells, nz), (cells, nz)],
        [(5, 2 * nz, nz)],
        [turned, left, right, inner],
    )
    return (outs[0].reshape(nx, ny, nz), outs[1].reshape(3, nx, ny, nz), outs[2].reshape(nx, ny, nz))


def solution(mesh):
    return jax.shard_map(
        body,
        mesh=mesh,
        in_specs=(P(None, "gy", "gz"), P(None, None, "gy", "gz"), P(None, "gy", "gz")),
        out_specs=(P(None, "gy", "gz"), P(None, None, "gy", "gz"), P(None, "gy", "gz")),
        check_vma=False,
    )
```

```python
import functools

import jax
import jax.numpy as jnp
from jax import lax
from jax.experimental import pallas as pl
from jax.experimental.pallas import tpu as pltpu
from jax.sharding import PartitionSpec as P

adiabatic = 1.4
courant = 0.15
halo = 3
quarters = 4


def primitives(fields):
    density, mx, my, mz, energy = fields
    inverse = pl.reciprocal(density, approx=True)
    vx, vy, vz = mx * inverse, my * inverse, mz * inverse
    doubled = mx * vx + my * vy + mz * vz
    pressure = (adiabatic - 1.0) * energy - (0.5 * (adiabatic - 1.0)) * doubled
    return [density, vx, vy, vz, pressure]


def half_slope(ahead, behind):
    top = jnp.maximum(jnp.minimum(ahead, behind), 0.0)
    bottom = jnp.minimum(jnp.maximum(ahead, behind), 0.0)
    return jnp.maximum(jnp.minimum(0.25 * (ahead + behind), top), bottom)


def face_offset(ahead, slope, slope_next):
    offset = 0.5 * ahead - (1.0 / 3.0) * (slope_next - slope)
    return jnp.minimum(jnp.maximum(offset, jnp.minimum(ahead, 0.0)), jnp.maximum(ahead, 0.0))


def limited(first, second):
    doubled = second + second
    return jnp.maximum(jnp.minimum(first, jnp.maximum(doubled, 0.0)), jnp.minimum(doubled, 0.0))


def hll(left, right, normal):
    dl, pl_, ul = left[0], left[4], left[1 + normal]
    dr, pr, ur = right[0], right[4], right[1 + normal]
    tl = adiabatic * pl_
    tr = adiabatic * pr
    al = tl * lax.rsqrt(tl * dl)
    ar = tr * lax.rsqrt(tr * dr)
    slowest = jnp.minimum(jnp.minimum(ul - al, ur - ar), 0.0)
    fastest = jnp.maximum(jnp.maximum(ul + al, ur + ar), 0.0)
    cl = fastest * (courant * pl.reciprocal(fastest - slowest, approx=True))
    cr = courant - cl
    wl = cl * (ul - slowest)
    wr = cr * (ur - fastest)
    ml = wl * dl
    mr = wr * dr
    ql = cl * pl_
    qr = cr * pr
    gl = [ml * left[1 + k] for k in range(3)]
    gr = [mr * right[1 + k] for k in range(3)]
    kinetic = (
        gl[0] * left[1] + gl[1] * left[2] + gl[2] * left[3]
        + gr[0] * right[1] + gr[1] * right[2] + gr[2] * right[3]
    )
    flux = [ml + mr] + [gl[k] + gr[k] for k in range(3)]
    flux[1 + normal] = flux[1 + normal] + (ql + qr)
    inner = (1.0 / (adiabatic - 1.0)) * (wl * pl_ + wr * pr)
    flux.append(0.5 * kinetic + inner + (ql * ul + qr * ur))
    return flux


class Line:
    def __init__(self, load, normal, period=None):
        self.load, self.normal, self.period = load, normal, period
        self.known = {}

    def once(self, name, index, make):
        if self.period is not None:
            index = index % self.period
        if (name, index) not in self.known:
            self.known[(name, index)] = make(index)
        return self.known[(name, index)]

    def prims(self, i):
        return self.once("q", i, lambda i: primitives(self.load(i)))

    def diff(self, i):
        return self.once("d", i, lambda i: [b - a for a, b in zip(self.prims(i), self.prims(i + 1))])

    def slope(self, i):
        return self.once("s", i, lambda i: [half_slope(a, b) for a, b in zip(self.diff(i), self.diff(i - 1))])

    def up(self, i):
        return self.once("u", i, lambda i: [face_offset(d, s, t) for d, s, t in zip(self.diff(i), self.slope(i), self.slope(i + 1))])

    def down(self, i):
        return self.once("w", i, lambda i: [d - u for d, u in zip(self.diff(i - 1), self.up(i - 1))])

    def low(self, i):
        return self.once("l", i, lambda i: [q - limited(w, u) for q, w, u in zip(self.prims(i), self.down(i), self.up(i))])

    def high(self, i):
        return self.once("h", i, lambda i: [q + limited(u, w) for q, w, u in zip(self.prims(i), self.down(i), self.up(i))])

    def flux(self, i):
        return self.once("f", i, lambda i: hll(self.high(i), self.low(i + 1), self.normal))

    def swept(self, i):
        before, after = self.flux(i - 1), self.flux(i)
        return [u - (b - a) for u, a, b in zip(self.load(i), before, after)]


def rolled(fields, ahead, behind, normal):
    states = primitives(fields)
    low, high = [], []
    for q in states:
        d = ahead(q) - q
        s = half_slope(d, behind(d))
        u = face_offset(d, s, ahead(s))
        w = behind(d - u)
        low.append(ahead(q - limited(w, u)))
        high.append(q + limited(u, w))
    return hll(high, low, normal)


def shifts(axis, size):
    return (lambda a: pltpu.roll(a, size - 1, axis), lambda a: pltpu.roll(a, 1, axis))


def row(index):
    return pl.ds(index, 8)


def fields_of(density, momentum, energy):
    return [density, momentum.at[0], momentum.at[1], momentum.at[2], energy]


def rows_kernel(density, momentum, energy, first, last, held, arrived):
    sources = fields_of(density, momentum, energy)
    nx, ny, nz = density.shape
    copies = []
    for side in range(2):
        for f in range(5):
            tile = sources[f].at[:, pl.ds(side * (ny - 8), 8), :]
            copies.append(pltpu.make_async_copy(tile, held.at[side, f], arrived.at[side, f]))
    for copy in copies:
        copy.start()
    for side, out in enumerate((first, last)):
        for f in range(5):
            copies[side * 5 + f].wait()
            flat = held.at[side, f].reshape(nx * 8, nz)
            for r in range(halo):
                out[f, r] = flat[pl.ds(side * (8 - halo) + r, nx, stride=8), :]


def turn_in(source, turned, count):
    lanes = source.shape[-1]
    span = lanes // quarters

    @pl.loop(0, 5)
    def _(f):
        for b in range(count):
            block = source[f, pl.ds(b * lanes, lanes), :].T
            for q in range(quarters):
                turned[f, pl.ds(q * count + b, span, stride=quarters * count), :] = block[q * span : (q + 1) * span]


def turn_out(turned, count, store):
    lanes = turned.shape[-1]
    span = lanes // quarters
    for f in range(5):
        for b in range(count):
            parts = [turned[f, pl.ds(q * count + b, span, stride=quarters * count), :] for q in range(quarters)]
            store(f, b, jnp.concatenate(parts, axis=0).T)


def ends(turned, count, upward, downward):
    span = turned.shape[1] // (quarters * count)
    for f in range(5):
        for k in range(halo):
            upward[f, k] = turned[f, row((span - halo + k + 1) * quarters * count - 8), :]
            downward[f, k] = turned[f, row(k * quarters * count), :]


def z_sweep(own, left, right, swept, count):
    width = quarters * count
    span = own.shape[1] // width
    place = lax.broadcasted_iota(jnp.int32, (8, own.shape[-1]), 0)
    for start in range(0, width, 8):

        def load(i):
            if 0 <= i < span:
                return [own[f, row(i * width + start), :] for f in range(5)]
            if i < 0:
                fields = [own[f, row((i + span) * width + start - count), :] for f in range(5)]
                if start == 0:
                    fields = [jnp.where(place < count, pltpu.roll(left[f, i + halo], count, 0), a) for f, a in enumerate(fields)]
                return fields
            fields = [own[f, row((i - span) * width + start + count), :] for f in range(5)]
            if start + 8 == width:
                fields = [jnp.where(place >= 8 - count, pltpu.roll(right[f, i - span], 8 - count, 0), a) for f, a in enumerate(fields)]
            return fields

        line = Line(load, 2)
        for i in range(span):
            for f, value in enumerate(line.swept(i)):
                swept[f, row(i * width + start), :] = value


def inner_kernel(density, momentum, energy, turned, both, rim, joint, held, inner):
    nx, ny, lanes = density.shape
    deep = lanes // nx
    sources = fields_of(density, momentum, energy)

    @pl.loop(0, ny // 8)
    def _(tile):
        start = pl.multiple_of(tile * 8, 8)
        line = Line(lambda i: [s[i, pl.ds(start, 8), :] for s in sources], 0, nx)
        for i in range(nx):
            for f, value in enumerate(line.swept(i)):
                held[f, pl.ds(pl.multiple_of(i * ny + start, 8), 8), :] = value

    @pl.loop(0, nx // 8)
    def _(tile):
        some = pl.ds(pl.multiple_of(tile * 8, 8), 8)
        line = Line(lambda i: [held[f, pl.ds(tile * (8 * ny) + i, 8, stride=ny), :] for f in range(5)], 1)
        for i in range(deep, ny - deep):
            for f, value in enumerate(line.swept(i)):
                inner[f, pl.ds(pl.multiple_of((i - deep) * nx + tile * 8, 8), 8), :] = value
        for f in range(5):
            joint[f, 0, some, :] = line.flux(deep - 1)[f]
            joint[f, 1, some, :] = line.flux(ny - deep - 1)[f]
        kept = deep + halo - 1
        for r in range(kept):
            for f, (a, b) in enumerate(zip(line.load(r), line.load(ny - kept + r))):
                rim[f, r, some, :] = a
                rim[f, kept + r, some, :] = b

    count = ny // deep - 2
    turn_in(inner, turned, count)
    ends(turned, count, both.at[0], both.at[1])


def edge_kernel(before, after, rim, joint, turned, upward, downward, ghost, outer):
    _, kept, nx, lanes = rim.shape
    kept = kept // 2
    deep = lanes // nx
    ahead, behind = shifts(0, nx)
    for side, source in enumerate((before, after)):

        @pl.loop(0, halo)
        def _(r):
            fields = [source[f, r] for f in range(5)]
            flux = rolled(fields, ahead, behind, 0)
            for f in range(5):
                ghost[f, side * halo + r] = fields[f] - (flux[f] - behind(flux[f]))

    @pl.loop(0, nx // 8)
    def _(tile):
        some = pl.ds(pl.multiple_of(tile * 8, 8), 8)
        for side in range(2):

            def load(i):
                if side == 0:
                    source, at = (ghost, i + halo) if i < 0 else (rim, i)
                else:
                    source, at = (ghost, i - deep + halo) if i >= deep else (rim, i + kept + kept - deep)
                return [source[f, at, some, :] for f in range(5)]

            line = Line(load, 1)
            known = deep - 1 if side == 0 else -1
            line.known[("f", known)] = [joint[f, side, some, :] for f in range(5)]
            for i in range(deep):
                for f, value in enumerate(line.swept(i)):
                    outer[f, pl.ds(pl.multiple_of((side * deep + i) * nx + tile * 8, 8), 8), :] = value

    turn_in(outer, turned, 2)
    ends(turned, 2, upward, downward)


def inner_z_kernel(count, _, own, left, right, out, swept):
    lanes = own.shape[-1]
    z_sweep(own, left.at[0, 0], right.at[0, 0], swept, count)

    def store(f, b, block):
        out[f, pl.ds(b * lanes, lanes), :] = block

    turn_out(swept, count, store)


def edge_z_kernel(ny, own, left, right, inner, density, momentum, energy, swept):
    lanes = own.shape[-1]
    nx = density.shape[0] // ny
    deep = lanes // nx
    outs = fields_of(density, momentum, energy)
    z_sweep(own, left, right, swept, 2)
    for f in range(5):
        for i in range(deep, ny - deep):
            outs[f][pl.ds(i, nx, stride=ny), :] = inner[f, pl.ds((i - deep) * nx, nx), :]

    def store(f, b, block):
        for r in range(deep):
            outs[f][pl.ds(b * (ny - deep) + r, nx, stride=ny), :] = block[r * nx : (r + 1) * nx]

    turn_out(swept, 2, store)


def call(kernel, shapes, scratch, arguments, in_specs=None):
    whole = pl.BlockSpec(memory_space=pltpu.VMEM)
    return pl.pallas_call(
        kernel,
        out_shape=[jax.ShapeDtypeStruct(shape, jnp.float32) for shape in shapes],
        in_specs=[whole] * len(arguments) if in_specs is None else in_specs,
        out_specs=[whole] * len(shapes),
        scratch_shapes=[pltpu.VMEM(shape, jnp.float32) for shape in scratch],
        compiler_params=pltpu.CompilerParams(vmem_limit_bytes=24 * 2**20),
    )(*arguments)


def both_ways(axis, upward, downward):
    ranks = lax.axis_size(axis)
    up = [(rank, (rank + 1) % ranks) for rank in range(ranks)]
    down = [((rank + 1) % ranks, rank) for rank in range(ranks)]
    return lax.ppermute(upward, axis, up), lax.ppermute(downward, axis, down)


def y_rows(density, momentum, energy):
    nx, ny, nz = density.shape
    shape = (5, halo, nx, nz)
    return pl.pallas_call(
        rows_kernel,
        out_shape=[jax.ShapeDtypeStruct(shape, jnp.float32)] * 2,
        in_specs=[pl.BlockSpec(memory_space=pltpu.HBM)] * 3,
        out_specs=[pl.BlockSpec(memory_space=pltpu.VMEM)] * 2,
        scratch_shapes=[pltpu.VMEM((2, 5, nx, 8, nz), jnp.float32), pltpu.SemaphoreType.DMA((2, 5))],
        compiler_params=pltpu.CompilerParams(vmem_limit_bytes=16 * 2**20),
    )(density, momentum, energy)


def inner_z(turned, gathered, sides):
    _, rows, nz = turned.shape
    end = (1, 1, *gathered.shape[2:])
    whole = pl.BlockSpec((5, rows, nz), lambda _, sides: (0, 0, 0))
    return pl.pallas_call(
        functools.partial(inner_z_kernel, rows // nz),
        out_shape=jax.ShapeDtypeStruct((5, rows, nz), jnp.float32),
        grid_spec=pltpu.PrefetchScalarGridSpec(
            num_scalar_prefetch=1,
            grid=(1,),
            in_specs=[
                whole,
                pl.BlockSpec(end, lambda _, sides: (sides[0], 0, 0, 0, 0, 0)),
                pl.BlockSpec(end, lambda _, sides: (sides[1], 1, 0, 0, 0, 0)),
            ],
            out_specs=whole,
            scratch_shapes=[pltpu.VMEM((5, rows, nz), jnp.float32)],
        ),
        compiler_params=pltpu.CompilerParams(vmem_limit_bytes=24 * 2**20),
    )(sides, turned, gathered, gathered)


def body(density, momentum, energy):
    nx, ny, nz = density.shape
    deep = nz // nx
    count = ny // deep - 2
    kept = deep + halo - 1
    end = (5, halo, 8, nz)

    first, last = y_rows(density, momentum, energy)
    before, after = both_ways("gy", last, first)
    turned, both, rim, joint = call(
        inner_kernel,
        [(5, count * nz, nz), (2, *end), (5, 2 * kept, nx, nz), (5, 2, nx, nz)],
        [(5, nx * ny, nz), (5, count * nz, nz)],
        [density, momentum, energy],
    )
    ranks, rank = lax.axis_size("gz"), lax.axis_index("gz")
    sides = jnp.stack([(rank + ranks - 1) % ranks, (rank + 1) % ranks])
    inner = inner_z(turned, lax.all_gather(both, "gz"), sides)
    turned, upward, downward = call(
        edge_kernel,
        [(5, 2 * nz, nz), end, end],
        [(5, 2 * halo, nx, nz), (5, 2 * nz, nz)],
        [before, after, rim, joint],
    )
    left, right = both_ways("gz", upward, downward)
    cells = nx * ny
    outs = call(
        functools.partial(edge_z_kernel, ny),
        [(cells, nz), (3, cells, nz), (cells, nz)],
        [(5, 2 * nz, nz)],
        [turned, left, right, inner],
    )
    return (outs[0].reshape(nx, ny, nz), outs[1].reshape(3, nx, ny, nz), outs[2].reshape(nx, ny, nz))


def solution(mesh):
    return jax.shard_map(
        body,
        mesh=mesh,
        in_specs=(P(None, "gy", "gz"), P(None, None, "gy", "gz"), P(None, "gy", "gz")),
        out_specs=(P(None, "gy", "gz"), P(None, None, "gy", "gz"), P(None, "gy", "gz")),
        check_vma=False,
    )
```

```python
import functools

import jax
import jax.numpy as jnp
from jax import lax
from jax.experimental import pallas as pl
from jax.experimental.pallas import tpu as pltpu
from jax.sharding import PartitionSpec as P

adiabatic = 1.4
courant = 0.15
halo = 3
quarters = 4


def primitives(fields):
    density, mx, my, mz, energy = fields
    inverse = pl.reciprocal(density, approx=True)
    vx, vy, vz = mx * inverse, my * inverse, mz * inverse
    doubled = mx * vx + my * vy + mz * vz
    pressure = (adiabatic - 1.0) * energy - (0.5 * (adiabatic - 1.0)) * doubled
    return [density, vx, vy, vz, pressure]


def half_slope(ahead, behind):
    top = jnp.maximum(jnp.minimum(ahead, behind), 0.0)
    bottom = jnp.minimum(jnp.maximum(ahead, behind), 0.0)
    return jnp.maximum(jnp.minimum(0.25 * (ahead + behind), top), bottom)


def face_offset(ahead, slope, slope_next):
    offset = 0.5 * ahead - (1.0 / 3.0) * (slope_next - slope)
    return jnp.minimum(jnp.maximum(offset, jnp.minimum(ahead, 0.0)), jnp.maximum(ahead, 0.0))


def limited(first, second):
    doubled = second + second
    return jnp.maximum(jnp.minimum(first, jnp.maximum(doubled, 0.0)), jnp.minimum(doubled, 0.0))


def hll(left, right, normal):
    dl, pl_, ul = left[0], left[4], left[1 + normal]
    dr, pr, ur = right[0], right[4], right[1 + normal]
    tl = adiabatic * pl_
    tr = adiabatic * pr
    al = tl * lax.rsqrt(tl * dl)
    ar = tr * lax.rsqrt(tr * dr)
    slowest = jnp.minimum(jnp.minimum(ul - al, ur - ar), 0.0)
    fastest = jnp.maximum(jnp.maximum(ul + al, ur + ar), 0.0)
    cl = fastest * (courant * pl.reciprocal(fastest - slowest, approx=True))
    cr = courant - cl
    wl = cl * (ul - slowest)
    wr = cr * (ur - fastest)
    ml = wl * dl
    mr = wr * dr
    ql = cl * pl_
    qr = cr * pr
    gl = [ml * left[1 + k] for k in range(3)]
    gr = [mr * right[1 + k] for k in range(3)]
    kinetic = (
        gl[0] * left[1] + gl[1] * left[2] + gl[2] * left[3]
        + gr[0] * right[1] + gr[1] * right[2] + gr[2] * right[3]
    )
    flux = [ml + mr] + [gl[k] + gr[k] for k in range(3)]
    flux[1 + normal] = flux[1 + normal] + (ql + qr)
    inner = (1.0 / (adiabatic - 1.0)) * (wl * pl_ + wr * pr)
    flux.append(0.5 * kinetic + inner + (ql * ul + qr * ur))
    return flux


class Line:
    def __init__(self, load, normal, period=None):
        self.load, self.normal, self.period = load, normal, period
        self.known = {}

    def once(self, name, index, make):
        if self.period is not None:
            index = index % self.period
        if (name, index) not in self.known:
            self.known[(name, index)] = make(index)
        return self.known[(name, index)]

    def prims(self, i):
        return self.once("q", i, lambda i: primitives(self.load(i)))

    def diff(self, i):
        return self.once("d", i, lambda i: [b - a for a, b in zip(self.prims(i), self.prims(i + 1))])

    def slope(self, i):
        return self.once("s", i, lambda i: [half_slope(a, b) for a, b in zip(self.diff(i), self.diff(i - 1))])

    def up(self, i):
        return self.once("u", i, lambda i: [face_offset(d, s, t) for d, s, t in zip(self.diff(i), self.slope(i), self.slope(i + 1))])

    def down(self, i):
        return self.once("w", i, lambda i: [d - u for d, u in zip(self.diff(i - 1), self.up(i - 1))])

    def low(self, i):
        return self.once("l", i, lambda i: [q - limited(w, u) for q, w, u in zip(self.prims(i), self.down(i), self.up(i))])

    def high(self, i):
        return self.once("h", i, lambda i: [q + limited(u, w) for q, w, u in zip(self.prims(i), self.down(i), self.up(i))])

    def flux(self, i):
        return self.once("f", i, lambda i: hll(self.high(i), self.low(i + 1), self.normal))

    def swept(self, i):
        before, after = self.flux(i - 1), self.flux(i)
        return [u - (b - a) for u, a, b in zip(self.load(i), before, after)]


def rolled(fields, ahead, behind, normal):
    states = primitives(fields)
    low, high = [], []
    for q in states:
        d = ahead(q) - q
        s = half_slope(d, behind(d))
        u = face_offset(d, s, ahead(s))
        w = behind(d - u)
        low.append(ahead(q - limited(w, u)))
        high.append(q + limited(u, w))
    return hll(high, low, normal)


def shifts(axis, size):
    return (lambda a: pltpu.roll(a, size - 1, axis), lambda a: pltpu.roll(a, 1, axis))


def row(index):
    return pl.ds(index, 8)


def fields_of(density, momentum, energy):
    return [density, momentum.at[0], momentum.at[1], momentum.at[2], energy]


def odd_rank(axis):
    return lax.axis_index(axis) % 2 == 1


class Received:
    def __init__(self, odd, on_odd, on_even):
        self.odd, self.on_odd, self.on_even = odd, on_odd, on_even

    def __getitem__(self, index):
        return jnp.where(self.odd, self.on_odd[index], self.on_even[index])


def sides_of(axis, far, near):
    odd = odd_rank(axis)
    return Received(odd, near, far), Received(odd, far, near)


def rows_kernel(density, momentum, energy, far, near, held, arrived):
    sources = fields_of(density, momentum, energy)
    nx, ny, nz = density.shape
    copies = []
    for f in range(5):
        for side in range(2):
            tile = sources[f].at[:, pl.ds(side * (ny - 8), 8), :]
            copies.append(pltpu.make_async_copy(tile, held.at[side, f], arrived.at[side, f]))
    for copy in copies:
        copy.start()
    odd = odd_rank("gy")
    for f in range(5):
        copies[2 * f].wait()
        copies[2 * f + 1].wait()
        top, bottom = (held.at[side, f].reshape(nx * 8, nz) for side in range(2))
        for r in range(halo):
            first = top[pl.ds(r, nx, stride=8), :]
            last = bottom[pl.ds(8 - halo + r, nx, stride=8), :]
            far[f, r] = jnp.where(odd, last, first)
            near[f, r] = jnp.where(odd, first, last)


def turn_in(source, turned, count):
    lanes = source.shape[-1]
    span = lanes // quarters

    @pl.loop(0, 5)
    def _(f):
        for b in range(count):
            block = source[f, pl.ds(b * lanes, lanes), :].T
            for q in range(quarters):
                turned[f, pl.ds(q * count + b, span, stride=quarters * count), :] = block[q * span : (q + 1) * span]


def turn_out(turned, count, store):
    lanes = turned.shape[-1]
    span = lanes // quarters
    for f in range(5):
        for b in range(count):
            parts = [turned[f, pl.ds(q * count + b, span, stride=quarters * count), :] for q in range(quarters)]
            store(f, b, jnp.concatenate(parts, axis=0).T)


def ends(turned, count, far, near):
    span = turned.shape[1] // (quarters * count)
    odd = odd_rank("gz")
    for f in range(5):
        for k in range(halo):
            upward = turned[f, row((span - halo + k + 1) * quarters * count - 8), :]
            downward = turned[f, row(k * quarters * count), :]
            far[f, k] = jnp.where(odd, upward, downward)
            near[f, k] = jnp.where(odd, downward, upward)


def z_sweep(own, far, near, swept, count):
    left, right = sides_of("gz", far, near)
    width = quarters * count
    span = own.shape[1] // width
    place = lax.broadcasted_iota(jnp.int32, (8, own.shape[-1]), 0)
    for start in range(0, width, 8):

        def load(i):
            if 0 <= i < span:
                return [own[f, row(i * width + start), :] for f in range(5)]
            if i < 0:
                fields = [own[f, row((i + span) * width + start - count), :] for f in range(5)]
                if start == 0:
                    fields = [jnp.where(place < count, pltpu.roll(left[f, i + halo], count, 0), a) for f, a in enumerate(fields)]
                return fields
            fields = [own[f, row((i - span) * width + start + count), :] for f in range(5)]
            if start + 8 == width:
                fields = [jnp.where(place >= 8 - count, pltpu.roll(right[f, i - span], 8 - count, 0), a) for f, a in enumerate(fields)]
            return fields

        line = Line(load, 2)
        for i in range(span):
            for f, value in enumerate(line.swept(i)):
                swept[f, row(i * width + start), :] = value


def inner_kernel(density, momentum, energy, turned, far, near, rim, joint, held, inner):
    nx, ny, lanes = density.shape
    deep = lanes // nx
    sources = fields_of(density, momentum, energy)

    @pl.loop(0, ny // 8)
    def _(tile):
        start = pl.multiple_of(tile * 8, 8)
        line = Line(lambda i: [s[i, pl.ds(start, 8), :] for s in sources], 0, nx)
        for i in range(nx):
            for f, value in enumerate(line.swept(i)):
                held[f, pl.ds(pl.multiple_of(i * ny + start, 8), 8), :] = value

    @pl.loop(0, nx // 8)
    def _(tile):
        some = pl.ds(pl.multiple_of(tile * 8, 8), 8)
        line = Line(lambda i: [held[f, pl.ds(tile * (8 * ny) + i, 8, stride=ny), :] for f in range(5)], 1)
        for i in range(deep, ny - deep):
            for f, value in enumerate(line.swept(i)):
                inner[f, pl.ds(pl.multiple_of((i - deep) * nx + tile * 8, 8), 8), :] = value
        for f in range(5):
            joint[f, 0, some, :] = line.flux(deep - 1)[f]
            joint[f, 1, some, :] = line.flux(ny - deep - 1)[f]
        kept = deep + halo - 1
        for r in range(kept):
            for f, (a, b) in enumerate(zip(line.load(r), line.load(ny - kept + r))):
                rim[f, r, some, :] = a
                rim[f, kept + r, some, :] = b

    count = ny // deep - 2
    turn_in(inner, turned, count)
    ends(turned, count, far, near)


def edge_kernel(far, near, rim, joint, _, turned, far_end, near_end, ghost, outer):
    _, kept, nx, lanes = rim.shape
    kept = kept // 2
    deep = lanes // nx
    ahead, behind = shifts(0, nx)
    for side, source in enumerate(sides_of("gy", far, near)):

        @pl.loop(0, halo)
        def _(r):
            fields = [source[f, r] for f in range(5)]
            flux = rolled(fields, ahead, behind, 0)
            for f in range(5):
                ghost[f, side * halo + r] = fields[f] - (flux[f] - behind(flux[f]))

    @pl.loop(0, nx // 8)
    def _(tile):
        some = pl.ds(pl.multiple_of(tile * 8, 8), 8)
        for side in range(2):

            def load(i):
                if side == 0:
                    source, at = (ghost, i + halo) if i < 0 else (rim, i)
                else:
                    source, at = (ghost, i - deep + halo) if i >= deep else (rim, i + kept + kept - deep)
                return [source[f, at, some, :] for f in range(5)]

            line = Line(load, 1)
            known = deep - 1 if side == 0 else -1
            line.known[("f", known)] = [joint[f, side, some, :] for f in range(5)]
            for i in range(deep):
                for f, value in enumerate(line.swept(i)):
                    outer[f, pl.ds(pl.multiple_of((side * deep + i) * nx + tile * 8, 8), 8), :] = value

    turn_in(outer, turned, 2)
    ends(turned, 2, far_end, near_end)


def inner_z_kernel(count, own, far, near, out, swept):
    lanes = own.shape[-1]
    z_sweep(own, far, near, swept, count)

    def store(f, b, block):
        out[f, pl.ds(b * lanes, lanes), :] = block

    turn_out(swept, count, store)


def edge_z_kernel(ny, own, far, near, inner, density, momentum, energy, swept):
    lanes = own.shape[-1]
    nx = density.shape[0] // ny
    deep = lanes // nx
    outs = fields_of(density, momentum, energy)
    z_sweep(own, far, near, swept, 2)
    for f in range(5):
        for i in range(deep, ny - deep):
            outs[f][pl.ds(i, nx, stride=ny), :] = inner[f, pl.ds((i - deep) * nx, nx), :]

    def store(f, b, block):
        for r in range(deep):
            outs[f][pl.ds(b * (ny - deep) + r, nx, stride=ny), :] = block[r * nx : (r + 1) * nx]

    turn_out(swept, 2, store)


def call(kernel, shapes, scratch, arguments, in_specs=None):
    whole = pl.BlockSpec(memory_space=pltpu.VMEM)
    return pl.pallas_call(
        kernel,
        out_shape=[jax.ShapeDtypeStruct(shape, jnp.float32) for shape in shapes],
        in_specs=[whole] * len(arguments) if in_specs is None else in_specs,
        out_specs=[whole] * len(shapes),
        scratch_shapes=[pltpu.VMEM(shape, jnp.float32) for shape in scratch],
        compiler_params=pltpu.CompilerParams(vmem_limit_bytes=24 * 2**20),
    )(*arguments)


def exchange(axis, far, near):
    ranks = lax.axis_size(axis)
    if ranks % 2:
        raise ValueError("odd ring")
    pairs = []
    for start in (1, 0):
        there = [(rank, (rank + 1) % ranks) for rank in range(start, ranks, 2)]
        pairs.append(there + [(b, a) for a, b in there])
    return lax.ppermute(far, axis, pairs[0]), lax.ppermute(near, axis, pairs[1])


def y_rows(density, momentum, energy):
    nx, ny, nz = density.shape
    shape = (5, halo, nx, nz)
    return pl.pallas_call(
        rows_kernel,
        out_shape=[pltpu.VMEM(shape, jnp.float32)] * 2,
        in_specs=[pl.BlockSpec(memory_space=pltpu.HBM)] * 3,
        out_specs=[pl.BlockSpec(memory_space=pltpu.VMEM)] * 2,
        scratch_shapes=[pltpu.VMEM((2, 5, nx, 8, nz), jnp.float32), pltpu.SemaphoreType.DMA((2, 5))],
        compiler_params=pltpu.CompilerParams(vmem_limit_bytes=16 * 2**20),
    )(*(pltpu.with_memory_space_constraint(a, pltpu.HBM) for a in (density, momentum, energy)))


def body(density, momentum, energy):
    nx, ny, nz = density.shape
    deep = nz // nx
    count = ny // deep - 2
    kept = deep + halo - 1
    end = (5, halo, 8, nz)

    far_rows, near_rows = exchange("gy", *y_rows(density, momentum, energy))
    turned, far, near, rim, joint = call(
        inner_kernel,
        [(5, count * nz, nz), end, end, (5, 2 * kept, nx, nz), (5, 2, nx, nz)],
        [(5, nx * ny, nz), (5, count * nz, nz)],
        [density, momentum, energy],
    )
    far, near = exchange("gz", far, near)
    (inner,) = call(
        functools.partial(inner_z_kernel, count),
        [(5, count * nz, nz)],
        [(5, count * nz, nz)],
        [turned, far, near],
    )
    whole = pl.BlockSpec(memory_space=pltpu.VMEM)
    turned, far, near = call(
        edge_kernel,
        [(5, 2 * nz, nz), end, end],
        [(5, 2 * halo, nx, nz), (5, 2 * nz, nz)],
        [far_rows, near_rows, rim, joint, inner],
        [whole] * 4 + [pl.BlockSpec(memory_space=pl.ANY)],
    )
    far, near = exchange("gz", far, near)
    cells = nx * ny
    outs = call(
        functools.partial(edge_z_kernel, ny),
        [(cells, nz), (3, cells, nz), (cells, nz)],
        [(5, 2 * nz, nz)],
        [turned, far, near, inner],
    )
    return (outs[0].reshape(nx, ny, nz), outs[1].reshape(3, nx, ny, nz), outs[2].reshape(nx, ny, nz))


def solution(mesh):
    return jax.shard_map(
        body,
        mesh=mesh,
        in_specs=(P(None, "gy", "gz"), P(None, None, "gy", "gz"), P(None, "gy", "gz")),
        out_specs=(P(None, "gy", "gz"), P(None, None, "gy", "gz"), P(None, "gy", "gz")),
        check_vma=False,
    )
```

```python
import functools

import jax
import jax.numpy as jnp
from jax import lax
from jax.experimental import pallas as pl
from jax.experimental.pallas import tpu as pltpu
from jax.sharding import PartitionSpec as P

adiabatic = 1.4
courant = 0.15
halo = 3
quarters = 4


def primitives(fields):
    density, mx, my, mz, energy = fields
    inverse = pl.reciprocal(density, approx=True)
    vx, vy, vz = mx * inverse, my * inverse, mz * inverse
    doubled = mx * vx + my * vy + mz * vz
    pressure = (adiabatic - 1.0) * energy - (0.5 * (adiabatic - 1.0)) * doubled
    return [density, vx, vy, vz, pressure]


def half_slope(ahead, behind):
    top = jnp.maximum(jnp.minimum(ahead, behind), 0.0)
    bottom = jnp.minimum(jnp.maximum(ahead, behind), 0.0)
    return jnp.maximum(jnp.minimum(0.25 * (ahead + behind), top), bottom)


def face_offset(ahead, slope, slope_next):
    offset = 0.5 * ahead - (1.0 / 3.0) * (slope_next - slope)
    return jnp.minimum(jnp.maximum(offset, jnp.minimum(ahead, 0.0)), jnp.maximum(ahead, 0.0))


def limited(first, second):
    doubled = second + second
    return jnp.maximum(jnp.minimum(first, jnp.maximum(doubled, 0.0)), jnp.minimum(doubled, 0.0))


def hll(left, right, normal):
    dl, pl_, ul = left[0], left[4], left[1 + normal]
    dr, pr, ur = right[0], right[4], right[1 + normal]
    tl = adiabatic * pl_
    tr = adiabatic * pr
    al = tl * lax.rsqrt(tl * dl)
    ar = tr * lax.rsqrt(tr * dr)
    slowest = jnp.minimum(jnp.minimum(ul - al, ur - ar), 0.0)
    fastest = jnp.maximum(jnp.maximum(ul + al, ur + ar), 0.0)
    cl = fastest * (courant * pl.reciprocal(fastest - slowest, approx=True))
    cr = courant - cl
    wl = cl * (ul - slowest)
    wr = cr * (ur - fastest)
    ml = wl * dl
    mr = wr * dr
    ql = cl * pl_
    qr = cr * pr
    gl = [ml * left[1 + k] for k in range(3)]
    gr = [mr * right[1 + k] for k in range(3)]
    kinetic = (
        gl[0] * left[1] + gl[1] * left[2] + gl[2] * left[3]
        + gr[0] * right[1] + gr[1] * right[2] + gr[2] * right[3]
    )
    flux = [ml + mr] + [gl[k] + gr[k] for k in range(3)]
    flux[1 + normal] = flux[1 + normal] + (ql + qr)
    inner = (1.0 / (adiabatic - 1.0)) * (wl * pl_ + wr * pr)
    flux.append(0.5 * kinetic + inner + (ql * ul + qr * ur))
    return flux


class Line:
    def __init__(self, load, normal, period=None):
        self.load, self.normal, self.period = load, normal, period
        self.known = {}

    def once(self, name, index, make):
        if self.period is not None:
            index = index % self.period
        if (name, index) not in self.known:
            self.known[(name, index)] = make(index)
        return self.known[(name, index)]

    def prims(self, i):
        return self.once("q", i, lambda i: primitives(self.load(i)))

    def diff(self, i):
        return self.once("d", i, lambda i: [b - a for a, b in zip(self.prims(i), self.prims(i + 1))])

    def slope(self, i):
        return self.once("s", i, lambda i: [half_slope(a, b) for a, b in zip(self.diff(i), self.diff(i - 1))])

    def up(self, i):
        return self.once("u", i, lambda i: [face_offset(d, s, t) for d, s, t in zip(self.diff(i), self.slope(i), self.slope(i + 1))])

    def down(self, i):
        return self.once("w", i, lambda i: [d - u for d, u in zip(self.diff(i - 1), self.up(i - 1))])

    def low(self, i):
        return self.once("l", i, lambda i: [q - limited(w, u) for q, w, u in zip(self.prims(i), self.down(i), self.up(i))])

    def high(self, i):
        return self.once("h", i, lambda i: [q + limited(u, w) for q, w, u in zip(self.prims(i), self.down(i), self.up(i))])

    def flux(self, i):
        return self.once("f", i, lambda i: hll(self.high(i), self.low(i + 1), self.normal))

    def swept(self, i):
        before, after = self.flux(i - 1), self.flux(i)
        return [u - (b - a) for u, a, b in zip(self.load(i), before, after)]


def rolled(fields, ahead, behind, normal):
    states = primitives(fields)
    low, high = [], []
    for q in states:
        d = ahead(q) - q
        s = half_slope(d, behind(d))
        u = face_offset(d, s, ahead(s))
        w = behind(d - u)
        low.append(ahead(q - limited(w, u)))
        high.append(q + limited(u, w))
    return hll(high, low, normal)


def shifts(axis, size):
    return (lambda a: pltpu.roll(a, size - 1, axis), lambda a: pltpu.roll(a, 1, axis))


def row(index):
    return pl.ds(index, 8)


def fields_of(density, momentum, energy):
    return [density, momentum.at[0], momentum.at[1], momentum.at[2], energy]


def odd_rank(axis):
    return lax.axis_index(axis) % 2 == 1


class Received:
    def __init__(self, odd, on_odd, on_even):
        self.odd, self.on_odd, self.on_even = odd, on_odd, on_even

    def __getitem__(self, index):
        return jnp.where(self.odd, self.on_odd[index], self.on_even[index])


def sides_of(axis, far, near):
    odd = odd_rank(axis)
    return Received(odd, near, far), Received(odd, far, near)


def rows_kernel(density, momentum, energy, far, near, held, arrived):
    sources = fields_of(density, momentum, energy)
    nx, ny, nz = density.shape
    copies = []
    for f in range(5):
        for side in range(2):
            tile = sources[f].at[:, pl.ds(side * (ny - 8), 8), :]
            copies.append(pltpu.make_async_copy(tile, held.at[side, f], arrived.at[side, f]))
    for copy in copies:
        copy.start()
    odd = odd_rank("gy")
    for f in range(5):
        copies[2 * f].wait()
        copies[2 * f + 1].wait()
        top, bottom = (held.at[side, f].reshape(nx * 8, nz) for side in range(2))
        for r in range(halo):
            first = top[pl.ds(r, nx, stride=8), :]
            last = bottom[pl.ds(8 - halo + r, nx, stride=8), :]
            far[f, r] = jnp.where(odd, last, first)
            near[f, r] = jnp.where(odd, first, last)


def turn_in(source, turned, count):
    lanes = source.shape[-1]
    span = lanes // quarters

    @pl.loop(0, 5)
    def _(f):
        for b in range(count):
            block = source[f, pl.ds(b * lanes, lanes), :].T
            for q in range(quarters):
                turned[f, pl.ds(q * count + b, span, stride=quarters * count), :] = block[q * span : (q + 1) * span]


def turn_out(turned, count, f, store):
    lanes = turned.shape[-1]
    span = lanes // quarters
    for b in range(count):
        parts = [turned[f, pl.ds(q * count + b, span, stride=quarters * count), :] for q in range(quarters)]
        store(f, b, jnp.concatenate(parts, axis=0).T)


def ends(turned, count, far, near):
    span = turned.shape[1] // (quarters * count)
    odd = odd_rank("gz")
    for f in range(5):
        for k in range(halo):
            upward = turned[f, row((span - halo + k + 1) * quarters * count - 8), :]
            downward = turned[f, row(k * quarters * count), :]
            far[f, k] = jnp.where(odd, upward, downward)
            near[f, k] = jnp.where(odd, downward, upward)


def z_lines(own, count, left=None, right=None):
    width = quarters * count
    span = own.shape[1] // width
    place = lax.broadcasted_iota(jnp.int32, (8, own.shape[-1]), 0)
    for start in range(0, width, 8):

        def load(i, start=start):
            if 0 <= i < span:
                return [own[f, row(i * width + start), :] for f in range(5)]
            if i < 0:
                fields = [own[f, row((i + span) * width + start - count), :] for f in range(5)]
                if start == 0:
                    fields = [jnp.where(place < count, pltpu.roll(left[f, i + halo], count, 0), a) for f, a in enumerate(fields)]
                return fields
            fields = [own[f, row((i - span) * width + start + count), :] for f in range(5)]
            if start + 8 == width:
                fields = [jnp.where(place >= 8 - count, pltpu.roll(right[f, i - span], 8 - count, 0), a) for f, a in enumerate(fields)]
            return fields

        yield start, span, Line(load, 2)


def z_middle(own, swept, joint, count):
    for start, span, line in z_lines(own, count):
        for i in range(halo, span - halo):
            for f, value in enumerate(line.swept(i)):
                swept[f, row(i * quarters * count + start), :] = value
        for end, face in enumerate((halo - 1, span - halo - 1)):
            for f, value in enumerate(line.flux(face)):
                joint[f, end, row(start), :] = value


def z_ends(own, far, near, middle, joint, swept, count):
    for start, span, line in z_lines(own, count, *sides_of("gz", far, near)):
        for end, face in enumerate((halo - 1, span - halo - 1)):
            line.known[("f", face)] = [joint[f, end, row(start), :] for f in range(5)]
        for i in range(span):
            at = row(i * quarters * count + start)
            inside = halo <= i < span - halo
            values = [middle[f, at, :] for f in range(5)] if inside else line.swept(i)
            for f, value in enumerate(values):
                swept[f, at, :] = value


def inner_kernel(density, momentum, energy, turned, far, near, rim, joint, held, inner):
    nx, ny, lanes = density.shape
    deep = lanes // nx
    sources = fields_of(density, momentum, energy)

    @pl.loop(0, ny // 8)
    def _(tile):
        start = pl.multiple_of(tile * 8, 8)
        line = Line(lambda i: [s[i, pl.ds(start, 8), :] for s in sources], 0, nx)
        for i in range(nx):
            for f, value in enumerate(line.swept(i)):
                held[f, pl.ds(pl.multiple_of(i * ny + start, 8), 8), :] = value

    @pl.loop(0, nx // 8)
    def _(tile):
        some = pl.ds(pl.multiple_of(tile * 8, 8), 8)
        line = Line(lambda i: [held[f, pl.ds(tile * (8 * ny) + i, 8, stride=ny), :] for f in range(5)], 1)
        for i in range(deep, ny - deep):
            for f, value in enumerate(line.swept(i)):
                inner[f, pl.ds(pl.multiple_of((i - deep) * nx + tile * 8, 8), 8), :] = value
        for f in range(5):
            joint[f, 0, some, :] = line.flux(deep - 1)[f]
            joint[f, 1, some, :] = line.flux(ny - deep - 1)[f]
        kept = deep + halo - 1
        for r in range(kept):
            for f, (a, b) in enumerate(zip(line.load(r), line.load(ny - kept + r))):
                rim[f, r, some, :] = a
                rim[f, kept + r, some, :] = b

    count = ny // deep - 2
    turn_in(inner, turned, count)
    ends(turned, count, far, near)


def edge_kernel(far, near, rim, joint, _, turned, far_end, near_end, ghost, outer):
    _, kept, nx, lanes = rim.shape
    kept = kept // 2
    deep = lanes // nx
    ahead, behind = shifts(0, nx)
    for side, source in enumerate(sides_of("gy", far, near)):

        @pl.loop(0, halo)
        def _(r):
            fields = [source[f, r] for f in range(5)]
            flux = rolled(fields, ahead, behind, 0)
            for f in range(5):
                ghost[f, side * halo + r] = fields[f] - (flux[f] - behind(flux[f]))

    @pl.loop(0, nx // 8)
    def _(tile):
        some = pl.ds(pl.multiple_of(tile * 8, 8), 8)
        for side in range(2):

            def load(i):
                if side == 0:
                    source, at = (ghost, i + halo) if i < 0 else (rim, i)
                else:
                    source, at = (ghost, i - deep + halo) if i >= deep else (rim, i + kept + kept - deep)
                return [source[f, at, some, :] for f in range(5)]

            line = Line(load, 1)
            known = deep - 1 if side == 0 else -1
            line.known[("f", known)] = [joint[f, side, some, :] for f in range(5)]
            for i in range(deep):
                for f, value in enumerate(line.swept(i)):
                    outer[f, pl.ds(pl.multiple_of((side * deep + i) * nx + tile * 8, 8), 8), :] = value

    turn_in(outer, turned, 2)
    ends(turned, 2, far_end, near_end)


def middle_kernel(count, own, swept, joint):
    z_middle(own, swept, joint, count)


def ends_kernel(count, own, far, near, middle, joint, edges, inner, edges_middle, edges_joint, swept):
    lanes = own.shape[-1]
    z_middle(edges, edges_middle, edges_joint, 2)
    z_ends(own, far, near, middle, joint, swept, count)

    def store(f, b, block):
        inner[f, pl.ds(b * lanes, lanes), :] = block

    for f in range(5):
        turn_out(swept, count, f, store)


def last_kernel(ny, own, far, near, middle, joint, inner, density, momentum, energy, swept, whole, sent):
    lanes = own.shape[-1]
    nx = density.shape[0] // ny
    deep = lanes // nx
    outs = fields_of(density, momentum, energy)
    z_ends(own, far, near, middle, joint, swept, 2)

    def store(f, b, block):
        for r in range(deep):
            whole[f, pl.ds(b * (ny - deep) + r, nx, stride=ny), :] = block[r * nx : (r + 1) * nx]

    copies = [pltpu.make_async_copy(whole.at[f], outs[f], sent.at[f]) for f in range(5)]
    for f in range(5):
        for i in range(deep, ny - deep):
            whole[f, pl.ds(i, nx, stride=ny), :] = inner[f, pl.ds((i - deep) * nx, nx), :]
        turn_out(swept, 2, f, store)
        copies[f].start()
    for copy in copies:
        copy.wait()


def call(kernel, shapes, scratch, arguments, in_specs=None, out_spec=None):
    whole = pl.BlockSpec(memory_space=pltpu.VMEM)
    return pl.pallas_call(
        kernel,
        out_shape=[jax.ShapeDtypeStruct(shape, jnp.float32) for shape in shapes],
        in_specs=[whole] * len(arguments) if in_specs is None else in_specs,
        out_specs=[whole if out_spec is None else out_spec] * len(shapes),
        scratch_shapes=[pltpu.VMEM(a, jnp.float32) if isinstance(a, tuple) else a for a in scratch],
        compiler_params=pltpu.CompilerParams(vmem_limit_bytes=24 * 2**20),
    )(*arguments)


def exchange(axis, far, near):
    ranks = lax.axis_size(axis)
    if ranks % 2:
        raise ValueError("odd ring")
    pairs = []
    for start in (1, 0):
        there = [(rank, (rank + 1) % ranks) for rank in range(start, ranks, 2)]
        pairs.append(there + [(b, a) for a, b in there])
    return lax.ppermute(far, axis, pairs[0]), lax.ppermute(near, axis, pairs[1])


def y_rows(density, momentum, energy):
    nx, ny, nz = density.shape
    shape = (5, halo, nx, nz)
    return pl.pallas_call(
        rows_kernel,
        out_shape=[pltpu.VMEM(shape, jnp.float32)] * 2,
        in_specs=[pl.BlockSpec(memory_space=pltpu.HBM)] * 3,
        out_specs=[pl.BlockSpec(memory_space=pltpu.VMEM)] * 2,
        scratch_shapes=[pltpu.VMEM((2, 5, nx, 8, nz), jnp.float32), pltpu.SemaphoreType.DMA((2, 5))],
        compiler_params=pltpu.CompilerParams(vmem_limit_bytes=16 * 2**20),
    )(*(pltpu.with_memory_space_constraint(a, pltpu.HBM) for a in (density, momentum, energy)))


def body(density, momentum, energy):
    nx, ny, nz = density.shape
    deep = nz // nx
    count = ny // deep - 2
    kept = deep + halo - 1
    end = (5, halo, 8, nz)

    far_rows, near_rows = exchange("gy", *y_rows(density, momentum, energy))
    turned, far, near, rim, joint = call(
        inner_kernel,
        [(5, count * nz, nz), end, end, (5, 2 * kept, nx, nz), (5, 2, nx, nz)],
        [(5, nx * ny, nz), (5, count * nz, nz)],
        [density, momentum, energy],
    )
    far, near = exchange("gz", far, near)
    middle, faces = call(
        functools.partial(middle_kernel, count),
        [(5, count * nz, nz), (5, 2, quarters * count, nz)],
        [],
        [turned],
    )
    whole, anywhere = (pl.BlockSpec(memory_space=space) for space in (pltpu.VMEM, pl.ANY))
    edges, far_edges, near_edges = call(
        edge_kernel,
        [(5, 2 * nz, nz), end, end],
        [(5, 2 * halo, nx, nz), (5, 2 * nz, nz)],
        [far_rows, near_rows, rim, joint, faces],
        [whole] * 4 + [anywhere],
    )
    far_edges, near_edges = exchange("gz", far_edges, near_edges)
    inner, edges_middle, edges_faces = call(
        functools.partial(ends_kernel, count),
        [(5, count * nz, nz), (5, 2 * nz, nz), (5, 2, quarters * 2, nz)],
        [(5, count * nz, nz)],
        [turned, far, near, middle, faces, edges],
    )
    cells = nx * ny
    outs = call(
        functools.partial(last_kernel, ny),
        [(cells, nz), (3, cells, nz), (cells, nz)],
        [(5, 2 * nz, nz), (5, cells, nz), pltpu.SemaphoreType.DMA((5,))],
        [edges, far_edges, near_edges, edges_middle, edges_faces, inner],
        out_spec=anywhere,
    )
    return (outs[0].reshape(nx, ny, nz), outs[1].reshape(3, nx, ny, nz), outs[2].reshape(nx, ny, nz))


def solution(mesh):
    return jax.shard_map(
        body,
        mesh=mesh,
        in_specs=(P(None, "gy", "gz"), P(None, None, "gy", "gz"), P(None, "gy", "gz")),
        out_specs=(P(None, "gy", "gz"), P(None, None, "gy", "gz"), P(None, "gy", "gz")),
        check_vma=False,
    )
```

```python
import functools

import jax
import jax.numpy as jnp
from jax import lax
from jax.experimental import pallas as pl
from jax.experimental.pallas import tpu as pltpu
from jax.sharding import PartitionSpec as P

adiabatic = 1.4
courant = 0.15
halo = 3
quarters = 4


def primitives(fields):
    density, mx, my, mz, energy = fields
    inverse = pl.reciprocal(density, approx=True)
    vx, vy, vz = mx * inverse, my * inverse, mz * inverse
    doubled = mx * vx + my * vy + mz * vz
    pressure = (adiabatic - 1.0) * energy - (0.5 * (adiabatic - 1.0)) * doubled
    return [density, vx, vy, vz, pressure]


def signed(step):
    return step, jnp.maximum(step, 0.0), jnp.minimum(step, 0.0)


def half_slope(ahead, behind):
    top = jnp.minimum(ahead[1], behind[1])
    bottom = jnp.maximum(ahead[2], behind[2])
    return jnp.maximum(jnp.minimum(0.25 * (ahead[0] + behind[0]), top), bottom)


def face_offset(ahead, slope, slope_next):
    offset = 0.5 * ahead[0] - (1.0 / 3.0) * (slope_next - slope)
    return jnp.minimum(jnp.maximum(offset, ahead[2]), ahead[1])


def limited(first, second):
    doubled = second + second
    return jnp.maximum(jnp.minimum(first, jnp.maximum(doubled, 0.0)), jnp.minimum(doubled, 0.0))


def hll(left, right, normal):
    dl, pl_, ul = left[0], left[4], left[1 + normal]
    dr, pr, ur = right[0], right[4], right[1 + normal]
    tl = adiabatic * pl_
    tr = adiabatic * pr
    al = tl * lax.rsqrt(tl * dl)
    ar = tr * lax.rsqrt(tr * dr)
    slowest = jnp.minimum(jnp.minimum(ul - al, ur - ar), 0.0)
    fastest = jnp.maximum(jnp.maximum(ul + al, ur + ar), 0.0)
    cl = fastest * (courant * pl.reciprocal(fastest - slowest, approx=True))
    cr = courant - cl
    wl = cl * (ul - slowest)
    wr = cr * (ur - fastest)
    ml = wl * dl
    mr = wr * dr
    ql = cl * pl_
    qr = cr * pr
    gl = [ml * left[1 + k] for k in range(3)]
    gr = [mr * right[1 + k] for k in range(3)]
    kinetic = (
        gl[0] * left[1] + gl[1] * left[2] + gl[2] * left[3]
        + gr[0] * right[1] + gr[1] * right[2] + gr[2] * right[3]
    )
    flux = [ml + mr] + [gl[k] + gr[k] for k in range(3)]
    flux[1 + normal] = flux[1 + normal] + (ql + qr)
    inner = (1.0 / (adiabatic - 1.0)) * (wl * pl_ + wr * pr)
    flux.append(0.5 * kinetic + inner + (ql * ul + qr * ur))
    return flux


class Line:
    def __init__(self, load, normal, period=None):
        self.load, self.normal, self.period = load, normal, period
        self.known = {}

    def once(self, name, index, make):
        if self.period is not None:
            index = index % self.period
        if (name, index) not in self.known:
            self.known[(name, index)] = make(index)
        return self.known[(name, index)]

    def prims(self, i):
        return self.once("q", i, lambda i: primitives(self.load(i)))

    def diff(self, i):
        return self.once("d", i, lambda i: [signed(b - a) for a, b in zip(self.prims(i), self.prims(i + 1))])

    def slope(self, i):
        return self.once("s", i, lambda i: [half_slope(a, b) for a, b in zip(self.diff(i), self.diff(i - 1))])

    def up(self, i):
        return self.once("u", i, lambda i: [face_offset(d, s, t) for d, s, t in zip(self.diff(i), self.slope(i), self.slope(i + 1))])

    def down(self, i):
        return self.once("w", i, lambda i: [d[0] - u for d, u in zip(self.diff(i - 1), self.up(i - 1))])

    def low(self, i):
        return self.once("l", i, lambda i: [q - limited(w, u) for q, w, u in zip(self.prims(i), self.down(i), self.up(i))])

    def high(self, i):
        return self.once("h", i, lambda i: [q + limited(u, w) for q, w, u in zip(self.prims(i), self.down(i), self.up(i))])

    def flux(self, i):
        return self.once("f", i, lambda i: hll(self.high(i), self.low(i + 1), self.normal))

    def swept(self, i):
        before, after = self.flux(i - 1), self.flux(i)
        return [u - (b - a) for u, a, b in zip(self.load(i), before, after)]


def rolled(fields, ahead, behind, normal):
    states = primitives(fields)
    low, high = [], []
    for q in states:
        d = ahead(q) - q
        s = half_slope(signed(d), signed(behind(d)))
        u = face_offset(signed(d), s, ahead(s))
        w = behind(d - u)
        low.append(ahead(q - limited(w, u)))
        high.append(q + limited(u, w))
    return hll(high, low, normal)


def shifts(axis, size):
    return (lambda a: pltpu.roll(a, size - 1, axis), lambda a: pltpu.roll(a, 1, axis))


def row(index):
    return pl.ds(index, 8)


def fields_of(density, momentum, energy):
    return [density, momentum.at[0], momentum.at[1], momentum.at[2], energy]


def odd_rank(axis):
    return lax.axis_index(axis) % 2 == 1


class Received:
    def __init__(self, odd, on_odd, on_even):
        self.odd, self.on_odd, self.on_even = odd, on_odd, on_even

    def __getitem__(self, index):
        return jnp.where(self.odd, self.on_odd[index], self.on_even[index])


def sides_of(axis, far, near):
    odd = odd_rank(axis)
    return Received(odd, near, far), Received(odd, far, near)


def rows_kernel(density, momentum, energy, far, near, held, arrived):
    sources = fields_of(density, momentum, energy)
    nx, ny, nz = density.shape
    copies = []
    for f in range(5):
        for side in range(2):
            tile = sources[f].at[:, pl.ds(side * (ny - 8), 8), :]
            copies.append(pltpu.make_async_copy(tile, held.at[side, f], arrived.at[side, f]))
    for copy in copies:
        copy.start()
    odd = odd_rank("gy")
    for f in range(5):
        copies[2 * f].wait()
        copies[2 * f + 1].wait()
        top, bottom = (held.at[side, f].reshape(nx * 8, nz) for side in range(2))
        for r in range(halo):
            first = top[pl.ds(r, nx, stride=8), :]
            last = bottom[pl.ds(8 - halo + r, nx, stride=8), :]
            far[f, r] = jnp.where(odd, last, first)
            near[f, r] = jnp.where(odd, first, last)


def alternate(steps, parts, others, other_parts):
    made = 0
    for part, _ in enumerate(steps):
        while made * parts < (part + 1) * other_parts:
            next(others, None)
            made += 1
    for _ in others:
        pass


def turn_in(source, turned, count, b):
    lanes = source.shape[-1]
    span = lanes // quarters
    for f in range(5):
        block = source[f].T
        for q in range(quarters):
            turned[f, pl.ds(q * count + b, span, stride=quarters * count), :] = block[q * span : (q + 1) * span]
        yield


def turn_out(turned, count, f, store):
    lanes = turned.shape[-1]
    span = lanes // quarters
    for b in range(count):
        parts = [turned[f, pl.ds(q * count + b, span, stride=quarters * count), :] for q in range(quarters)]
        store(f, b, jnp.concatenate(parts, axis=0).T)
        yield


def ends(turned, count, far, near):
    span = turned.shape[1] // (quarters * count)
    odd = odd_rank("gz")
    for f in range(5):
        for k in range(halo):
            upward = turned[f, row((span - halo + k + 1) * quarters * count - 8), :]
            downward = turned[f, row(k * quarters * count), :]
            far[f, k] = jnp.where(odd, upward, downward)
            near[f, k] = jnp.where(odd, downward, upward)


def z_lines(own, count, left=None, right=None):
    width = quarters * count
    span = own.shape[1] // width
    place = lax.broadcasted_iota(jnp.int32, (8, own.shape[-1]), 0)
    for start in range(0, width, 8):

        def load(i, start=start):
            if 0 <= i < span:
                return [own[f, row(i * width + start), :] for f in range(5)]
            if i < 0:
                fields = [own[f, row((i + span) * width + start - count), :] for f in range(5)]
                if start == 0:
                    fields = [jnp.where(place < count, pltpu.roll(left[f, i + halo], count, 0), a) for f, a in enumerate(fields)]
                return fields
            fields = [own[f, row((i - span) * width + start + count), :] for f in range(5)]
            if start + 8 == width:
                fields = [jnp.where(place >= 8 - count, pltpu.roll(right[f, i - span], 8 - count, 0), a) for f, a in enumerate(fields)]
            return fields

        yield start, span, Line(load, 2)


def z_middle(own, swept, joint, count):
    for start, span, line in z_lines(own, count):
        for i in range(halo, span - halo):
            for f, value in enumerate(line.swept(i)):
                swept[f, row(i * quarters * count + start), :] = value
            yield
        for end, face in enumerate((halo - 1, span - halo - 1)):
            for f, value in enumerate(line.flux(face)):
                joint[f, end, row(start), :] = value


def z_ends(own, far, near, middle, joint, swept, count):
    for start, span, line in z_lines(own, count, *sides_of("gz", far, near)):
        for end, face in enumerate((halo - 1, span - halo - 1)):
            line.known[("f", face)] = [joint[f, end, row(start), :] for f in range(5)]
        for i in range(span):
            at = row(i * quarters * count + start)
            inside = halo <= i < span - halo
            values = [middle[f, at, :] for f in range(5)] if inside else line.swept(i)
            for f, value in enumerate(values):
                swept[f, at, :] = value


def inner_kernel(density, momentum, energy, turned, far, near, rim, joint, held, *strips):
    nx, ny, lanes = density.shape
    deep = lanes // nx
    sources = fields_of(density, momentum, energy)

    @pl.loop(0, ny // 8)
    def _(tile):
        start = pl.multiple_of(tile * 8, 8)
        line = Line(lambda i: [s[i, pl.ds(start, 8), :] for s in sources], 0, nx)
        for i in range(nx):
            for f, value in enumerate(line.swept(i)):
                held[f, pl.ds(pl.multiple_of(i * ny + start, 8), 8), :] = value

    def sweep(tile):
        some = row(tile * 8)
        line = Line(lambda i: [held[f, pl.ds(tile * (8 * ny) + i, 8, stride=ny), :] for f in range(5)], 1)
        for i in range(deep, ny - deep):
            for f, value in enumerate(line.swept(i)):
                strips[tile][f, row((i - deep) * 8), :] = value
            yield
        for f in range(5):
            joint[f, 0, some, :] = line.flux(deep - 1)[f]
            joint[f, 1, some, :] = line.flux(ny - deep - 1)[f]
        kept = deep + halo - 1
        for r in range(kept):
            for f, (a, b) in enumerate(zip(line.load(r), line.load(ny - kept + r))):
                rim[f, r, some, :] = a
                rim[f, kept + r, some, :] = b

    count = len(strips)
    turns = iter(())
    for tile in range(count):
        alternate(sweep(tile), ny - 2 * deep, turns, 5)
        turns = turn_in(strips[tile], turned, count, tile)
    for _ in turns:
        pass
    ends(turned, count, far, near)


def edge_kernel(far, near, rim, joint, _, turned, far_end, near_end, ghost, *outers):
    _, kept, nx, lanes = rim.shape
    kept = kept // 2
    deep = lanes // nx
    ahead, behind = shifts(0, nx)
    for side, source in enumerate(sides_of("gy", far, near)):

        @pl.loop(0, halo)
        def _(r):
            fields = [source[f, r] for f in range(5)]
            flux = rolled(fields, ahead, behind, 0)
            for f in range(5):
                ghost[f, side * halo + r] = fields[f] - (flux[f] - behind(flux[f]))

    share = nx // 8 // len(outers)

    def sweep(block):
        for half in range(share):
            some = row((block * share + half) * 8)
            for side in range(2):

                def load(i, side=side, some=some):
                    if side == 0:
                        source, at = (ghost, i + halo) if i < 0 else (rim, i)
                    else:
                        source, at = (ghost, i - deep + halo) if i >= deep else (rim, i + kept + kept - deep)
                    return [source[f, at, some, :] for f in range(5)]

                line = Line(load, 1)
                known = deep - 1 if side == 0 else -1
                line.known[("f", known)] = [joint[f, side, some, :] for f in range(5)]
                for i in range(deep):
                    for f, value in enumerate(line.swept(i)):
                        outers[block][f, row(((half * 2 + side) * deep + i) * 8), :] = value
                    yield

    turns = iter(())
    for block, outer in enumerate(outers):
        alternate(sweep(block), share * 2 * deep, turns, 5)
        turns = turn_in(outer, turned, len(outers), block)
    for _ in turns:
        pass
    ends(turned, 2, far_end, near_end)


def middle_kernel(count, own, swept, joint):
    for _ in z_middle(own, swept, joint, count):
        pass


def ends_kernel(count, own, far, near, middle, joint, edges, inner, edges_middle, edges_joint, swept):
    lanes = own.shape[-1]
    z_ends(own, far, near, middle, joint, swept, count)

    def store(f, b, block):
        inner[f, pl.ds(b * lanes, lanes), :] = block

    cells = edges.shape[1] // (quarters * 2) - 2 * halo
    turns = (None for f in range(5) for _ in turn_out(swept, count, f, store))
    alternate(z_middle(edges, edges_middle, edges_joint, 2), cells, turns, 5 * count)


def last_kernel(ny, own, far, near, middle, joint, inner, density, momentum, energy, swept, whole, sent):
    lanes = own.shape[-1]
    nx = density.shape[0] // ny
    deep = lanes // nx
    strip = 2 * deep * 8
    outs = fields_of(density, momentum, energy)
    z_ends(own, far, near, middle, joint, swept, 2)

    def store(f, b, block):
        for half in range(lanes // strip):
            for k in range(2 * deep):
                y = k if k < deep else ny - 2 * deep + k
                at = half * strip + k * 8
                whole[f, pl.ds((b * (lanes // strip) + half) * 8 * ny + y, 8, stride=ny), :] = block[at : at + 8]

    copies = [pltpu.make_async_copy(whole.at[f], outs[f], sent.at[f]) for f in range(5)]
    for f in range(5):
        for b in range(nx // 8):
            for i in range(deep, ny - deep):
                whole[f, pl.ds(b * 8 * ny + i, 8, stride=ny), :] = inner[f, row(b * lanes + (i - deep) * 8), :]
        for _ in turn_out(swept, 2, f, store):
            pass
        copies[f].start()
    for copy in copies:
        copy.wait()


def call(kernel, shapes, scratch, arguments, in_specs=None, out_spec=None):
    whole = pl.BlockSpec(memory_space=pltpu.VMEM)
    return pl.pallas_call(
        kernel,
        out_shape=[jax.ShapeDtypeStruct(shape, jnp.float32) for shape in shapes],
        in_specs=[whole] * len(arguments) if in_specs is None else in_specs,
        out_specs=[whole if out_spec is None else out_spec] * len(shapes),
        scratch_shapes=[pltpu.VMEM(a, jnp.float32) if isinstance(a, tuple) else a for a in scratch],
        compiler_params=pltpu.CompilerParams(vmem_limit_bytes=24 * 2**20),
    )(*arguments)


def exchange(axis, far, near):
    ranks = lax.axis_size(axis)
    if ranks % 2:
        raise ValueError("odd ring")
    pairs = []
    for start in (1, 0):
        there = [(rank, (rank + 1) % ranks) for rank in range(start, ranks, 2)]
        pairs.append(there + [(b, a) for a, b in there])
    return lax.ppermute(far, axis, pairs[0]), lax.ppermute(near, axis, pairs[1])


def y_rows(density, momentum, energy):
    nx, ny, nz = density.shape
    shape = (5, halo, nx, nz)
    return pl.pallas_call(
        rows_kernel,
        out_shape=[pltpu.VMEM(shape, jnp.float32)] * 2,
        in_specs=[pl.BlockSpec(memory_space=pltpu.HBM)] * 3,
        out_specs=[pl.BlockSpec(memory_space=pltpu.VMEM)] * 2,
        scratch_shapes=[pltpu.VMEM((2, 5, nx, 8, nz), jnp.float32), pltpu.SemaphoreType.DMA((2, 5))],
        compiler_params=pltpu.CompilerParams(vmem_limit_bytes=16 * 2**20),
    )(*(pltpu.with_memory_space_constraint(a, pltpu.HBM) for a in (density, momentum, energy)))


def body(density, momentum, energy):
    nx, ny, nz = density.shape
    deep = nz // nx
    count = ny // deep - 2
    kept = deep + halo - 1
    end = (5, halo, 8, nz)

    far_rows, near_rows = exchange("gy", *y_rows(density, momentum, energy))
    turned, far, near, rim, joint = call(
        inner_kernel,
        [(5, count * nz, nz), end, end, (5, 2 * kept, nx, nz), (5, 2, nx, nz)],
        [(5, nx * ny, nz)] + [(5, nz, nz)] * count,
        [density, momentum, energy],
    )
    far, near = exchange("gz", far, near)
    middle, faces = call(
        functools.partial(middle_kernel, count),
        [(5, count * nz, nz), (5, 2, quarters * count, nz)],
        [],
        [turned],
    )
    whole, anywhere = (pl.BlockSpec(memory_space=space) for space in (pltpu.VMEM, pl.ANY))
    edges, far_edges, near_edges = call(
        edge_kernel,
        [(5, 2 * nz, nz), end, end],
        [(5, 2 * halo, nx, nz)] + [(5, nz, nz)] * 2,
        [far_rows, near_rows, rim, joint, faces],
        [whole] * 4 + [anywhere],
    )
    far_edges, near_edges = exchange("gz", far_edges, near_edges)
    inner, edges_middle, edges_faces = call(
        functools.partial(ends_kernel, count),
        [(5, count * nz, nz), (5, 2 * nz, nz), (5, 2, quarters * 2, nz)],
        [(5, count * nz, nz)],
        [turned, far, near, middle, faces, edges],
    )
    cells = nx * ny
    outs = call(
        functools.partial(last_kernel, ny),
        [(cells, nz), (3, cells, nz), (cells, nz)],
        [(5, 2 * nz, nz), (5, cells, nz), pltpu.SemaphoreType.DMA((5,))],
        [edges, far_edges, near_edges, edges_middle, edges_faces, inner],
        out_spec=anywhere,
    )
    return (outs[0].reshape(nx, ny, nz), outs[1].reshape(3, nx, ny, nz), outs[2].reshape(nx, ny, nz))


def solution(mesh):
    return jax.shard_map(
        body,
        mesh=mesh,
        in_specs=(P(None, "gy", "gz"), P(None, None, "gy", "gz"), P(None, "gy", "gz")),
        out_specs=(P(None, "gy", "gz"), P(None, None, "gy", "gz"), P(None, "gy", "gz")),
        check_vma=False,
    )
```

```python
import functools

import jax
import jax.numpy as jnp
from jax import lax
from jax.experimental import pallas as pl
from jax.experimental.pallas import tpu as pltpu
from jax.sharding import PartitionSpec as P

adiabatic = 1.4
courant = 0.15
halo = 3
quarters = 4


def primitives(fields):
    density, mx, my, mz, energy = fields
    inverse = pl.reciprocal(density, approx=True)
    vx, vy, vz = mx * inverse, my * inverse, mz * inverse
    doubled = mx * vx + my * vy + mz * vz
    pressure = (adiabatic - 1.0) * energy - (0.5 * (adiabatic - 1.0)) * doubled
    return [density, vx, vy, vz, pressure]


def signed(step):
    return step, jnp.maximum(step, 0.0), jnp.minimum(step, 0.0)


def half_slope(ahead, behind):
    top = jnp.minimum(ahead[1], behind[1])
    bottom = jnp.maximum(ahead[2], behind[2])
    return jnp.maximum(jnp.minimum(0.25 * (ahead[0] + behind[0]), top), bottom)


def face_offset(ahead, slope, slope_next):
    offset = 0.5 * ahead[0] - (1.0 / 3.0) * (slope_next - slope)
    return jnp.minimum(jnp.maximum(offset, ahead[2]), ahead[1])


def limited(first, second):
    doubled = second + second
    return jnp.maximum(jnp.minimum(first, jnp.maximum(doubled, 0.0)), jnp.minimum(doubled, 0.0))


def hll(left, right, normal):
    dl, pl_, ul = left[0], left[4], left[1 + normal]
    dr, pr, ur = right[0], right[4], right[1 + normal]
    tl = adiabatic * pl_
    tr = adiabatic * pr
    al = tl * lax.rsqrt(tl * dl)
    ar = tr * lax.rsqrt(tr * dr)
    slowest = jnp.minimum(jnp.minimum(ul - al, ur - ar), 0.0)
    fastest = jnp.maximum(jnp.maximum(ul + al, ur + ar), 0.0)
    cl = fastest * (courant * pl.reciprocal(fastest - slowest, approx=True))
    cr = courant - cl
    wl = cl * (ul - slowest)
    wr = cr * (ur - fastest)
    ml = wl * dl
    mr = wr * dr
    ql = cl * pl_
    qr = cr * pr
    gl = [ml * left[1 + k] for k in range(3)]
    gr = [mr * right[1 + k] for k in range(3)]
    kinetic = (
        gl[0] * left[1] + gl[1] * left[2] + gl[2] * left[3]
        + gr[0] * right[1] + gr[1] * right[2] + gr[2] * right[3]
    )
    flux = [ml + mr] + [gl[k] + gr[k] for k in range(3)]
    flux[1 + normal] = flux[1 + normal] + (ql + qr)
    inner = (1.0 / (adiabatic - 1.0)) * (wl * pl_ + wr * pr)
    flux.append(0.5 * kinetic + inner + (ql * ul + qr * ur))
    return flux


class Line:
    def __init__(self, load, normal, period=None):
        self.load, self.normal, self.period = load, normal, period
        self.known = {}

    def once(self, name, index, make):
        if self.period is not None:
            index = index % self.period
        if (name, index) not in self.known:
            self.known[(name, index)] = make(index)
        return self.known[(name, index)]

    def prims(self, i):
        return self.once("q", i, lambda i: primitives(self.load(i)))

    def diff(self, i):
        return self.once("d", i, lambda i: [signed(b - a) for a, b in zip(self.prims(i), self.prims(i + 1))])

    def slope(self, i):
        return self.once("s", i, lambda i: [half_slope(a, b) for a, b in zip(self.diff(i), self.diff(i - 1))])

    def up(self, i):
        return self.once("u", i, lambda i: [face_offset(d, s, t) for d, s, t in zip(self.diff(i), self.slope(i), self.slope(i + 1))])

    def down(self, i):
        return self.once("w", i, lambda i: [d[0] - u for d, u in zip(self.diff(i - 1), self.up(i - 1))])

    def low(self, i):
        return self.once("l", i, lambda i: [q - limited(w, u) for q, w, u in zip(self.prims(i), self.down(i), self.up(i))])

    def high(self, i):
        return self.once("h", i, lambda i: [q + limited(u, w) for q, w, u in zip(self.prims(i), self.down(i), self.up(i))])

    def flux(self, i):
        return self.once("f", i, lambda i: hll(self.high(i), self.low(i + 1), self.normal))

    def swept(self, i):
        before, after = self.flux(i - 1), self.flux(i)
        return [u - (b - a) for u, a, b in zip(self.load(i), before, after)]


def rolled(fields, ahead, behind, normal):
    states = primitives(fields)
    low, high = [], []
    for q in states:
        d = ahead(q) - q
        s = half_slope(signed(d), signed(behind(d)))
        u = face_offset(signed(d), s, ahead(s))
        w = behind(d - u)
        low.append(ahead(q - limited(w, u)))
        high.append(q + limited(u, w))
    return hll(high, low, normal)


def shifts(axis, size):
    return (lambda a: pltpu.roll(a, size - 1, axis), lambda a: pltpu.roll(a, 1, axis))


def row(index):
    return pl.ds(index, 8)


def fields_of(density, momentum, energy):
    return [density, momentum.at[0], momentum.at[1], momentum.at[2], energy]


def odd_rank(axis):
    return lax.axis_index(axis) % 2 == 1


class Received:
    def __init__(self, odd, on_odd, on_even):
        self.odd, self.on_odd, self.on_even = odd, on_odd, on_even

    def __getitem__(self, index):
        return jnp.where(self.odd, self.on_odd[index], self.on_even[index])


def sides_of(axis, far, near):
    odd = odd_rank(axis)
    return Received(odd, near, far), Received(odd, far, near)


def rows_kernel(far, density, momentum, energy, out, held, arrived):
    sources = fields_of(density, momentum, energy)
    nx, ny, nz = density.shape
    bottom = odd_rank("gy") == far
    start = pl.multiple_of(jnp.where(bottom, ny - 8, 0), 8)
    copies = [pltpu.make_async_copy(s.at[:, pl.ds(start, 8), :], held.at[f], arrived.at[f]) for f, s in enumerate(sources)]
    for copy in copies:
        copy.start()
    for f in range(5):
        copies[f].wait()
        flat = held.at[f].reshape(nx * 8, nz)
        for r in range(halo):
            first, last = (flat[pl.ds(at, nx, stride=8), :] for at in (r, 8 - halo + r))
            out[f, r] = jnp.where(bottom, last, first)


def alternate(steps, parts, others, other_parts):
    made = 0
    for part, _ in enumerate(steps):
        while made * parts < (part + 1) * other_parts:
            next(others, None)
            made += 1
    for _ in others:
        pass


def turn_in(source, turned, count, b):
    lanes = source.shape[-1]
    span = lanes // quarters
    for f in range(5):
        block = source[f].T
        for q in range(quarters):
            turned[f, pl.ds(q * count + b, span, stride=quarters * count), :] = block[q * span : (q + 1) * span]
        yield


def turn_out(turned, count, f, store):
    lanes = turned.shape[-1]
    span = lanes // quarters
    for b in range(count):
        parts = [turned[f, pl.ds(q * count + b, span, stride=quarters * count), :] for q in range(quarters)]
        store(f, b, jnp.concatenate(parts, axis=0).T)
        yield


def ends(turned, count, far, near):
    span = turned.shape[1] // (quarters * count)
    odd = odd_rank("gz")
    for f in range(5):
        for k in range(halo):
            upward = turned[f, row((span - halo + k + 1) * quarters * count - 8), :]
            downward = turned[f, row(k * quarters * count), :]
            far[f, k] = jnp.where(odd, upward, downward)
            near[f, k] = jnp.where(odd, downward, upward)


def z_lines(own, count, left=None, right=None):
    width = quarters * count
    span = own.shape[1] // width
    place = lax.broadcasted_iota(jnp.int32, (8, own.shape[-1]), 0)
    for start in range(0, width, 8):

        def load(i, start=start):
            if 0 <= i < span:
                return [own[f, row(i * width + start), :] for f in range(5)]
            if i < 0:
                fields = [own[f, row((i + span) * width + start - count), :] for f in range(5)]
                if start == 0:
                    fields = [jnp.where(place < count, pltpu.roll(left[f, i + halo], count, 0), a) for f, a in enumerate(fields)]
                return fields
            fields = [own[f, row((i - span) * width + start + count), :] for f in range(5)]
            if start + 8 == width:
                fields = [jnp.where(place >= 8 - count, pltpu.roll(right[f, i - span], 8 - count, 0), a) for f, a in enumerate(fields)]
            return fields

        yield start, span, Line(load, 2)


def z_middle(own, swept, joint, count):
    for start, span, line in z_lines(own, count):
        for i in range(halo, span - halo):
            for f, value in enumerate(line.swept(i)):
                swept[f, row(i * quarters * count + start), :] = value
            yield
        for end, face in enumerate((halo - 1, span - halo - 1)):
            for f, value in enumerate(line.flux(face)):
                joint[f, end, row(start), :] = value


def z_ends(own, far, near, middle, joint, swept, count):
    for start, span, line in z_lines(own, count, *sides_of("gz", far, near)):
        for end, face in enumerate((halo - 1, span - halo - 1)):
            line.known[("f", face)] = [joint[f, end, row(start), :] for f in range(5)]
        for i in range(span):
            at = row(i * quarters * count + start)
            inside = halo <= i < span - halo
            values = [middle[f, at, :] for f in range(5)] if inside else line.swept(i)
            for f, value in enumerate(values):
                swept[f, at, :] = value


def inner_kernel(density, momentum, energy, turned, far, near, rim, joint, held, *strips):
    nx, ny, lanes = density.shape
    deep = lanes // nx
    sources = fields_of(density, momentum, energy)

    @pl.loop(0, ny // 8)
    def _(tile):
        start = pl.multiple_of(tile * 8, 8)
        line = Line(lambda i: [s[i, pl.ds(start, 8), :] for s in sources], 0, nx)
        for i in range(nx):
            for f, value in enumerate(line.swept(i)):
                held[f, pl.ds(pl.multiple_of(i * ny + start, 8), 8), :] = value

    def sweep(tile):
        some = row(tile * 8)
        line = Line(lambda i: [held[f, pl.ds(tile * (8 * ny) + i, 8, stride=ny), :] for f in range(5)], 1)
        for i in range(deep, ny - deep):
            for f, value in enumerate(line.swept(i)):
                strips[tile][f, row((i - deep) * 8), :] = value
            yield
        for f in range(5):
            joint[f, 0, some, :] = line.flux(deep - 1)[f]
            joint[f, 1, some, :] = line.flux(ny - deep - 1)[f]
        kept = deep + halo - 1
        for r in range(kept):
            for f, (a, b) in enumerate(zip(line.load(r), line.load(ny - kept + r))):
                rim[f, r, some, :] = a
                rim[f, kept + r, some, :] = b

    count = len(strips)
    turns = iter(())
    for tile in range(count):
        alternate(sweep(tile), ny - 2 * deep, turns, 5)
        turns = turn_in(strips[tile], turned, count, tile)
    for _ in turns:
        pass
    ends(turned, count, far, near)


def edge_kernel(near, far, rim, joint, _, turned, far_end, near_end, ghost, *outers):
    _, kept, nx, lanes = rim.shape
    kept = kept // 2
    deep = lanes // nx
    ahead, behind = shifts(0, nx)
    for side, source in enumerate(sides_of("gy", far, near)):

        @pl.loop(0, halo)
        def _(r):
            fields = [source[f, r] for f in range(5)]
            flux = rolled(fields, ahead, behind, 0)
            for f in range(5):
                ghost[f, side * halo + r] = fields[f] - (flux[f] - behind(flux[f]))

    share = nx // 8 // len(outers)

    def sweep(block):
        for half in range(share):
            some = row((block * share + half) * 8)
            for side in range(2):

                def load(i, side=side, some=some):
                    if side == 0:
                        source, at = (ghost, i + halo) if i < 0 else (rim, i)
                    else:
                        source, at = (ghost, i - deep + halo) if i >= deep else (rim, i + kept + kept - deep)
                    return [source[f, at, some, :] for f in range(5)]

                line = Line(load, 1)
                known = deep - 1 if side == 0 else -1
                line.known[("f", known)] = [joint[f, side, some, :] for f in range(5)]
                for i in range(deep):
                    for f, value in enumerate(line.swept(i)):
                        outers[block][f, row(((half * 2 + side) * deep + i) * 8), :] = value
                    yield

    turns = iter(())
    for block, outer in enumerate(outers):
        alternate(sweep(block), share * 2 * deep, turns, 5)
        turns = turn_in(outer, turned, len(outers), block)
    for _ in turns:
        pass
    ends(turned, 2, far_end, near_end)


def middle_kernel(count, own, swept, joint):
    for _ in z_middle(own, swept, joint, count):
        pass


def ends_kernel(count, own, near, far, middle, joint, edges, inner, edges_middle, edges_joint, swept):
    lanes = own.shape[-1]
    z_ends(own, far, near, middle, joint, swept, count)

    def store(f, b, block):
        inner[f, pl.ds(b * lanes, lanes), :] = block

    cells = edges.shape[1] // (quarters * 2) - 2 * halo
    turns = (None for f in range(5) for _ in turn_out(swept, count, f, store))
    alternate(z_middle(edges, edges_middle, edges_joint, 2), cells, turns, 5 * count)


def last_kernel(ny, own, near, far, middle, joint, inner, density, momentum, energy, swept, whole, sent):
    lanes = own.shape[-1]
    nx = density.shape[0] // ny
    deep = lanes // nx
    strip = 2 * deep * 8
    outs = fields_of(density, momentum, energy)
    z_ends(own, far, near, middle, joint, swept, 2)

    def store(f, b, block):
        for half in range(lanes // strip):
            for k in range(2 * deep):
                y = k if k < deep else ny - 2 * deep + k
                at = half * strip + k * 8
                whole[f, pl.ds((b * (lanes // strip) + half) * 8 * ny + y, 8, stride=ny), :] = block[at : at + 8]

    copies = [pltpu.make_async_copy(whole.at[f], outs[f], sent.at[f]) for f in range(5)]
    for f in range(5):
        for b in range(nx // 8):
            for i in range(deep, ny - deep):
                whole[f, pl.ds(b * 8 * ny + i, 8, stride=ny), :] = inner[f, row(b * lanes + (i - deep) * 8), :]
        for _ in turn_out(swept, 2, f, store):
            pass
        copies[f].start()
    for copy in copies:
        copy.wait()


def call(kernel, shapes, scratch, arguments, in_specs=None, out_spec=None):
    whole = pl.BlockSpec(memory_space=pltpu.VMEM)
    return pl.pallas_call(
        kernel,
        out_shape=[jax.ShapeDtypeStruct(shape, jnp.float32) for shape in shapes],
        in_specs=[whole] * len(arguments) if in_specs is None else in_specs,
        out_specs=[whole if out_spec is None else out_spec] * len(shapes),
        scratch_shapes=[pltpu.VMEM(a, jnp.float32) if isinstance(a, tuple) else a for a in scratch],
        compiler_params=pltpu.CompilerParams(vmem_limit_bytes=24 * 2**20),
    )(*arguments)


def exchange(axis, block, far):
    ranks = lax.axis_size(axis)
    if ranks % 2:
        raise ValueError("odd ring")
    there = [(rank, (rank + 1) % ranks) for rank in range(int(far), ranks, 2)]
    return lax.ppermute(block, axis, there + [(b, a) for a, b in there])


def y_rows(far, fields):
    nx, _, nz = fields[0].shape
    return pl.pallas_call(
        functools.partial(rows_kernel, far),
        out_shape=pltpu.VMEM((5, halo, nx, nz), jnp.float32),
        in_specs=[pl.BlockSpec(memory_space=pltpu.HBM)] * 3,
        out_specs=pl.BlockSpec(memory_space=pltpu.VMEM),
        scratch_shapes=[pltpu.VMEM((5, nx, 8, nz), jnp.float32), pltpu.SemaphoreType.DMA((5,))],
        compiler_params=pltpu.CompilerParams(vmem_limit_bytes=16 * 2**20),
    )(*(pltpu.with_memory_space_constraint(a, pltpu.HBM) for a in fields))


def body(density, momentum, energy):
    nx, ny, nz = density.shape
    deep = nz // nx
    count = ny // deep - 2
    kept = deep + halo - 1
    end = (5, halo, 8, nz)

    fields = (density, momentum, energy)
    near_rows, far_rows = (exchange("gy", y_rows(far, fields), far) for far in (False, True))
    turned, far, near, rim, joint = call(
        inner_kernel,
        [(5, count * nz, nz), end, end, (5, 2 * kept, nx, nz), (5, 2, nx, nz)],
        [(5, nx * ny, nz)] + [(5, nz, nz)] * count,
        list(fields),
    )
    near, far = exchange("gz", near, False), exchange("gz", far, True)
    middle, faces = call(
        functools.partial(middle_kernel, count),
        [(5, count * nz, nz), (5, 2, quarters * count, nz)],
        [],
        [turned],
    )
    whole, anywhere = (pl.BlockSpec(memory_space=space) for space in (pltpu.VMEM, pl.ANY))
    edges, far_edges, near_edges = call(
        edge_kernel,
        [(5, 2 * nz, nz), end, end],
        [(5, 2 * halo, nx, nz)] + [(5, nz, nz)] * 2,
        [near_rows, far_rows, rim, joint, faces],
        [whole] * 4 + [anywhere],
    )
    near_edges, far_edges = exchange("gz", near_edges, False), exchange("gz", far_edges, True)
    inner, edges_middle, edges_faces = call(
        functools.partial(ends_kernel, count),
        [(5, count * nz, nz), (5, 2 * nz, nz), (5, 2, quarters * 2, nz)],
        [(5, count * nz, nz)],
        [turned, near, far, middle, faces, edges],
    )
    cells = nx * ny
    outs = call(
        functools.partial(last_kernel, ny),
        [(cells, nz), (3, cells, nz), (cells, nz)],
        [(5, 2 * nz, nz), (5, cells, nz), pltpu.SemaphoreType.DMA((5,))],
        [edges, near_edges, far_edges, edges_middle, edges_faces, inner],
        out_spec=anywhere,
    )
    return (outs[0].reshape(nx, ny, nz), outs[1].reshape(3, nx, ny, nz), outs[2].reshape(nx, ny, nz))


def solution(mesh):
    return jax.shard_map(
        body,
        mesh=mesh,
        in_specs=(P(None, "gy", "gz"), P(None, None, "gy", "gz"), P(None, "gy", "gz")),
        out_specs=(P(None, "gy", "gz"), P(None, None, "gy", "gz"), P(None, "gy", "gz")),
        check_vma=False,
    )
```

```python
import functools

import jax
import jax.numpy as jnp
from jax import lax
from jax.experimental import pallas as pl
from jax.experimental.pallas import tpu as pltpu
from jax.sharding import PartitionSpec as P

adiabatic = 1.4
courant = 0.15
halo = 3
quarters = 4


def primitives(fields):
    density, mx, my, mz, energy = fields
    inverse = pl.reciprocal(density, approx=True)
    vx, vy, vz = mx * inverse, my * inverse, mz * inverse
    doubled = mx * vx + my * vy + mz * vz
    pressure = (adiabatic - 1.0) * energy - (0.5 * (adiabatic - 1.0)) * doubled
    return [density, vx, vy, vz, pressure]


def signed(step):
    return step, jnp.maximum(step, 0.0), jnp.minimum(step, 0.0)


def half_slope(ahead, behind):
    top = jnp.minimum(ahead[1], behind[1])
    bottom = jnp.maximum(ahead[2], behind[2])
    return jnp.maximum(jnp.minimum(0.25 * (ahead[0] + behind[0]), top), bottom)


def face_offset(ahead, slope, slope_next):
    offset = 0.5 * ahead[0] - (1.0 / 3.0) * (slope_next - slope)
    return jnp.minimum(jnp.maximum(offset, ahead[2]), ahead[1])


def limited(first, second):
    doubled = second + second
    return jnp.maximum(jnp.minimum(first, jnp.maximum(doubled, 0.0)), jnp.minimum(doubled, 0.0))


def hll(left, right, normal):
    dl, pl_, ul = left[0], left[4], left[1 + normal]
    dr, pr, ur = right[0], right[4], right[1 + normal]
    tl = adiabatic * pl_
    tr = adiabatic * pr
    al = tl * lax.rsqrt(tl * dl)
    ar = tr * lax.rsqrt(tr * dr)
    slowest = jnp.minimum(jnp.minimum(ul - al, ur - ar), 0.0)
    fastest = jnp.maximum(jnp.maximum(ul + al, ur + ar), 0.0)
    cl = fastest * (courant * pl.reciprocal(fastest - slowest, approx=True))
    cr = courant - cl
    wl = cl * (ul - slowest)
    wr = cr * (ur - fastest)
    ml = wl * dl
    mr = wr * dr
    ql = cl * pl_
    qr = cr * pr
    gl = [ml * left[1 + k] for k in range(3)]
    gr = [mr * right[1 + k] for k in range(3)]
    kinetic = (
        gl[0] * left[1] + gl[1] * left[2] + gl[2] * left[3]
        + gr[0] * right[1] + gr[1] * right[2] + gr[2] * right[3]
    )
    flux = [ml + mr] + [gl[k] + gr[k] for k in range(3)]
    flux[1 + normal] = flux[1 + normal] + (ql + qr)
    inner = (1.0 / (adiabatic - 1.0)) * (wl * pl_ + wr * pr)
    flux.append(0.5 * kinetic + inner + (ql * ul + qr * ur))
    return flux


class Line:
    def __init__(self, load, normal, period=None):
        self.load, self.normal, self.period = load, normal, period
        self.known = {}

    def once(self, name, index, make):
        if self.period is not None:
            index = index % self.period
        if (name, index) not in self.known:
            self.known[(name, index)] = make(index)
        return self.known[(name, index)]

    def prims(self, i):
        return self.once("q", i, lambda i: primitives(self.load(i)))

    def diff(self, i):
        return self.once("d", i, lambda i: [signed(b - a) for a, b in zip(self.prims(i), self.prims(i + 1))])

    def slope(self, i):
        return self.once("s", i, lambda i: [half_slope(a, b) for a, b in zip(self.diff(i), self.diff(i - 1))])

    def up(self, i):
        return self.once("u", i, lambda i: [face_offset(d, s, t) for d, s, t in zip(self.diff(i), self.slope(i), self.slope(i + 1))])

    def down(self, i):
        return self.once("w", i, lambda i: [d[0] - u for d, u in zip(self.diff(i - 1), self.up(i - 1))])

    def low(self, i):
        return self.once("l", i, lambda i: [q - limited(w, u) for q, w, u in zip(self.prims(i), self.down(i), self.up(i))])

    def high(self, i):
        return self.once("h", i, lambda i: [q + limited(u, w) for q, w, u in zip(self.prims(i), self.down(i), self.up(i))])

    def flux(self, i):
        return self.once("f", i, lambda i: hll(self.high(i), self.low(i + 1), self.normal))

    def swept(self, i):
        before, after = self.flux(i - 1), self.flux(i)
        return [u - (b - a) for u, a, b in zip(self.load(i), before, after)]


def rolled(fields, ahead, behind, normal):
    states = primitives(fields)
    low, high = [], []
    for q in states:
        d = ahead(q) - q
        s = half_slope(signed(d), signed(behind(d)))
        u = face_offset(signed(d), s, ahead(s))
        w = behind(d - u)
        low.append(ahead(q - limited(w, u)))
        high.append(q + limited(u, w))
    return hll(high, low, normal)


def shifts(axis, size):
    return (lambda a: pltpu.roll(a, size - 1, axis), lambda a: pltpu.roll(a, 1, axis))


def row(index):
    return pl.ds(index, 8)


def fields_of(density, momentum, energy):
    return [density, momentum.at[0], momentum.at[1], momentum.at[2], energy]


def odd_rank(axis):
    return lax.axis_index(axis) % 2 == 1


class Received:
    def __init__(self, odd, on_odd, on_even):
        self.odd, self.on_odd, self.on_even = odd, on_odd, on_even

    def __getitem__(self, index):
        return jnp.where(self.odd, self.on_odd[index], self.on_even[index])


def sides_of(axis, far, near):
    odd = odd_rank(axis)
    return Received(odd, near, far), Received(odd, far, near)


def rows_kernel(density, momentum, energy, far, near, held, arrived):
    sources = fields_of(density, momentum, energy)
    nx, ny, nz = density.shape
    copies = []
    for f in range(5):
        for side in range(2):
            tile = sources[f].at[:, pl.ds(side * (ny - 8), 8), :]
            copies.append(pltpu.make_async_copy(tile, held.at[side, f], arrived.at[side, f]))
    for copy in copies:
        copy.start()
    odd = odd_rank("gy")
    for f in range(5):
        copies[2 * f].wait()
        copies[2 * f + 1].wait()
        top, bottom = (held.at[side, f].reshape(nx * 8, nz) for side in range(2))
        for r in range(halo):
            first = top[pl.ds(r, nx, stride=8), :]
            last = bottom[pl.ds(8 - halo + r, nx, stride=8), :]
            far[f, r] = jnp.where(odd, last, first)
            near[f, r] = jnp.where(odd, first, last)


def alternate(steps, parts, others, other_parts):
    made = 0
    for part, _ in enumerate(steps):
        while made * parts < (part + 1) * other_parts:
            next(others, None)
            made += 1
    for _ in others:
        pass


def turn_in(source, turned, count, b):
    lanes = source.shape[-1]
    span = lanes // quarters
    for f in range(5):
        block = source[f].T
        for q in range(quarters):
            turned[f, pl.ds(q * count + b, span, stride=quarters * count), :] = block[q * span : (q + 1) * span]
        yield


def turn_out(turned, count, f, store):
    lanes = turned.shape[-1]
    span = lanes // quarters
    for b in range(count):
        parts = [turned[f, pl.ds(q * count + b, span, stride=quarters * count), :] for q in range(quarters)]
        store(f, b, jnp.concatenate(parts, axis=0).T)
        yield


def ends(turned, count, far, near):
    span = turned.shape[1] // (quarters * count)
    odd = odd_rank("gz")
    for f in range(5):
        for k in range(halo):
            upward = turned[f, row((span - halo + k + 1) * quarters * count - 8), :]
            downward = turned[f, row(k * quarters * count), :]
            far[f, k] = jnp.where(odd, upward, downward)
            near[f, k] = jnp.where(odd, downward, upward)


def z_lines(own, count, left=None, right=None):
    width = quarters * count
    span = own.shape[1] // width
    place = lax.broadcasted_iota(jnp.int32, (8, own.shape[-1]), 0)
    for start in range(0, width, 8):

        def load(i, start=start):
            if 0 <= i < span:
                return [own[f, row(i * width + start), :] for f in range(5)]
            if i < 0:
                fields = [own[f, row((i + span) * width + start - count), :] for f in range(5)]
                if start == 0:
                    fields = [jnp.where(place < count, pltpu.roll(left[f, i + halo], count, 0), a) for f, a in enumerate(fields)]
                return fields
            fields = [own[f, row((i - span) * width + start + count), :] for f in range(5)]
            if start + 8 == width:
                fields = [jnp.where(place >= 8 - count, pltpu.roll(right[f, i - span], 8 - count, 0), a) for f, a in enumerate(fields)]
            return fields

        yield start, span, Line(load, 2)


def z_middle(own, swept, joint, count):
    for start, span, line in z_lines(own, count):
        for i in range(halo, span - halo):
            for f, value in enumerate(line.swept(i)):
                swept[f, row(i * quarters * count + start), :] = value
            yield
        for end, face in enumerate((halo - 1, span - halo - 1)):
            for f, value in enumerate(line.flux(face)):
                joint[f, end, row(start), :] = value


def z_ends(own, far, near, middle, joint, swept, count):
    for start, span, line in z_lines(own, count, *sides_of("gz", far, near)):
        for end, face in enumerate((halo - 1, span - halo - 1)):
            line.known[("f", face)] = [joint[f, end, row(start), :] for f in range(5)]
        for i in range(span):
            at = row(i * quarters * count + start)
            inside = halo <= i < span - halo
            values = [middle[f, at, :] for f in range(5)] if inside else line.swept(i)
            for f, value in enumerate(values):
                swept[f, at, :] = value


def inner_kernel(density, momentum, energy, turned, far, near, rim, beside, joint, held, *strips):
    nx, ny, lanes = density.shape
    deep = lanes // nx
    sources = fields_of(density, momentum, energy)

    @pl.loop(0, ny // 8)
    def _(tile):
        start = pl.multiple_of(tile * 8, 8)
        line = Line(lambda i: [s[i, pl.ds(start, 8), :] for s in sources], 0, nx)
        for i in range(nx):
            for f, value in enumerate(line.swept(i)):
                held[f, pl.ds(pl.multiple_of(i * ny + start, 8), 8), :] = value

    def sweep(tile):
        some = row(tile * 8)
        line = Line(lambda i: [held[f, pl.ds(tile * (8 * ny) + i, 8, stride=ny), :] for f in range(5)], 1)
        for i in range(halo, ny - halo):
            for f, value in enumerate(line.swept(i)):
                if deep <= i < ny - deep:
                    strips[tile][f, row((i - deep) * 8), :] = value
                else:
                    beside[f, i - halo if i < deep else i - ny + 2 * deep - halo, some, :] = value
            yield
        for f in range(5):
            joint[f, 0, some, :] = line.flux(halo - 1)[f]
            joint[f, 1, some, :] = line.flux(ny - halo - 1)[f]
        kept = deep + halo - 1
        for r in range(kept):
            for f, (a, b) in enumerate(zip(line.load(r), line.load(ny - kept + r))):
                rim[f, r, some, :] = a
                rim[f, kept + r, some, :] = b

    count = len(strips)
    turns = iter(())
    for tile in range(count):
        alternate(sweep(tile), ny - 2 * halo, turns, 5)
        turns = turn_in(strips[tile], turned, count, tile)
    for _ in turns:
        pass
    ends(turned, count, far, near)


def edge_kernel(far, near, rim, beside, joint, _, turned, far_end, near_end, ghost, *outers):
    _, kept, nx, lanes = rim.shape
    kept = kept // 2
    deep = lanes // nx
    ahead, behind = shifts(0, nx)
    for side, source in enumerate(sides_of("gy", far, near)):

        @pl.loop(0, halo)
        def _(r):
            fields = [source[f, r] for f in range(5)]
            flux = rolled(fields, ahead, behind, 0)
            for f in range(5):
                ghost[f, side * halo + r] = fields[f] - (flux[f] - behind(flux[f]))

    share = nx // 8 // len(outers)

    def sweep(block):
        for half in range(share):
            some = row((block * share + half) * 8)
            for side in range(2):

                def load(i, side=side, some=some):
                    if side == 0:
                        source, at = (ghost, i + halo) if i < 0 else (rim, i)
                    else:
                        source, at = (ghost, i - deep + halo) if i >= deep else (rim, i + kept + kept - deep)
                    return [source[f, at, some, :] for f in range(5)]

                line = Line(load, 1)
                known = halo - 1 if side == 0 else deep - halo - 1
                line.known[("f", known)] = [joint[f, side, some, :] for f in range(5)]
                for i in range(deep):
                    if side == 0 and i >= halo:
                        values = [beside[f, i - halo, some, :] for f in range(5)]
                    elif side == 1 and i < deep - halo:
                        values = [beside[f, i + deep - halo, some, :] for f in range(5)]
                    else:
                        values = line.swept(i)
                    for f, value in enumerate(values):
                        outers[block][f, row(((half * 2 + side) * deep + i) * 8), :] = value
                    yield

    turns = iter(())
    for block, outer in enumerate(outers):
        alternate(sweep(block), share * 2 * deep, turns, 5)
        turns = turn_in(outer, turned, len(outers), block)
    for _ in turns:
        pass
    ends(turned, 2, far_end, near_end)


def middle_kernel(count, own, swept, joint):
    for _ in z_middle(own, swept, joint, count):
        pass


def ends_kernel(count, own, far, near, middle, joint, edges, inner, edges_middle, edges_joint, swept):
    lanes = own.shape[-1]
    z_ends(own, far, near, middle, joint, swept, count)

    def store(f, b, block):
        inner[f, pl.ds(b * lanes, lanes), :] = block

    cells = edges.shape[1] // (quarters * 2) - 2 * halo
    turns = (None for f in range(5) for _ in turn_out(swept, count, f, store))
    alternate(z_middle(edges, edges_middle, edges_joint, 2), cells, turns, 5 * count)


def last_kernel(ny, own, far, near, middle, joint, inner, density, momentum, energy, swept, whole, sent):
    lanes = own.shape[-1]
    nx = density.shape[0] // ny
    deep = lanes // nx
    strip = 2 * deep * 8
    outs = fields_of(density, momentum, energy)
    z_ends(own, far, near, middle, joint, swept, 2)

    def store(f, b, block):
        for half in range(lanes // strip):
            for k in range(2 * deep):
                y = k if k < deep else ny - 2 * deep + k
                at = half * strip + k * 8
                whole[f, pl.ds((b * (lanes // strip) + half) * 8 * ny + y, 8, stride=ny), :] = block[at : at + 8]

    copies = [pltpu.make_async_copy(whole.at[f], outs[f], sent.at[f]) for f in range(5)]
    for f in range(5):
        for b in range(nx // 8):
            for i in range(deep, ny - deep):
                whole[f, pl.ds(b * 8 * ny + i, 8, stride=ny), :] = inner[f, row(b * lanes + (i - deep) * 8), :]
        for _ in turn_out(swept, 2, f, store):
            pass
        copies[f].start()
    for copy in copies:
        copy.wait()


def call(kernel, shapes, scratch, arguments, in_specs=None, out_spec=None):
    whole = pl.BlockSpec(memory_space=pltpu.VMEM)
    return pl.pallas_call(
        kernel,
        out_shape=[jax.ShapeDtypeStruct(shape, jnp.float32) for shape in shapes],
        in_specs=[whole] * len(arguments) if in_specs is None else in_specs,
        out_specs=[whole if out_spec is None else out_spec] * len(shapes),
        scratch_shapes=[pltpu.VMEM(a, jnp.float32) if isinstance(a, tuple) else a for a in scratch],
        compiler_params=pltpu.CompilerParams(vmem_limit_bytes=24 * 2**20),
    )(*arguments)


def exchange(axis, far, near):
    ranks = lax.axis_size(axis)
    if ranks % 2:
        raise ValueError("odd ring")
    pairs = []
    for start in (1, 0):
        there = [(rank, (rank + 1) % ranks) for rank in range(start, ranks, 2)]
        pairs.append(there + [(b, a) for a, b in there])
    return lax.ppermute(far, axis, pairs[0]), lax.ppermute(near, axis, pairs[1])


def y_rows(density, momentum, energy):
    nx, ny, nz = density.shape
    shape = (5, halo, nx, nz)
    return pl.pallas_call(
        rows_kernel,
        out_shape=[pltpu.VMEM(shape, jnp.float32)] * 2,
        in_specs=[pl.BlockSpec(memory_space=pltpu.HBM)] * 3,
        out_specs=[pl.BlockSpec(memory_space=pltpu.VMEM)] * 2,
        scratch_shapes=[pltpu.VMEM((2, 5, nx, 8, nz), jnp.float32), pltpu.SemaphoreType.DMA((2, 5))],
        compiler_params=pltpu.CompilerParams(vmem_limit_bytes=16 * 2**20),
    )(*(pltpu.with_memory_space_constraint(a, pltpu.HBM) for a in (density, momentum, energy)))


def body(density, momentum, energy):
    nx, ny, nz = density.shape
    deep = nz // nx
    count = ny // deep - 2
    kept = deep + halo - 1
    end = (5, halo, 8, nz)

    far_rows, near_rows = exchange("gy", *y_rows(density, momentum, energy))
    turned, far, near, rim, beside, joint = call(
        inner_kernel,
        [(5, count * nz, nz), end, end, (5, 2 * kept, nx, nz), (5, 2 * (deep - halo), nx, nz), (5, 2, nx, nz)],
        [(5, nx * ny, nz)] + [(5, nz, nz)] * count,
        [density, momentum, energy],
    )
    far, near = exchange("gz", far, near)
    middle, faces = call(
        functools.partial(middle_kernel, count),
        [(5, count * nz, nz), (5, 2, quarters * count, nz)],
        [],
        [turned],
    )
    whole, anywhere = (pl.BlockSpec(memory_space=space) for space in (pltpu.VMEM, pl.ANY))
    edges, far_edges, near_edges = call(
        edge_kernel,
        [(5, 2 * nz, nz), end, end],
        [(5, 2 * halo, nx, nz)] + [(5, nz, nz)] * 2,
        [far_rows, near_rows, rim, beside, joint, faces],
        [whole] * 5 + [anywhere],
    )
    far_edges, near_edges = exchange("gz", far_edges, near_edges)
    inner, edges_middle, edges_faces = call(
        functools.partial(ends_kernel, count),
        [(5, count * nz, nz), (5, 2 * nz, nz), (5, 2, quarters * 2, nz)],
        [(5, count * nz, nz)],
        [turned, far, near, middle, faces, edges],
    )
    cells = nx * ny
    outs = call(
        functools.partial(last_kernel, ny),
        [(cells, nz), (3, cells, nz), (cells, nz)],
        [(5, 2 * nz, nz), (5, cells, nz), pltpu.SemaphoreType.DMA((5,))],
        [edges, far_edges, near_edges, edges_middle, edges_faces, inner],
        out_spec=anywhere,
    )
    return (outs[0].reshape(nx, ny, nz), outs[1].reshape(3, nx, ny, nz), outs[2].reshape(nx, ny, nz))


def solution(mesh):
    return jax.shard_map(
        body,
        mesh=mesh,
        in_specs=(P(None, "gy", "gz"), P(None, None, "gy", "gz"), P(None, "gy", "gz")),
        out_specs=(P(None, "gy", "gz"), P(None, None, "gy", "gz"), P(None, "gy", "gz")),
        check_vma=False,
    )
```

```python
import functools

import jax
import jax.numpy as jnp
from jax import lax
from jax.experimental import pallas as pl
from jax.experimental.pallas import tpu as pltpu
from jax.sharding import PartitionSpec as P

adiabatic = 1.4
courant = 0.15
halo = 3
quarters = 4


def primitives(fields):
    density, mx, my, mz, energy = fields
    inverse = pl.reciprocal(density, approx=True)
    vx, vy, vz = mx * inverse, my * inverse, mz * inverse
    doubled = mx * vx + my * vy + mz * vz
    pressure = (adiabatic - 1.0) * energy - (0.5 * (adiabatic - 1.0)) * doubled
    return [density, vx, vy, vz, pressure]


def signed(step):
    return step, jnp.maximum(step, 0.0), jnp.minimum(step, 0.0)


def half_slope(ahead, behind):
    top = jnp.minimum(ahead[1], behind[1])
    bottom = jnp.maximum(ahead[2], behind[2])
    return jnp.maximum(jnp.minimum(0.25 * (ahead[0] + behind[0]), top), bottom)


def face_offset(ahead, slope, slope_next):
    offset = 0.5 * ahead[0] - (1.0 / 3.0) * (slope_next - slope)
    return jnp.minimum(jnp.maximum(offset, ahead[2]), ahead[1])


def limited(first, second):
    doubled = second + second
    return jnp.maximum(jnp.minimum(first, jnp.maximum(doubled, 0.0)), jnp.minimum(doubled, 0.0))


def hll(left, right, normal):
    dl, pl_, ul = left[0], left[4], left[1 + normal]
    dr, pr, ur = right[0], right[4], right[1 + normal]
    tl = adiabatic * pl_
    tr = adiabatic * pr
    al = tl * lax.rsqrt(tl * dl)
    ar = tr * lax.rsqrt(tr * dr)
    slowest = jnp.minimum(jnp.minimum(ul - al, ur - ar), 0.0)
    fastest = jnp.maximum(jnp.maximum(ul + al, ur + ar), 0.0)
    cl = fastest * (courant * pl.reciprocal(fastest - slowest, approx=True))
    cr = courant - cl
    wl = cl * (ul - slowest)
    wr = cr * (ur - fastest)
    ml = wl * dl
    mr = wr * dr
    ql = cl * pl_
    qr = cr * pr
    gl = [ml * left[1 + k] for k in range(3)]
    gr = [mr * right[1 + k] for k in range(3)]
    kinetic = (
        gl[0] * left[1] + gl[1] * left[2] + gl[2] * left[3]
        + gr[0] * right[1] + gr[1] * right[2] + gr[2] * right[3]
    )
    flux = [ml + mr] + [gl[k] + gr[k] for k in range(3)]
    flux[1 + normal] = flux[1 + normal] + (ql + qr)
    inner = (1.0 / (adiabatic - 1.0)) * (wl * pl_ + wr * pr)
    flux.append(0.5 * kinetic + inner + (ql * ul + qr * ur))
    return flux


class Line:
    def __init__(self, load, normal, period=None):
        self.load, self.normal, self.period = load, normal, period
        self.known = {}

    def once(self, name, index, make):
        if self.period is not None:
            index = index % self.period
        if (name, index) not in self.known:
            self.known[(name, index)] = make(index)
        return self.known[(name, index)]

    def prims(self, i):
        return self.once("q", i, lambda i: primitives(self.load(i)))

    def diff(self, i):
        return self.once("d", i, lambda i: [signed(b - a) for a, b in zip(self.prims(i), self.prims(i + 1))])

    def slope(self, i):
        return self.once("s", i, lambda i: [half_slope(a, b) for a, b in zip(self.diff(i), self.diff(i - 1))])

    def up(self, i):
        return self.once("u", i, lambda i: [face_offset(d, s, t) for d, s, t in zip(self.diff(i), self.slope(i), self.slope(i + 1))])

    def down(self, i):
        return self.once("w", i, lambda i: [d[0] - u for d, u in zip(self.diff(i - 1), self.up(i - 1))])

    def low(self, i):
        return self.once("l", i, lambda i: [q - limited(w, u) for q, w, u in zip(self.prims(i), self.down(i), self.up(i))])

    def high(self, i):
        return self.once("h", i, lambda i: [q + limited(u, w) for q, w, u in zip(self.prims(i), self.down(i), self.up(i))])

    def flux(self, i):
        return self.once("f", i, lambda i: hll(self.high(i), self.low(i + 1), self.normal))

    def swept(self, i):
        before, after = self.flux(i - 1), self.flux(i)
        return [u - (b - a) for u, a, b in zip(self.load(i), before, after)]


def rolled(fields, ahead, behind, normal):
    states = primitives(fields)
    low, high = [], []
    for q in states:
        d = ahead(q) - q
        s = half_slope(signed(d), signed(behind(d)))
        u = face_offset(signed(d), s, ahead(s))
        w = behind(d - u)
        low.append(ahead(q - limited(w, u)))
        high.append(q + limited(u, w))
    return hll(high, low, normal)


def shifts(axis, size):
    return (lambda a: pltpu.roll(a, size - 1, axis), lambda a: pltpu.roll(a, 1, axis))


def row(index):
    return pl.ds(index, 8)


def fields_of(density, momentum, energy):
    return [density, momentum.at[0], momentum.at[1], momentum.at[2], energy]


def odd_rank(axis):
    return lax.axis_index(axis) % 2 == 1


class Received:
    def __init__(self, odd, on_odd, on_even):
        self.odd, self.on_odd, self.on_even = odd, on_odd, on_even

    def __getitem__(self, index):
        return jnp.where(self.odd, self.on_odd[index], self.on_even[index])


def sides_of(axis, far, near):
    odd = odd_rank(axis)
    return Received(odd, near, far), Received(odd, far, near)


def rows_kernel(density, momentum, energy, far, near, held, arrived):
    sources = fields_of(density, momentum, energy)
    nx, ny, nz = density.shape
    copies = []
    for f in range(5):
        for side in range(2):
            tile = sources[f].at[:, pl.ds(side * (ny - 8), 8), :]
            copies.append(pltpu.make_async_copy(tile, held.at[side, f], arrived.at[side, f]))
    for copy in copies:
        copy.start()
    odd = odd_rank("gy")
    for f in range(5):
        copies[2 * f].wait()
        copies[2 * f + 1].wait()
        top, bottom = (held.at[side, f].reshape(nx * 8, nz) for side in range(2))
        for r in range(halo):
            first = top[pl.ds(r, nx, stride=8), :]
            last = bottom[pl.ds(8 - halo + r, nx, stride=8), :]
            far[f, r] = jnp.where(odd, last, first)
            near[f, r] = jnp.where(odd, first, last)


def alternate(steps, parts, others, other_parts):
    made = 0
    for part, _ in enumerate(steps):
        while made * parts < (part + 1) * other_parts:
            next(others, None)
            made += 1
    for _ in others:
        pass


def turn_in(source, turned, count, b):
    lanes = source.shape[-1]
    span = lanes // quarters
    for f in range(5):
        block = source[f].T
        for q in range(quarters):
            turned[f, pl.ds(q * count + b, span, stride=quarters * count), :] = block[q * span : (q + 1) * span]
        yield


def turn_out(turned, count, f, store):
    lanes = turned.shape[-1]
    span = lanes // quarters
    for b in range(count):
        parts = [turned[f, pl.ds(q * count + b, span, stride=quarters * count), :] for q in range(quarters)]
        store(f, b, jnp.concatenate(parts, axis=0).T)
        yield


def ends(turned, count, far, near):
    width = quarters * count
    span = turned.shape[1] // width
    odd = odd_rank("gz")
    for f in range(5):
        for k in range(halo):
            upward = turned[f, pl.ds((span - halo + k + 1) * width - count, count), :]
            downward = turned[f, pl.ds(k * width, count), :]
            at = pl.ds((f * halo + k) * count, count)
            far[at, :] = jnp.where(odd, upward, downward)
            near[at, :] = jnp.where(odd, downward, upward)


def placed(ends, f, k, count, at):
    first = (f * halo + k) * count
    start = min(max(first - at, 0), 5 * halo * count - 8)
    window = ends[row(start), :]
    shift = (at + start - first) % 8
    return pltpu.roll(window, shift, 0) if shift else window


def z_lines(own, count, left=None, right=None):
    width = quarters * count
    span = own.shape[1] // width
    place = lax.broadcasted_iota(jnp.int32, (8, own.shape[-1]), 0)
    for start in range(0, width, 8):

        def load(i, start=start):
            if 0 <= i < span:
                return [own[f, row(i * width + start), :] for f in range(5)]
            if i < 0:
                fields = [own[f, row((i + span) * width + start - count), :] for f in range(5)]
                if start == 0:
                    fields = [jnp.where(place < count, placed(left, f, i + halo, count, 0), a) for f, a in enumerate(fields)]
                return fields
            fields = [own[f, row((i - span) * width + start + count), :] for f in range(5)]
            if start + 8 == width:
                fields = [jnp.where(place >= 8 - count, placed(right, f, i - span, count, 8 - count), a) for f, a in enumerate(fields)]
            return fields

        yield start, span, Line(load, 2)


def z_middle(own, swept, joint, count):
    for start, span, line in z_lines(own, count):
        for i in range(halo, span - halo):
            for f, value in enumerate(line.swept(i)):
                swept[f, row(i * quarters * count + start), :] = value
            yield
        for end, face in enumerate((halo - 1, span - halo - 1)):
            for f, value in enumerate(line.flux(face)):
                joint[f, end, row(start), :] = value


def z_ends(own, far, near, middle, joint, swept, count):
    for start, span, line in z_lines(own, count, *sides_of("gz", far, near)):
        for end, face in enumerate((halo - 1, span - halo - 1)):
            line.known[("f", face)] = [joint[f, end, row(start), :] for f in range(5)]
        for i in range(span):
            at = row(i * quarters * count + start)
            inside = halo <= i < span - halo
            values = [middle[f, at, :] for f in range(5)] if inside else line.swept(i)
            for f, value in enumerate(values):
                swept[f, at, :] = value


def inner_kernel(density, momentum, energy, turned, far, near, rim, beside, joint, held, *strips):
    nx, ny, lanes = density.shape
    deep = lanes // nx
    sources = fields_of(density, momentum, energy)

    @pl.loop(0, ny // 8)
    def _(tile):
        start = pl.multiple_of(tile * 8, 8)
        line = Line(lambda i: [s[i, pl.ds(start, 8), :] for s in sources], 0, nx)
        for i in range(nx):
            for f, value in enumerate(line.swept(i)):
                held[f, pl.ds(pl.multiple_of(i * ny + start, 8), 8), :] = value

    def sweep(tile):
        some = row(tile * 8)
        line = Line(lambda i: [held[f, pl.ds(tile * (8 * ny) + i, 8, stride=ny), :] for f in range(5)], 1)
        for i in range(halo, ny - halo):
            for f, value in enumerate(line.swept(i)):
                if deep <= i < ny - deep:
                    strips[tile][f, row((i - deep) * 8), :] = value
                else:
                    beside[f, i - halo if i < deep else i - ny + 2 * deep - halo, some, :] = value
            yield
        for f in range(5):
            joint[f, 0, some, :] = line.flux(halo - 1)[f]
            joint[f, 1, some, :] = line.flux(ny - halo - 1)[f]
        kept = deep + halo - 1
        for r in range(kept):
            for f, (a, b) in enumerate(zip(line.load(r), line.load(ny - kept + r))):
                rim[f, r, some, :] = a
                rim[f, kept + r, some, :] = b

    count = len(strips)
    turns = iter(())
    for tile in range(count):
        alternate(sweep(tile), ny - 2 * halo, turns, 5)
        turns = turn_in(strips[tile], turned, count, tile)
    for _ in turns:
        pass
    ends(turned, count, far, near)


def edge_kernel(far, near, rim, beside, joint, _, turned, far_end, near_end, ghost, *outers):
    _, kept, nx, lanes = rim.shape
    kept = kept // 2
    deep = lanes // nx
    ahead, behind = shifts(0, nx)
    for side, source in enumerate(sides_of("gy", far, near)):

        @pl.loop(0, halo)
        def _(r):
            fields = [source[f, r] for f in range(5)]
            flux = rolled(fields, ahead, behind, 0)
            for f in range(5):
                ghost[f, side * halo + r] = fields[f] - (flux[f] - behind(flux[f]))

    share = nx // 8 // len(outers)

    def sweep(block):
        for half in range(share):
            some = row((block * share + half) * 8)
            for side in range(2):

                def load(i, side=side, some=some):
                    if side == 0:
                        source, at = (ghost, i + halo) if i < 0 else (rim, i)
                    else:
                        source, at = (ghost, i - deep + halo) if i >= deep else (rim, i + kept + kept - deep)
                    return [source[f, at, some, :] for f in range(5)]

                line = Line(load, 1)
                known = halo - 1 if side == 0 else deep - halo - 1
                line.known[("f", known)] = [joint[f, side, some, :] for f in range(5)]
                for i in range(deep):
                    if side == 0 and i >= halo:
                        values = [beside[f, i - halo, some, :] for f in range(5)]
                    elif side == 1 and i < deep - halo:
                        values = [beside[f, i + deep - halo, some, :] for f in range(5)]
                    else:
                        values = line.swept(i)
                    for f, value in enumerate(values):
                        outers[block][f, row(((half * 2 + side) * deep + i) * 8), :] = value
                    yield

    turns = iter(())
    for block, outer in enumerate(outers):
        alternate(sweep(block), share * 2 * deep, turns, 5)
        turns = turn_in(outer, turned, len(outers), block)
    for _ in turns:
        pass
    ends(turned, 2, far_end, near_end)


def middle_kernel(count, own, swept, joint):
    for _ in z_middle(own, swept, joint, count):
        pass


def ends_kernel(count, own, far, near, middle, joint, edges, inner, edges_middle, edges_joint, swept):
    lanes = own.shape[-1]
    z_ends(own, far, near, middle, joint, swept, count)

    def store(f, b, block):
        inner[f, pl.ds(b * lanes, lanes), :] = block

    cells = edges.shape[1] // (quarters * 2) - 2 * halo
    turns = (None for f in range(5) for _ in turn_out(swept, count, f, store))
    alternate(z_middle(edges, edges_middle, edges_joint, 2), cells, turns, 5 * count)


def last_kernel(ny, own, far, near, middle, joint, inner, density, momentum, energy, swept, whole, sent):
    lanes = own.shape[-1]
    nx = density.shape[0] // ny
    deep = lanes // nx
    strip = 2 * deep * 8
    outs = fields_of(density, momentum, energy)
    z_ends(own, far, near, middle, joint, swept, 2)

    def store(f, b, block):
        for half in range(lanes // strip):
            for k in range(2 * deep):
                y = k if k < deep else ny - 2 * deep + k
                at = half * strip + k * 8
                whole[f, pl.ds((b * (lanes // strip) + half) * 8 * ny + y, 8, stride=ny), :] = block[at : at + 8]

    copies = [pltpu.make_async_copy(whole.at[f], outs[f], sent.at[f]) for f in range(5)]
    for f in range(5):
        for b in range(nx // 8):
            for i in range(deep, ny - deep):
                whole[f, pl.ds(b * 8 * ny + i, 8, stride=ny), :] = inner[f, row(b * lanes + (i - deep) * 8), :]
        for _ in turn_out(swept, 2, f, store):
            pass
        copies[f].start()
    for copy in copies:
        copy.wait()


def call(kernel, shapes, scratch, arguments, in_specs=None, out_spec=None):
    whole = pl.BlockSpec(memory_space=pltpu.VMEM)
    return pl.pallas_call(
        kernel,
        out_shape=[jax.ShapeDtypeStruct(shape, jnp.float32) for shape in shapes],
        in_specs=[whole] * len(arguments) if in_specs is None else in_specs,
        out_specs=[whole if out_spec is None else out_spec] * len(shapes),
        scratch_shapes=[pltpu.VMEM(a, jnp.float32) if isinstance(a, tuple) else a for a in scratch],
        compiler_params=pltpu.CompilerParams(vmem_limit_bytes=24 * 2**20),
    )(*arguments)


def exchange(axis, far, near):
    ranks = lax.axis_size(axis)
    if ranks % 2:
        raise ValueError("odd ring")
    pairs = []
    for start in (1, 0):
        there = [(rank, (rank + 1) % ranks) for rank in range(start, ranks, 2)]
        pairs.append(there + [(b, a) for a, b in there])
    return lax.ppermute(far, axis, pairs[0]), lax.ppermute(near, axis, pairs[1])


def y_rows(density, momentum, energy):
    nx, ny, nz = density.shape
    shape = (5, halo, nx, nz)
    return pl.pallas_call(
        rows_kernel,
        out_shape=[pltpu.VMEM(shape, jnp.float32)] * 2,
        in_specs=[pl.BlockSpec(memory_space=pltpu.HBM)] * 3,
        out_specs=[pl.BlockSpec(memory_space=pltpu.VMEM)] * 2,
        scratch_shapes=[pltpu.VMEM((2, 5, nx, 8, nz), jnp.float32), pltpu.SemaphoreType.DMA((2, 5))],
        compiler_params=pltpu.CompilerParams(vmem_limit_bytes=16 * 2**20),
    )(*(pltpu.with_memory_space_constraint(a, pltpu.HBM) for a in (density, momentum, energy)))


def body(density, momentum, energy):
    nx, ny, nz = density.shape
    deep = nz // nx
    count = ny // deep - 2
    kept = deep + halo - 1

    far_rows, near_rows = exchange("gy", *y_rows(density, momentum, energy))
    turned, far, near, rim, beside, joint = call(
        inner_kernel,
        [(5, count * nz, nz)] + [(5 * halo * count, nz)] * 2 + [(5, 2 * kept, nx, nz), (5, 2 * (deep - halo), nx, nz), (5, 2, nx, nz)],
        [(5, nx * ny, nz)] + [(5, nz, nz)] * count,
        [density, momentum, energy],
    )
    far, near = exchange("gz", far, near)
    middle, faces = call(
        functools.partial(middle_kernel, count),
        [(5, count * nz, nz), (5, 2, quarters * count, nz)],
        [],
        [turned],
    )
    whole, anywhere = (pl.BlockSpec(memory_space=space) for space in (pltpu.VMEM, pl.ANY))
    edges, far_edges, near_edges = call(
        edge_kernel,
        [(5, 2 * nz, nz)] + [(5 * halo * 2, nz)] * 2,
        [(5, 2 * halo, nx, nz)] + [(5, nz, nz)] * 2,
        [far_rows, near_rows, rim, beside, joint, faces],
        [whole] * 5 + [anywhere],
    )
    far_edges, near_edges = exchange("gz", far_edges, near_edges)
    inner, edges_middle, edges_faces = call(
        functools.partial(ends_kernel, count),
        [(5, count * nz, nz), (5, 2 * nz, nz), (5, 2, quarters * 2, nz)],
        [(5, count * nz, nz)],
        [turned, far, near, middle, faces, edges],
    )
    cells = nx * ny
    outs = call(
        functools.partial(last_kernel, ny),
        [(cells, nz), (3, cells, nz), (cells, nz)],
        [(5, 2 * nz, nz), (5, cells, nz), pltpu.SemaphoreType.DMA((5,))],
        [edges, far_edges, near_edges, edges_middle, edges_faces, inner],
        out_spec=anywhere,
    )
    return (outs[0].reshape(nx, ny, nz), outs[1].reshape(3, nx, ny, nz), outs[2].reshape(nx, ny, nz))


def solution(mesh):
    return jax.shard_map(
        body,
        mesh=mesh,
        in_specs=(P(None, "gy", "gz"), P(None, None, "gy", "gz"), P(None, "gy", "gz")),
        out_specs=(P(None, "gy", "gz"), P(None, None, "gy", "gz"), P(None, "gy", "gz")),
        check_vma=False,
    )
```

```python
import functools

import jax
import jax.numpy as jnp
from jax import lax
from jax.experimental import pallas as pl
from jax.experimental.pallas import tpu as pltpu
from jax.sharding import PartitionSpec as P

adiabatic = 1.4
courant = 0.15
halo = 3
quarters = 4


def primitives(fields):
    density, mx, my, mz, energy = fields
    inverse = pl.reciprocal(density, approx=True)
    vx, vy, vz = mx * inverse, my * inverse, mz * inverse
    doubled = mx * vx + my * vy + mz * vz
    pressure = (adiabatic - 1.0) * energy - (0.5 * (adiabatic - 1.0)) * doubled
    return [density, vx, vy, vz, pressure]


def signed(step):
    return step, jnp.maximum(step, 0.0), jnp.minimum(step, 0.0)


def half_slope(ahead, behind):
    top = jnp.minimum(ahead[1], behind[1])
    bottom = jnp.maximum(ahead[2], behind[2])
    return jnp.maximum(jnp.minimum(0.25 * (ahead[0] + behind[0]), top), bottom)


def face_offset(ahead, slope, slope_next):
    offset = 0.5 * ahead[0] - (1.0 / 3.0) * (slope_next - slope)
    return jnp.minimum(jnp.maximum(offset, ahead[2]), ahead[1])


def limited(first, second):
    doubled = second + second
    return jnp.maximum(jnp.minimum(first, jnp.maximum(doubled, 0.0)), jnp.minimum(doubled, 0.0))


def hll(left, right, normal):
    dl, pl_, ul = left[0], left[4], left[1 + normal]
    dr, pr, ur = right[0], right[4], right[1 + normal]
    tl = adiabatic * pl_
    tr = adiabatic * pr
    al = tl * lax.rsqrt(tl * dl)
    ar = tr * lax.rsqrt(tr * dr)
    slowest = jnp.minimum(jnp.minimum(ul - al, ur - ar), 0.0)
    fastest = jnp.maximum(jnp.maximum(ul + al, ur + ar), 0.0)
    cl = fastest * (courant * pl.reciprocal(fastest - slowest, approx=True))
    cr = courant - cl
    wl = cl * (ul - slowest)
    wr = cr * (ur - fastest)
    ml = wl * dl
    mr = wr * dr
    ql = cl * pl_
    qr = cr * pr
    gl = [ml * left[1 + k] for k in range(3)]
    gr = [mr * right[1 + k] for k in range(3)]
    kinetic = (
        gl[0] * left[1] + gl[1] * left[2] + gl[2] * left[3]
        + gr[0] * right[1] + gr[1] * right[2] + gr[2] * right[3]
    )
    flux = [ml + mr] + [gl[k] + gr[k] for k in range(3)]
    flux[1 + normal] = flux[1 + normal] + (ql + qr)
    inner = (1.0 / (adiabatic - 1.0)) * (wl * pl_ + wr * pr)
    flux.append(0.5 * kinetic + inner + (ql * ul + qr * ur))
    return flux


class Line:
    def __init__(self, load, normal, period=None):
        self.load, self.normal, self.period = load, normal, period
        self.known = {}

    def once(self, name, index, make):
        if self.period is not None:
            index = index % self.period
        if (name, index) not in self.known:
            self.known[(name, index)] = make(index)
        return self.known[(name, index)]

    def prims(self, i):
        return self.once("q", i, lambda i: primitives(self.load(i)))

    def diff(self, i):
        return self.once("d", i, lambda i: [signed(b - a) for a, b in zip(self.prims(i), self.prims(i + 1))])

    def slope(self, i):
        return self.once("s", i, lambda i: [half_slope(a, b) for a, b in zip(self.diff(i), self.diff(i - 1))])

    def up(self, i):
        return self.once("u", i, lambda i: [face_offset(d, s, t) for d, s, t in zip(self.diff(i), self.slope(i), self.slope(i + 1))])

    def down(self, i):
        return self.once("w", i, lambda i: [d[0] - u for d, u in zip(self.diff(i - 1), self.up(i - 1))])

    def low(self, i):
        return self.once("l", i, lambda i: [q - limited(w, u) for q, w, u in zip(self.prims(i), self.down(i), self.up(i))])

    def high(self, i):
        return self.once("h", i, lambda i: [q + limited(u, w) for q, w, u in zip(self.prims(i), self.down(i), self.up(i))])

    def flux(self, i):
        return self.once("f", i, lambda i: hll(self.high(i), self.low(i + 1), self.normal))

    def swept(self, i):
        before, after = self.flux(i - 1), self.flux(i)
        return [u - (b - a) for u, a, b in zip(self.load(i), before, after)]


def rolled(fields, ahead, behind, normal):
    states = primitives(fields)
    low, high = [], []
    for q in states:
        d = ahead(q) - q
        s = half_slope(signed(d), signed(behind(d)))
        u = face_offset(signed(d), s, ahead(s))
        w = behind(d - u)
        low.append(ahead(q - limited(w, u)))
        high.append(q + limited(u, w))
    return hll(high, low, normal)


def shifts(axis, size):
    return (lambda a: pltpu.roll(a, size - 1, axis), lambda a: pltpu.roll(a, 1, axis))


def row(index):
    return pl.ds(index, 8)


def fields_of(density, momentum, energy):
    return [density, momentum.at[0], momentum.at[1], momentum.at[2], energy]


def odd_rank(axis):
    return lax.axis_index(axis) % 2 == 1


class Received:
    def __init__(self, odd, on_odd, on_even):
        self.odd, self.on_odd, self.on_even = odd, on_odd, on_even

    def __getitem__(self, index):
        return jnp.where(self.odd, self.on_odd[index], self.on_even[index])


def sides_of(axis, far, near):
    odd = odd_rank(axis)
    return Received(odd, near, far), Received(odd, far, near)


def rows_kernel(density, momentum, energy, far, near, held, arrived):
    sources = fields_of(density, momentum, energy)
    nx, ny, nz = density.shape
    copies = []
    for f in range(5):
        for side in range(2):
            tile = sources[f].at[:, pl.ds(side * (ny - 8), 8), :]
            copies.append(pltpu.make_async_copy(tile, held.at[side, f], arrived.at[side, f]))
    for copy in copies:
        copy.start()
    odd = odd_rank("gy")
    for f in range(5):
        copies[2 * f].wait()
        copies[2 * f + 1].wait()
        top, bottom = (held.at[side, f].reshape(nx * 8, nz) for side in range(2))
        for r in range(halo):
            first = top[pl.ds(r, nx, stride=8), :]
            last = bottom[pl.ds(8 - halo + r, nx, stride=8), :]
            far[f, r] = jnp.where(odd, last, first)
            near[f, r] = jnp.where(odd, first, last)


def alternate(steps, parts, others, other_parts):
    made = 0
    for part, _ in enumerate(steps):
        while made * parts < (part + 1) * other_parts:
            next(others, None)
            made += 1
    for _ in others:
        pass


def turn_in(source, turned, count, b):
    lanes = source.shape[-1]
    span = lanes // quarters
    for f in range(5):
        block = source[f].T
        for q in range(quarters):
            turned[f, pl.ds(q * count + b, span, stride=quarters * count), :] = block[q * span : (q + 1) * span]
        yield


def turn_out(turned, count, f, store):
    lanes = turned.shape[-1]
    span = lanes // quarters
    for b in range(count):
        parts = [turned[f, pl.ds(q * count + b, span, stride=quarters * count), :] for q in range(quarters)]
        store(f, b, jnp.concatenate(parts, axis=0).T)
        yield


def ends(turned, count, far, near):
    width = quarters * count
    span = turned.shape[1] // width
    odd = odd_rank("gz")
    for f in range(5):
        for k in range(halo):
            upward = turned[f, pl.ds((span - halo + k + 1) * width - count, count), :]
            downward = turned[f, pl.ds(k * width, count), :]
            at = pl.ds((f * halo + k) * count, count)
            far[at, :] = jnp.where(odd, upward, downward)
            near[at, :] = jnp.where(odd, downward, upward)


def placed(ends, f, k, count, at):
    first = (f * halo + k) * count
    start = min(max(first - at, 0), 5 * halo * count - 8)
    window = ends[row(start), :]
    shift = (at + start - first) % 8
    return pltpu.roll(window, shift, 0) if shift else window


def z_lines(own, count, left=None, right=None):
    width = quarters * count
    span = own.shape[1] // width
    place = lax.broadcasted_iota(jnp.int32, (8, own.shape[-1]), 0)
    for start in range(0, width, 8):

        def load(i, start=start):
            if 0 <= i < span:
                return [own[f, row(i * width + start), :] for f in range(5)]
            if i < 0:
                fields = [own[f, row((i + span) * width + start - count), :] for f in range(5)]
                if start == 0:
                    fields = [jnp.where(place < count, placed(left, f, i + halo, count, 0), a) for f, a in enumerate(fields)]
                return fields
            fields = [own[f, row((i - span) * width + start + count), :] for f in range(5)]
            if start + 8 == width:
                fields = [jnp.where(place >= 8 - count, placed(right, f, i - span, count, 8 - count), a) for f, a in enumerate(fields)]
            return fields

        yield start, span, Line(load, 2)


def z_middle(own, swept, joint, count):
    for start, span, line in z_lines(own, count):
        for i in range(halo, span - halo):
            for f, value in enumerate(line.swept(i)):
                swept[f, row(i * quarters * count + start), :] = value
            yield
        for end, face in enumerate((halo - 1, span - halo - 1)):
            for f, value in enumerate(line.flux(face)):
                joint[f, end, row(start), :] = value


def z_ends(own, far, near, middle, joint, swept, count):
    for start, span, line in z_lines(own, count, *sides_of("gz", far, near)):
        for end, face in enumerate((halo - 1, span - halo - 1)):
            line.known[("f", face)] = [joint[f, end, row(start), :] for f in range(5)]
        for i in range(span):
            at = row(i * quarters * count + start)
            inside = halo <= i < span - halo
            values = [middle[f, at, :] for f in range(5)] if inside else line.swept(i)
            for f, value in enumerate(values):
                swept[f, at, :] = value


def inner_kernel(density, momentum, energy, turned, far, near, rim, beside, joint, held, *strips):
    nx, ny, lanes = density.shape
    deep = lanes // nx
    sources = fields_of(density, momentum, energy)

    @pl.loop(0, ny // 8)
    def _(tile):
        start = pl.multiple_of(tile * 8, 8)
        line = Line(lambda i: [s[i, pl.ds(start, 8), :] for s in sources], 0, nx)
        for i in range(nx):
            for f, value in enumerate(line.swept(i)):
                held[f, pl.ds(pl.multiple_of(i * ny + start, 8), 8), :] = value

    def sweep(tile):
        some = row(tile * 8)
        line = Line(lambda i: [held[f, pl.ds(tile * (8 * ny) + i, 8, stride=ny), :] for f in range(5)], 1)
        for i in range(halo, ny - halo):
            for f, value in enumerate(line.swept(i)):
                if deep <= i < ny - deep:
                    strips[tile][f, row((i - deep) * 8), :] = value
                else:
                    beside[f, i - halo if i < deep else i - ny + 2 * deep - halo, some, :] = value
            yield
        for f in range(5):
            joint[f, 0, some, :] = line.flux(halo - 1)[f]
            joint[f, 1, some, :] = line.flux(ny - halo - 1)[f]
        kept = deep + halo - 1
        for r in range(kept):
            for f, (a, b) in enumerate(zip(line.load(r), line.load(ny - kept + r))):
                rim[f, r, some, :] = a
                rim[f, kept + r, some, :] = b

    count = len(strips)
    turns = iter(())
    for tile in range(count):
        alternate(sweep(tile), ny - 2 * halo, turns, 5)
        turns = turn_in(strips[tile], turned, count, tile)
    for _ in turns:
        pass
    ends(turned, count, far, near)


def edge_kernel(far, near, rim, beside, joint, _, turned, far_end, near_end, ghost, *outers):
    _, kept, nx, lanes = rim.shape
    kept = kept // 2
    deep = lanes // nx
    ahead, behind = shifts(0, nx)
    for side, source in enumerate(sides_of("gy", far, near)):
        for r in range(halo):
            fields = [source[f, r] for f in range(5)]
            flux = rolled(fields, ahead, behind, 0)
            for f in range(5):
                ghost[f, side * halo + r] = fields[f] - (flux[f] - behind(flux[f]))

    share = nx // 8 // len(outers)

    def sweep(block):
        for half in range(share):
            some = row((block * share + half) * 8)
            for side in range(2):

                def load(i, side=side, some=some):
                    if side == 0:
                        source, at = (ghost, i + halo) if i < 0 else (rim, i)
                    else:
                        source, at = (ghost, i - deep + halo) if i >= deep else (rim, i + kept + kept - deep)
                    return [source[f, at, some, :] for f in range(5)]

                line = Line(load, 1)
                known = halo - 1 if side == 0 else deep - halo - 1
                line.known[("f", known)] = [joint[f, side, some, :] for f in range(5)]
                for i in range(deep):
                    if side == 0 and i >= halo:
                        values = [beside[f, i - halo, some, :] for f in range(5)]
                    elif side == 1 and i < deep - halo:
                        values = [beside[f, i + deep - halo, some, :] for f in range(5)]
                    else:
                        values = line.swept(i)
                    for f, value in enumerate(values):
                        outers[block][f, row(((half * 2 + side) * deep + i) * 8), :] = value
                    yield

    turns = iter(())
    for block, outer in enumerate(outers):
        alternate(sweep(block), share * 2 * deep, turns, 5)
        turns = turn_in(outer, turned, len(outers), block)
    for _ in turns:
        pass
    ends(turned, 2, far_end, near_end)


def middle_kernel(count, own, swept, joint):
    for _ in z_middle(own, swept, joint, count):
        pass


def ends_kernel(count, own, far, near, middle, joint, edges, inner, edges_middle, edges_joint, swept):
    lanes = own.shape[-1]
    z_ends(own, far, near, middle, joint, swept, count)

    def store(f, b, block):
        inner[f, pl.ds(b * lanes, lanes), :] = block

    cells = edges.shape[1] // (quarters * 2) - 2 * halo
    turns = (None for f in range(5) for _ in turn_out(swept, count, f, store))
    alternate(z_middle(edges, edges_middle, edges_joint, 2), cells, turns, 5 * count)


def last_kernel(ny, own, far, near, middle, joint, inner, density, momentum, energy, swept, whole, sent):
    lanes = own.shape[-1]
    nx = density.shape[0] // ny
    deep = lanes // nx
    strip = 2 * deep * 8
    outs = fields_of(density, momentum, energy)
    z_ends(own, far, near, middle, joint, swept, 2)

    def store(f, b, block):
        for half in range(lanes // strip):
            for k in range(2 * deep):
                y = k if k < deep else ny - 2 * deep + k
                at = half * strip + k * 8
                whole[f, pl.ds((b * (lanes // strip) + half) * 8 * ny + y, 8, stride=ny), :] = block[at : at + 8]

    copies = [pltpu.make_async_copy(whole.at[f], outs[f], sent.at[f]) for f in range(5)]
    for f in range(5):
        for b in range(nx // 8):
            for i in range(deep, ny - deep):
                whole[f, pl.ds(b * 8 * ny + i, 8, stride=ny), :] = inner[f, row(b * lanes + (i - deep) * 8), :]
        for _ in turn_out(swept, 2, f, store):
            pass
        copies[f].start()
    for copy in copies:
        copy.wait()


def call(kernel, shapes, scratch, arguments, in_specs=None, out_spec=None):
    whole = pl.BlockSpec(memory_space=pltpu.VMEM)
    return pl.pallas_call(
        kernel,
        out_shape=[jax.ShapeDtypeStruct(shape, jnp.float32) for shape in shapes],
        in_specs=[whole] * len(arguments) if in_specs is None else in_specs,
        out_specs=[whole if out_spec is None else out_spec] * len(shapes),
        scratch_shapes=[pltpu.VMEM(a, jnp.float32) if isinstance(a, tuple) else a for a in scratch],
        compiler_params=pltpu.CompilerParams(vmem_limit_bytes=24 * 2**20),
    )(*arguments)


def exchange(axis, far, near):
    ranks = lax.axis_size(axis)
    if ranks % 2:
        raise ValueError("odd ring")
    pairs = []
    for start in (1, 0):
        there = [(rank, (rank + 1) % ranks) for rank in range(start, ranks, 2)]
        pairs.append(there + [(b, a) for a, b in there])
    return lax.ppermute(far, axis, pairs[0]), lax.ppermute(near, axis, pairs[1])


def y_rows(density, momentum, energy):
    nx, ny, nz = density.shape
    shape = (5, halo, nx, nz)
    return pl.pallas_call(
        rows_kernel,
        out_shape=[pltpu.VMEM(shape, jnp.float32)] * 2,
        in_specs=[pl.BlockSpec(memory_space=pltpu.HBM)] * 3,
        out_specs=[pl.BlockSpec(memory_space=pltpu.VMEM)] * 2,
        scratch_shapes=[pltpu.VMEM((2, 5, nx, 8, nz), jnp.float32), pltpu.SemaphoreType.DMA((2, 5))],
        compiler_params=pltpu.CompilerParams(vmem_limit_bytes=16 * 2**20),
    )(*(pltpu.with_memory_space_constraint(a, pltpu.HBM) for a in (density, momentum, energy)))


def body(density, momentum, energy):
    nx, ny, nz = density.shape
    deep = nz // nx
    count = ny // deep - 2
    kept = deep + halo - 1

    far_rows, near_rows = exchange("gy", *y_rows(density, momentum, energy))
    turned, far, near, rim, beside, joint = call(
        inner_kernel,
        [(5, count * nz, nz)] + [(5 * halo * count, nz)] * 2 + [(5, 2 * kept, nx, nz), (5, 2 * (deep - halo), nx, nz), (5, 2, nx, nz)],
        [(5, nx * ny, nz)] + [(5, nz, nz)] * count,
        [density, momentum, energy],
    )
    far, near = exchange("gz", far, near)
    middle, faces = call(
        functools.partial(middle_kernel, count),
        [(5, count * nz, nz), (5, 2, quarters * count, nz)],
        [],
        [turned],
    )
    whole, anywhere = (pl.BlockSpec(memory_space=space) for space in (pltpu.VMEM, pl.ANY))
    edges, far_edges, near_edges = call(
        edge_kernel,
        [(5, 2 * nz, nz)] + [(5 * halo * 2, nz)] * 2,
        [(5, 2 * halo, nx, nz)] + [(5, nz, nz)] * 2,
        [far_rows, near_rows, rim, beside, joint, faces],
        [whole] * 5 + [anywhere],
    )
    far_edges, near_edges = exchange("gz", far_edges, near_edges)
    inner, edges_middle, edges_faces = call(
        functools.partial(ends_kernel, count),
        [(5, count * nz, nz), (5, 2 * nz, nz), (5, 2, quarters * 2, nz)],
        [(5, count * nz, nz)],
        [turned, far, near, middle, faces, edges],
    )
    cells = nx * ny
    outs = call(
        functools.partial(last_kernel, ny),
        [(cells, nz), (3, cells, nz), (cells, nz)],
        [(5, 2 * nz, nz), (5, cells, nz), pltpu.SemaphoreType.DMA((5,))],
        [edges, far_edges, near_edges, edges_middle, edges_faces, inner],
        out_spec=anywhere,
    )
    return (outs[0].reshape(nx, ny, nz), outs[1].reshape(3, nx, ny, nz), outs[2].reshape(nx, ny, nz))


def solution(mesh):
    return jax.shard_map(
        body,
        mesh=mesh,
        in_specs=(P(None, "gy", "gz"), P(None, None, "gy", "gz"), P(None, "gy", "gz")),
        out_specs=(P(None, "gy", "gz"), P(None, None, "gy", "gz"), P(None, "gy", "gz")),
        check_vma=False,
    )
```

```python
import functools

import jax
import jax.numpy as jnp
from jax import lax
from jax.experimental import pallas as pl
from jax.experimental.pallas import tpu as pltpu
from jax.sharding import PartitionSpec as P

adiabatic = 1.4
courant = 0.15
halo = 3
quarters = 4


def primitives(fields):
    density, mx, my, mz, energy = fields
    inverse = pl.reciprocal(density, approx=True)
    vx, vy, vz = mx * inverse, my * inverse, mz * inverse
    doubled = mx * vx + my * vy + mz * vz
    pressure = (adiabatic - 1.0) * energy - (0.5 * (adiabatic - 1.0)) * doubled
    return [density, vx, vy, vz, pressure]


def signed(step):
    return step, jnp.maximum(step, 0.0), jnp.minimum(step, 0.0)


def half_slope(ahead, behind):
    top = jnp.minimum(ahead[1], behind[1])
    bottom = jnp.maximum(ahead[2], behind[2])
    return jnp.maximum(jnp.minimum(0.25 * (ahead[0] + behind[0]), top), bottom)


def face_offset(ahead, slope, slope_next):
    offset = 0.5 * ahead[0] - (1.0 / 3.0) * (slope_next - slope)
    return jnp.minimum(jnp.maximum(offset, ahead[2]), ahead[1])


def limited(first, second):
    doubled = second + second
    return jnp.maximum(jnp.minimum(first, jnp.maximum(doubled, 0.0)), jnp.minimum(doubled, 0.0))


def hll(left, right, normal):
    dl, pl_, ul = left[0], left[4], left[1 + normal]
    dr, pr, ur = right[0], right[4], right[1 + normal]
    tl = adiabatic * pl_
    tr = adiabatic * pr
    al = tl * lax.rsqrt(tl * dl)
    ar = tr * lax.rsqrt(tr * dr)
    slowest = jnp.minimum(jnp.minimum(ul - al, ur - ar), 0.0)
    fastest = jnp.maximum(jnp.maximum(ul + al, ur + ar), 0.0)
    cl = fastest * (courant * pl.reciprocal(fastest - slowest, approx=True))
    cr = courant - cl
    wl = cl * (ul - slowest)
    wr = cr * (ur - fastest)
    ml = wl * dl
    mr = wr * dr
    ql = cl * pl_
    qr = cr * pr
    gl = [ml * left[1 + k] for k in range(3)]
    gr = [mr * right[1 + k] for k in range(3)]
    kinetic = (
        gl[0] * left[1] + gl[1] * left[2] + gl[2] * left[3]
        + gr[0] * right[1] + gr[1] * right[2] + gr[2] * right[3]
    )
    flux = [ml + mr] + [gl[k] + gr[k] for k in range(3)]
    flux[1 + normal] = flux[1 + normal] + (ql + qr)
    inner = (1.0 / (adiabatic - 1.0)) * (wl * pl_ + wr * pr)
    flux.append(0.5 * kinetic + inner + (ql * ul + qr * ur))
    return flux


class Line:
    def __init__(self, load, normal, period=None):
        self.load, self.normal, self.period = load, normal, period
        self.known = {}

    def once(self, name, index, make):
        if self.period is not None:
            index = index % self.period
        if (name, index) not in self.known:
            self.known[(name, index)] = make(index)
        return self.known[(name, index)]

    def prims(self, i):
        return self.once("q", i, lambda i: primitives(self.load(i)))

    def diff(self, i):
        return self.once("d", i, lambda i: [signed(b - a) for a, b in zip(self.prims(i), self.prims(i + 1))])

    def slope(self, i):
        return self.once("s", i, lambda i: [half_slope(a, b) for a, b in zip(self.diff(i), self.diff(i - 1))])

    def up(self, i):
        return self.once("u", i, lambda i: [face_offset(d, s, t) for d, s, t in zip(self.diff(i), self.slope(i), self.slope(i + 1))])

    def down(self, i):
        return self.once("w", i, lambda i: [d[0] - u for d, u in zip(self.diff(i - 1), self.up(i - 1))])

    def low(self, i):
        return self.once("l", i, lambda i: [q - limited(w, u) for q, w, u in zip(self.prims(i), self.down(i), self.up(i))])

    def high(self, i):
        return self.once("h", i, lambda i: [q + limited(u, w) for q, w, u in zip(self.prims(i), self.down(i), self.up(i))])

    def flux(self, i):
        return self.once("f", i, lambda i: hll(self.high(i), self.low(i + 1), self.normal))

    def swept(self, i):
        before, after = self.flux(i - 1), self.flux(i)
        return [u - (b - a) for u, a, b in zip(self.load(i), before, after)]


def rolled(fields, ahead, behind, normal):
    states = primitives(fields)
    low, high = [], []
    for q in states:
        d = ahead(q) - q
        s = half_slope(signed(d), signed(behind(d)))
        u = face_offset(signed(d), s, ahead(s))
        w = behind(d - u)
        low.append(ahead(q - limited(w, u)))
        high.append(q + limited(u, w))
    return hll(high, low, normal)


def shifts(axis, size):
    return (lambda a: pltpu.roll(a, size - 1, axis), lambda a: pltpu.roll(a, 1, axis))


def row(index):
    return pl.ds(index, 8)


def fields_of(density, momentum, energy):
    return [density, momentum.at[0], momentum.at[1], momentum.at[2], energy]


def odd_rank(axis):
    return lax.axis_index(axis) % 2 == 1


class Received:
    def __init__(self, odd, on_odd, on_even):
        self.odd, self.on_odd, self.on_even = odd, on_odd, on_even

    def __getitem__(self, index):
        return jnp.where(self.odd, self.on_odd[index], self.on_even[index])


def sides_of(axis, far, near):
    odd = odd_rank(axis)
    return Received(odd, near, far), Received(odd, far, near)


def rows_kernel(density, momentum, energy, far, near, held, arrived):
    sources = fields_of(density, momentum, energy)
    nx, ny, nz = density.shape
    copies = []
    for f in range(5):
        for side in range(2):
            tile = sources[f].at[:, pl.ds(side * (ny - 8), 8), :]
            copies.append(pltpu.make_async_copy(tile, held.at[side, f], arrived.at[side, f]))
    for copy in copies:
        copy.start()
    odd = odd_rank("gy")
    for f in range(5):
        copies[2 * f].wait()
        copies[2 * f + 1].wait()
        top, bottom = (held.at[side, f].reshape(nx * 8, nz) for side in range(2))
        for r in range(halo):
            first = top[pl.ds(r, nx, stride=8), :]
            last = bottom[pl.ds(8 - halo + r, nx, stride=8), :]
            far[f, r] = jnp.where(odd, last, first)
            near[f, r] = jnp.where(odd, first, last)


def alternate(steps, parts, others, other_parts):
    made = 0
    for part, _ in enumerate(steps):
        while made * parts < (part + 1) * other_parts:
            next(others, None)
            made += 1
    for _ in others:
        pass


def turn_in(source, turned, count, b):
    lanes = source.shape[-1]
    span = lanes // quarters
    for f in range(5):
        block = source[f].T
        for q in range(quarters):
            turned[f, pl.ds(q * count + b, span, stride=quarters * count), :] = block[q * span : (q + 1) * span]
        yield


def turn_out(turned, count, f, store):
    lanes = turned.shape[-1]
    span = lanes // quarters
    for b in range(count):
        parts = [turned[f, pl.ds(q * count + b, span, stride=quarters * count), :] for q in range(quarters)]
        store(f, b, jnp.concatenate(parts, axis=0).T)
        yield


def ends(turned, count, far, near):
    width = quarters * count
    span = turned.shape[1] // width
    odd = odd_rank("gz")
    for f in range(5):
        for k in range(halo):
            upward = turned[f, pl.ds((span - halo + k + 1) * width - count, count), :]
            downward = turned[f, pl.ds(k * width, count), :]
            at = pl.ds((f * halo + k) * count, count)
            far[at, :] = jnp.where(odd, upward, downward)
            near[at, :] = jnp.where(odd, downward, upward)


def placed(ends, f, k, count, at):
    first = (f * halo + k) * count
    start = min(max(first - at, 0), 5 * halo * count - 8)
    window = ends[row(start), :]
    shift = (at + start - first) % 8
    return pltpu.roll(window, shift, 0) if shift else window


def z_lines(own, count, left=None, right=None):
    width = quarters * count
    span = own.shape[1] // width
    place = lax.broadcasted_iota(jnp.int32, (8, own.shape[-1]), 0)
    for start in range(0, width, 8):

        def load(i, start=start):
            if 0 <= i < span:
                return [own[f, row(i * width + start), :] for f in range(5)]
            if i < 0:
                fields = [own[f, row((i + span) * width + start - count), :] for f in range(5)]
                if start == 0:
                    fields = [jnp.where(place < count, placed(left, f, i + halo, count, 0), a) for f, a in enumerate(fields)]
                return fields
            fields = [own[f, row((i - span) * width + start + count), :] for f in range(5)]
            if start + 8 == width:
                fields = [jnp.where(place >= 8 - count, placed(right, f, i - span, count, 8 - count), a) for f, a in enumerate(fields)]
            return fields

        yield start, span, Line(load, 2)


def z_middle(own, swept, joint, count):
    for start, span, line in z_lines(own, count):
        for i in range(halo, span - halo):
            for f, value in enumerate(line.swept(i)):
                swept[f, row(i * quarters * count + start), :] = value
            yield
        for end, face in enumerate((halo - 1, span - halo - 1)):
            for f, value in enumerate(line.flux(face)):
                joint[f, end, row(start), :] = value


def z_ends(own, far, near, middle, joint, swept, count):
    for start, span, line in z_lines(own, count, *sides_of("gz", far, near)):
        for end, face in enumerate((halo - 1, span - halo - 1)):
            line.known[("f", face)] = [joint[f, end, row(start), :] for f in range(5)]
        for i in range(span):
            at = row(i * quarters * count + start)
            inside = halo <= i < span - halo
            values = [middle[f, at, :] for f in range(5)] if inside else line.swept(i)
            for f, value in enumerate(values):
                swept[f, at, :] = value


def inner_kernel(density, momentum, energy, turned, far, near, rim, beside, joint, held, *strips):
    nx, ny, lanes = density.shape
    deep = lanes // nx
    sources = fields_of(density, momentum, energy)

    @pl.loop(0, ny // 8)
    def _(tile):
        start = pl.multiple_of(tile * 8, 8)
        line = Line(lambda i: [s[i, pl.ds(start, 8), :] for s in sources], 0, nx)
        for i in range(nx):
            for f, value in enumerate(line.swept(i)):
                held[f, pl.ds(pl.multiple_of(i * ny + start, 8), 8), :] = value

    def sweep(tile):
        some = row(tile * 8)
        line = Line(lambda i: [held[f, pl.ds(tile * (8 * ny) + i, 8, stride=ny), :] for f in range(5)], 1)
        for i in range(halo, ny - halo):
            for f, value in enumerate(line.swept(i)):
                if deep <= i < ny - deep:
                    strips[tile][f, row((i - deep) * 8), :] = value
                else:
                    beside[f, i - halo if i < deep else i - ny + 2 * deep - halo, some, :] = value
            yield
        for f in range(5):
            joint[f, 0, some, :] = line.flux(halo - 1)[f]
            joint[f, 1, some, :] = line.flux(ny - halo - 1)[f]
        kept = deep + halo - 1
        for r in range(kept):
            for f, (a, b) in enumerate(zip(line.load(r), line.load(ny - kept + r))):
                rim[f, r, some, :] = a
                rim[f, kept + r, some, :] = b

    count = len(strips)
    turns = iter(())
    for tile in range(count):
        alternate(sweep(tile), ny - 2 * halo, turns, 5)
        turns = turn_in(strips[tile], turned, count, tile)
    for _ in turns:
        pass
    ends(turned, count, far, near)


def edge_kernel(far, near, rim, beside, joint, _, turned, far_end, near_end, ghost, *outers):
    _, kept, nx, lanes = rim.shape
    kept = kept // 2
    deep = lanes // nx
    ahead, behind = shifts(0, nx)
    for side, source in enumerate(sides_of("gy", far, near)):

        @pl.loop(0, halo)
        def _(r):
            fields = [source[f, r] for f in range(5)]
            flux = rolled(fields, ahead, behind, 0)
            for f in range(5):
                ghost[f, side * halo + r] = fields[f] - (flux[f] - behind(flux[f]))

    share = nx // 8 // len(outers)

    def sweep(block):
        for half in range(share):
            some = row((block * share + half) * 8)
            for side in range(2):

                def load(i, side=side, some=some):
                    if side == 0:
                        source, at = (ghost, i + halo) if i < 0 else (rim, i)
                    else:
                        source, at = (ghost, i - deep + halo) if i >= deep else (rim, i + kept + kept - deep)
                    return [source[f, at, some, :] for f in range(5)]

                line = Line(load, 1)
                known = halo - 1 if side == 0 else deep - halo - 1
                line.known[("f", known)] = [joint[f, side, some, :] for f in range(5)]
                for i in range(deep):
                    if side == 0 and i >= halo:
                        values = [beside[f, i - halo, some, :] for f in range(5)]
                    elif side == 1 and i < deep - halo:
                        values = [beside[f, i + deep - halo, some, :] for f in range(5)]
                    else:
                        values = line.swept(i)
                    for f, value in enumerate(values):
                        outers[block][f, row(((half * 2 + side) * deep + i) * 8), :] = value
                    yield

    turns = iter(())
    for block, outer in enumerate(outers):
        alternate(sweep(block), share * 2 * deep, turns, 5)
        turns = turn_in(outer, turned, len(outers), block)
    for _ in turns:
        pass
    ends(turned, 2, far_end, near_end)


def middle_kernel(count, own, swept, joint):
    for _ in z_middle(own, swept, joint, count):
        pass


def ends_kernel(count, own, far, near, middle, joint, edges, inner, edges_middle, edges_joint, density, momentum, energy, swept, whole, sent):
    lanes = own.shape[-1]
    nx, ny, _ = density.shape
    deep = lanes // nx
    outs = fields_of(density, momentum, energy)
    z_ends(own, far, near, middle, joint, swept, count)
    copies = [pltpu.make_async_copy(whole.at[f], outs[f].at[:, pl.ds(8, ny - 16), :], sent.at[f]) for f in range(5)]

    def store(f, b, block):
        inner[f, pl.ds(b * lanes, lanes), :] = block
        flat = whole.at[f].reshape(nx * (ny - 16), lanes)
        for y in range(8, ny - 8):
            at = (y - deep) * 8
            flat[pl.ds(b * 8 * (ny - 16) + y - 8, 8, stride=ny - 16), :] = block[at : at + 8]

    def turns():
        for f in range(5):
            yield from turn_out(swept, count, f, store)
            copies[f].start()

    cells = edges.shape[1] // (quarters * 2) - 2 * halo
    alternate(z_middle(edges, edges_middle, edges_joint, 2), cells // 2, turns(), 5 * count)
    for copy in copies:
        copy.wait()


def last_kernel(own, far, near, middle, joint, inner, _, __, ___, density, momentum, energy, swept, whole, sent):
    lanes = own.shape[-1]
    nx, ny, _ = density.shape
    deep = lanes // nx
    strip = 2 * deep * 8
    outs = fields_of(density, momentum, energy)
    z_ends(own, far, near, middle, joint, swept, 2)

    def put(f, x, y, value):
        flat = whole.at[f, int(y >= 8)].reshape(nx * 8, lanes)
        flat[pl.ds(x * 8 + y % 8, 8, stride=8), :] = value

    def store(f, b, block):
        for half in range(lanes // strip):
            for k in range(2 * deep):
                at = half * strip + k * 8
                put(f, (b * (lanes // strip) + half) * 8, k if k < deep else ny - 2 * deep + k, block[at : at + 8])

    for f in range(5):
        for b in range(nx // 8):
            for y in [*range(deep, 8), *range(ny - 8, ny - deep)]:
                put(f, b * 8, y, inner[f, row(b * lanes + (y - deep) * 8), :])
    copies = []
    for f in range(5):
        for _ in turn_out(swept, 2, f, store):
            pass
        for side in range(2):
            rows = outs[f].at[:, pl.ds(side * (ny - 8), 8), :]
            copies.append(pltpu.make_async_copy(whole.at[f, side], rows, sent.at[f, side]))
            copies[-1].start()
    for copy in copies:
        copy.wait()


def call(kernel, shapes, scratch, arguments, in_specs=None, out_specs=None, aliases=None):
    whole = pl.BlockSpec(memory_space=pltpu.VMEM)
    return pl.pallas_call(
        kernel,
        out_shape=[jax.ShapeDtypeStruct(shape, jnp.float32) for shape in shapes],
        in_specs=[whole] * len(arguments) if in_specs is None else in_specs,
        out_specs=[whole] * len(shapes) if out_specs is None else out_specs,
        scratch_shapes=[pltpu.VMEM(a, jnp.float32) if isinstance(a, tuple) else a for a in scratch],
        input_output_aliases=aliases or {},
        compiler_params=pltpu.CompilerParams(vmem_limit_bytes=24 * 2**20),
    )(*arguments)


def exchange(axis, far, near):
    ranks = lax.axis_size(axis)
    if ranks % 2:
        raise ValueError("odd ring")
    pairs = []
    for start in (1, 0):
        there = [(rank, (rank + 1) % ranks) for rank in range(start, ranks, 2)]
        pairs.append(there + [(b, a) for a, b in there])
    return lax.ppermute(far, axis, pairs[0]), lax.ppermute(near, axis, pairs[1])


def y_rows(density, momentum, energy):
    nx, ny, nz = density.shape
    shape = (5, halo, nx, nz)
    return pl.pallas_call(
        rows_kernel,
        out_shape=[pltpu.VMEM(shape, jnp.float32)] * 2,
        in_specs=[pl.BlockSpec(memory_space=pltpu.HBM)] * 3,
        out_specs=[pl.BlockSpec(memory_space=pltpu.VMEM)] * 2,
        scratch_shapes=[pltpu.VMEM((2, 5, nx, 8, nz), jnp.float32), pltpu.SemaphoreType.DMA((2, 5))],
        compiler_params=pltpu.CompilerParams(vmem_limit_bytes=16 * 2**20),
    )(*(pltpu.with_memory_space_constraint(a, pltpu.HBM) for a in (density, momentum, energy)))


def body(density, momentum, energy):
    nx, ny, nz = density.shape
    deep = nz // nx
    count = ny // deep - 2
    kept = deep + halo - 1

    far_rows, near_rows = exchange("gy", *y_rows(density, momentum, energy))
    turned, far, near, rim, beside, joint = call(
        inner_kernel,
        [(5, count * nz, nz)] + [(5 * halo * count, nz)] * 2 + [(5, 2 * kept, nx, nz), (5, 2 * (deep - halo), nx, nz), (5, 2, nx, nz)],
        [(5, nx * ny, nz)] + [(5, nz, nz)] * count,
        [density, momentum, energy],
    )
    far, near = exchange("gz", far, near)
    middle, faces = call(
        functools.partial(middle_kernel, count),
        [(5, count * nz, nz), (5, 2, quarters * count, nz)],
        [],
        [turned],
    )
    whole, anywhere = (pl.BlockSpec(memory_space=space) for space in (pltpu.VMEM, pl.ANY))
    edges, far_edges, near_edges = call(
        edge_kernel,
        [(5, 2 * nz, nz)] + [(5 * halo * 2, nz)] * 2,
        [(5, 2 * halo, nx, nz)] + [(5, nz, nz)] * 2,
        [far_rows, near_rows, rim, beside, joint, faces],
        [whole] * 5 + [anywhere],
    )
    far_edges, near_edges = exchange("gz", far_edges, near_edges)
    results = [(nx, ny, nz), (3, nx, ny, nz), (nx, ny, nz)]
    inner, edges_middle, edges_faces, *outs = call(
        functools.partial(ends_kernel, count),
        [(5, count * nz, nz), (5, 2 * nz, nz), (5, 2, quarters * 2, nz)] + results,
        [(5, count * nz, nz), (5, nx, ny - 16, nz), pltpu.SemaphoreType.DMA((5,))],
        [turned, far, near, middle, faces, edges],
        out_specs=[whole] * 3 + [anywhere] * 3,
    )
    outs = call(
        last_kernel,
        results,
        [(5, 2 * nz, nz), (5, 2, nx, 8, nz), pltpu.SemaphoreType.DMA((5, 2))],
        [edges, far_edges, near_edges, edges_middle, edges_faces, inner, *outs],
        [whole] * 6 + [anywhere] * 3,
        [anywhere] * 3,
        {6: 0, 7: 1, 8: 2},
    )
    return tuple(outs)


def solution(mesh):
    return jax.shard_map(
        body,
        mesh=mesh,
        in_specs=(P(None, "gy", "gz"), P(None, None, "gy", "gz"), P(None, "gy", "gz")),
        out_specs=(P(None, "gy", "gz"), P(None, None, "gy", "gz"), P(None, "gy", "gz")),
        check_vma=False,
    )
```

```python
import functools

import jax
import jax.numpy as jnp
from jax import lax
from jax.experimental import pallas as pl
from jax.experimental.pallas import tpu as pltpu
from jax.sharding import PartitionSpec as P

adiabatic = 1.4
courant = 0.15
halo = 3
quarters = 4


def primitives(fields):
    density, mx, my, mz, energy = fields
    inverse = pl.reciprocal(density, approx=True)
    vx, vy, vz = mx * inverse, my * inverse, mz * inverse
    doubled = mx * vx + my * vy + mz * vz
    pressure = (adiabatic - 1.0) * energy - (0.5 * (adiabatic - 1.0)) * doubled
    return [density, vx, vy, vz, pressure]


def signed(step):
    return step, jnp.maximum(step, 0.0), jnp.minimum(step, 0.0)


def half_slope(ahead, behind):
    top = jnp.minimum(ahead[1], behind[1])
    bottom = jnp.maximum(ahead[2], behind[2])
    return jnp.maximum(jnp.minimum(0.25 * (ahead[0] + behind[0]), top), bottom)


def face_offset(ahead, slope, slope_next):
    offset = 0.5 * ahead[0] - (1.0 / 3.0) * (slope_next - slope)
    return jnp.minimum(jnp.maximum(offset, ahead[2]), ahead[1])


def limited(first, second):
    doubled = second + second
    return jnp.maximum(jnp.minimum(first, jnp.maximum(doubled, 0.0)), jnp.minimum(doubled, 0.0))


def hll(left, right, normal):
    dl, pl_, ul = left[0], left[4], left[1 + normal]
    dr, pr, ur = right[0], right[4], right[1 + normal]
    tl = adiabatic * pl_
    tr = adiabatic * pr
    al = tl * lax.rsqrt(tl * dl)
    ar = tr * lax.rsqrt(tr * dr)
    slowest = jnp.minimum(jnp.minimum(ul - al, ur - ar), 0.0)
    fastest = jnp.maximum(jnp.maximum(ul + al, ur + ar), 0.0)
    cl = fastest * (courant * pl.reciprocal(fastest - slowest, approx=True))
    cr = courant - cl
    wl = cl * (ul - slowest)
    wr = cr * (ur - fastest)
    ml = wl * dl
    mr = wr * dr
    ql = cl * pl_
    qr = cr * pr
    gl = [ml * left[1 + k] for k in range(3)]
    gr = [mr * right[1 + k] for k in range(3)]
    kinetic = (
        gl[0] * left[1] + gl[1] * left[2] + gl[2] * left[3]
        + gr[0] * right[1] + gr[1] * right[2] + gr[2] * right[3]
    )
    flux = [ml + mr] + [gl[k] + gr[k] for k in range(3)]
    flux[1 + normal] = flux[1 + normal] + (ql + qr)
    inner = (1.0 / (adiabatic - 1.0)) * (wl * pl_ + wr * pr)
    flux.append(0.5 * kinetic + inner + (ql * ul + qr * ur))
    return flux


class Line:
    def __init__(self, load, normal, period=None):
        self.load, self.normal, self.period = load, normal, period
        self.known = {}

    def once(self, name, index, make):
        if self.period is not None:
            index = index % self.period
        if (name, index) not in self.known:
            self.known[(name, index)] = make(index)
        return self.known[(name, index)]

    def prims(self, i):
        return self.once("q", i, lambda i: primitives(self.load(i)))

    def diff(self, i):
        return self.once("d", i, lambda i: [signed(b - a) for a, b in zip(self.prims(i), self.prims(i + 1))])

    def slope(self, i):
        return self.once("s", i, lambda i: [half_slope(a, b) for a, b in zip(self.diff(i), self.diff(i - 1))])

    def up(self, i):
        return self.once("u", i, lambda i: [face_offset(d, s, t) for d, s, t in zip(self.diff(i), self.slope(i), self.slope(i + 1))])

    def down(self, i):
        return self.once("w", i, lambda i: [d[0] - u for d, u in zip(self.diff(i - 1), self.up(i - 1))])

    def low(self, i):
        return self.once("l", i, lambda i: [q - limited(w, u) for q, w, u in zip(self.prims(i), self.down(i), self.up(i))])

    def high(self, i):
        return self.once("h", i, lambda i: [q + limited(u, w) for q, w, u in zip(self.prims(i), self.down(i), self.up(i))])

    def flux(self, i):
        return self.once("f", i, lambda i: hll(self.high(i), self.low(i + 1), self.normal))

    def swept(self, i):
        before, after = self.flux(i - 1), self.flux(i)
        return [u - (b - a) for u, a, b in zip(self.load(i), before, after)]


def rolled(fields, ahead, behind, normal):
    states = primitives(fields)
    low, high = [], []
    for q in states:
        d = ahead(q) - q
        s = half_slope(signed(d), signed(behind(d)))
        u = face_offset(signed(d), s, ahead(s))
        w = behind(d - u)
        low.append(ahead(q - limited(w, u)))
        high.append(q + limited(u, w))
    return hll(high, low, normal)


def shifts(axis, size):
    return (lambda a: pltpu.roll(a, size - 1, axis), lambda a: pltpu.roll(a, 1, axis))


def row(index):
    return pl.ds(index, 8)


def fields_of(density, momentum, energy):
    return [density, momentum.at[0], momentum.at[1], momentum.at[2], energy]


def odd_rank(axis):
    return lax.axis_index(axis) % 2 == 1


class Received:
    def __init__(self, odd, on_odd, on_even):
        self.odd, self.on_odd, self.on_even = odd, on_odd, on_even

    def __getitem__(self, index):
        return jnp.where(self.odd, self.on_odd[index], self.on_even[index])


def sides_of(axis, far, near):
    odd = odd_rank(axis)
    return Received(odd, near, far), Received(odd, far, near)


def rows_kernel(density, momentum, energy, far, near, held, arrived):
    sources = fields_of(density, momentum, energy)
    nx, ny, nz = density.shape
    copies = []
    for f in range(5):
        for side in range(2):
            tile = sources[f].at[:, pl.ds(side * (ny - 8), 8), :]
            copies.append(pltpu.make_async_copy(tile, held.at[side, f], arrived.at[side, f]))
    for copy in copies:
        copy.start()
    odd = odd_rank("gy")
    for f in range(5):
        copies[2 * f].wait()
        copies[2 * f + 1].wait()
        top, bottom = (held.at[side, f].reshape(nx * 8, nz) for side in range(2))
        for r in range(halo):
            first = top[pl.ds(r, nx, stride=8), :]
            last = bottom[pl.ds(8 - halo + r, nx, stride=8), :]
            far[f, r] = jnp.where(odd, last, first)
            near[f, r] = jnp.where(odd, first, last)


def alternate(steps, parts, others, other_parts):
    made = 0
    for part, _ in enumerate(steps):
        while made * parts < (part + 1) * other_parts:
            next(others, None)
            made += 1
    for _ in others:
        pass


def turn_in(source, turned, count, b):
    lanes = source.shape[-1]
    span = lanes // quarters
    for f in range(5):
        block = source[f].T
        for q in range(quarters):
            turned[f, pl.ds(q * count + b, span, stride=quarters * count), :] = block[q * span : (q + 1) * span]
        yield


def turn_out(turned, count, f, store):
    lanes = turned.shape[-1]
    span = lanes // quarters
    for b in range(count):
        parts = [turned[f, pl.ds(q * count + b, span, stride=quarters * count), :] for q in range(quarters)]
        store(f, b, jnp.concatenate(parts, axis=0).T)
        yield


def ends(turned, count, far, near):
    width = quarters * count
    span = turned.shape[1] // width
    odd = odd_rank("gz")
    for f in range(5):
        for k in range(halo):
            upward = turned[f, pl.ds((span - halo + k + 1) * width - count, count), :]
            downward = turned[f, pl.ds(k * width, count), :]
            at = pl.ds((f * halo + k) * count, count)
            far[at, :] = jnp.where(odd, upward, downward)
            near[at, :] = jnp.where(odd, downward, upward)


def placed(ends, f, k, count, at):
    first = (f * halo + k) * count
    start = min(max(first - at, 0), 5 * halo * count - 8)
    window = ends[row(start), :]
    shift = (at + start - first) % 8
    return pltpu.roll(window, shift, 0) if shift else window


def z_lines(own, count, left=None, right=None):
    width = quarters * count
    span = own.shape[1] // width
    place = lax.broadcasted_iota(jnp.int32, (8, own.shape[-1]), 0)
    for start in range(0, width, 8):

        def load(i, start=start):
            if 0 <= i < span:
                return [own[f, row(i * width + start), :] for f in range(5)]
            if i < 0:
                fields = [own[f, row((i + span) * width + start - count), :] for f in range(5)]
                if start == 0:
                    fields = [jnp.where(place < count, placed(left, f, i + halo, count, 0), a) for f, a in enumerate(fields)]
                return fields
            fields = [own[f, row((i - span) * width + start + count), :] for f in range(5)]
            if start + 8 == width:
                fields = [jnp.where(place >= 8 - count, placed(right, f, i - span, count, 8 - count), a) for f, a in enumerate(fields)]
            return fields

        yield start, span, Line(load, 2)


def z_middle(own, swept, joint, count):
    for start, span, line in z_lines(own, count):
        for i in range(halo, span - halo):
            for f, value in enumerate(line.swept(i)):
                swept[f, row(i * quarters * count + start), :] = value
            yield
        for end, face in enumerate((halo - 1, span - halo - 1)):
            for f, value in enumerate(line.flux(face)):
                joint[f, end, row(start), :] = value


def z_ends(own, far, near, middle, joint, swept, count):
    for start, span, line in z_lines(own, count, *sides_of("gz", far, near)):
        for end, face in enumerate((halo - 1, span - halo - 1)):
            line.known[("f", face)] = [joint[f, end, row(start), :] for f in range(5)]
        for i in range(span):
            at = row(i * quarters * count + start)
            inside = halo <= i < span - halo
            values = [middle[f, at, :] for f in range(5)] if inside else line.swept(i)
            for f, value in enumerate(values):
                swept[f, at, :] = value


def inner_kernel(density, momentum, energy, turned, far, near, rim, beside, joint, held, *strips):
    nx, ny, lanes = density.shape
    deep = lanes // nx
    sources = fields_of(density, momentum, energy)

    @pl.loop(0, ny // 8)
    def _(tile):
        start = pl.multiple_of(tile * 8, 8)
        line = Line(lambda i: [s[i, pl.ds(start, 8), :] for s in sources], 0, nx)
        for i in range(nx):
            for f, value in enumerate(line.swept(i)):
                held[f, pl.ds(pl.multiple_of(i * ny + start, 8), 8), :] = value

    def sweep(tile):
        some = row(tile * 8)
        line = Line(lambda i: [held[f, pl.ds(tile * (8 * ny) + i, 8, stride=ny), :] for f in range(5)], 1)
        for i in range(halo, ny - halo):
            for f, value in enumerate(line.swept(i)):
                if deep <= i < ny - deep:
                    strips[tile][f, row((i - deep) * 8), :] = value
                else:
                    beside[f, i - halo if i < deep else i - ny + 2 * deep - halo, some, :] = value
            yield
        for f in range(5):
            joint[f, 0, some, :] = line.flux(halo - 1)[f]
            joint[f, 1, some, :] = line.flux(ny - halo - 1)[f]
        kept = deep + halo - 1
        for r in range(kept):
            for f, (a, b) in enumerate(zip(line.load(r), line.load(ny - kept + r))):
                rim[f, r, some, :] = a
                rim[f, kept + r, some, :] = b

    count = len(strips)
    turns = iter(())
    for tile in range(count):
        alternate(sweep(tile), ny - 2 * halo, turns, 5)
        turns = turn_in(strips[tile], turned, count, tile)
    for _ in turns:
        pass
    ends(turned, count, far, near)


def edge_kernel(near, far, rim, beside, joint, _, turned, far_end, near_end, ghost, *outers):
    _, kept, nx, lanes = rim.shape
    kept = kept // 2
    deep = lanes // nx
    ahead, behind = shifts(0, nx)
    for side, source in enumerate(sides_of("gy", far, near)):

        @pl.loop(0, halo)
        def _(r):
            fields = [source[f, r] for f in range(5)]
            flux = rolled(fields, ahead, behind, 0)
            for f in range(5):
                ghost[f, side * halo + r] = fields[f] - (flux[f] - behind(flux[f]))

    share = nx // 8 // len(outers)

    def sweep(block):
        for half in range(share):
            some = row((block * share + half) * 8)
            for side in range(2):

                def load(i, side=side, some=some):
                    if side == 0:
                        source, at = (ghost, i + halo) if i < 0 else (rim, i)
                    else:
                        source, at = (ghost, i - deep + halo) if i >= deep else (rim, i + kept + kept - deep)
                    return [source[f, at, some, :] for f in range(5)]

                line = Line(load, 1)
                known = halo - 1 if side == 0 else deep - halo - 1
                line.known[("f", known)] = [joint[f, side, some, :] for f in range(5)]
                for i in range(deep):
                    if side == 0 and i >= halo:
                        values = [beside[f, i - halo, some, :] for f in range(5)]
                    elif side == 1 and i < deep - halo:
                        values = [beside[f, i + deep - halo, some, :] for f in range(5)]
                    else:
                        values = line.swept(i)
                    for f, value in enumerate(values):
                        outers[block][f, row(((half * 2 + side) * deep + i) * 8), :] = value
                    yield

    turns = iter(())
    for block, outer in enumerate(outers):
        alternate(sweep(block), share * 2 * deep, turns, 5)
        turns = turn_in(outer, turned, len(outers), block)
    for _ in turns:
        pass
    ends(turned, 2, far_end, near_end)


def middle_kernel(count, own, swept, joint):
    for _ in z_middle(own, swept, joint, count):
        pass


def ends_kernel(count, own, far, near, middle, joint, edges, inner, edges_middle, edges_joint, swept):
    lanes = own.shape[-1]
    z_ends(own, far, near, middle, joint, swept, count)

    def store(f, b, block):
        inner[f, pl.ds(b * lanes, lanes), :] = block

    cells = edges.shape[1] // (quarters * 2) - 2 * halo
    turns = (None for f in range(5) for _ in turn_out(swept, count, f, store))
    alternate(z_middle(edges, edges_middle, edges_joint, 2), cells, turns, 5 * count)


def last_kernel(ny, own, far, near, middle, joint, inner, density, momentum, energy, swept, whole, sent):
    lanes = own.shape[-1]
    nx = density.shape[0] // ny
    deep = lanes // nx
    strip = 2 * deep * 8
    outs = fields_of(density, momentum, energy)
    z_ends(own, far, near, middle, joint, swept, 2)

    def store(f, b, block):
        for half in range(lanes // strip):
            for k in range(2 * deep):
                y = k if k < deep else ny - 2 * deep + k
                at = half * strip + k * 8
                whole[f, pl.ds((b * (lanes // strip) + half) * 8 * ny + y, 8, stride=ny), :] = block[at : at + 8]

    copies = [pltpu.make_async_copy(whole.at[f], outs[f], sent.at[f]) for f in range(5)]
    for f in range(5):
        for b in range(nx // 8):
            for i in range(deep, ny - deep):
                whole[f, pl.ds(b * 8 * ny + i, 8, stride=ny), :] = inner[f, row(b * lanes + (i - deep) * 8), :]
        for _ in turn_out(swept, 2, f, store):
            pass
        copies[f].start()
    for copy in copies:
        copy.wait()


def call(kernel, shapes, scratch, arguments, in_specs=None, out_spec=None):
    whole = pl.BlockSpec(memory_space=pltpu.VMEM)
    return pl.pallas_call(
        kernel,
        out_shape=[jax.ShapeDtypeStruct(shape, jnp.float32) for shape in shapes],
        in_specs=[whole] * len(arguments) if in_specs is None else in_specs,
        out_specs=[whole if out_spec is None else out_spec] * len(shapes),
        scratch_shapes=[pltpu.VMEM(a, jnp.float32) if isinstance(a, tuple) else a for a in scratch],
        compiler_params=pltpu.CompilerParams(vmem_limit_bytes=24 * 2**20),
    )(*arguments)


def exchange(axis, far, near):
    ranks = lax.axis_size(axis)
    if ranks % 2:
        raise ValueError("odd ring")
    pairs = []
    for start in (1, 0):
        there = [(rank, (rank + 1) % ranks) for rank in range(start, ranks, 2)]
        pairs.append(there + [(b, a) for a, b in there])
    return lax.ppermute(far, axis, pairs[0]), lax.ppermute(near, axis, pairs[1])


def y_rows(density, momentum, energy):
    nx, ny, nz = density.shape
    shape = (5, halo, nx, nz)
    return pl.pallas_call(
        rows_kernel,
        out_shape=[pltpu.VMEM(shape, jnp.float32)] * 2,
        in_specs=[pl.BlockSpec(memory_space=pltpu.HBM)] * 3,
        out_specs=[pl.BlockSpec(memory_space=pltpu.VMEM)] * 2,
        scratch_shapes=[pltpu.VMEM((2, 5, nx, 8, nz), jnp.float32), pltpu.SemaphoreType.DMA((2, 5))],
        compiler_params=pltpu.CompilerParams(vmem_limit_bytes=16 * 2**20),
    )(*(pltpu.with_memory_space_constraint(a, pltpu.HBM) for a in (density, momentum, energy)))


def body(density, momentum, energy):
    nx, ny, nz = density.shape
    deep = nz // nx
    count = ny // deep - 2
    kept = deep + halo - 1

    far_rows, near_rows = exchange("gy", *y_rows(density, momentum, energy))
    turned, far, near, rim, beside, joint = call(
        inner_kernel,
        [(5, count * nz, nz)] + [(5 * halo * count, nz)] * 2 + [(5, 2 * kept, nx, nz), (5, 2 * (deep - halo), nx, nz), (5, 2, nx, nz)],
        [(5, nx * ny, nz)] + [(5, nz, nz)] * count,
        [density, momentum, energy],
    )
    far, near = exchange("gz", far, near)
    middle, faces = call(
        functools.partial(middle_kernel, count),
        [(5, count * nz, nz), (5, 2, quarters * count, nz)],
        [],
        [turned],
    )
    whole, anywhere = (pl.BlockSpec(memory_space=space) for space in (pltpu.VMEM, pl.ANY))
    edges, far_edges, near_edges = call(
        edge_kernel,
        [(5, 2 * nz, nz)] + [(5 * halo * 2, nz)] * 2,
        [(5, 2 * halo, nx, nz)] + [(5, nz, nz)] * 2,
        [near_rows, far_rows, rim, beside, joint, faces],
        [whole] * 5 + [anywhere],
    )
    far_edges, near_edges = exchange("gz", far_edges, near_edges)
    inner, edges_middle, edges_faces = call(
        functools.partial(ends_kernel, count),
        [(5, count * nz, nz), (5, 2 * nz, nz), (5, 2, quarters * 2, nz)],
        [(5, count * nz, nz)],
        [turned, far, near, middle, faces, edges],
    )
    cells = nx * ny
    outs = call(
        functools.partial(last_kernel, ny),
        [(cells, nz), (3, cells, nz), (cells, nz)],
        [(5, 2 * nz, nz), (5, cells, nz), pltpu.SemaphoreType.DMA((5,))],
        [edges, far_edges, near_edges, edges_middle, edges_faces, inner],
        out_spec=anywhere,
    )
    return (outs[0].reshape(nx, ny, nz), outs[1].reshape(3, nx, ny, nz), outs[2].reshape(nx, ny, nz))


def solution(mesh):
    return jax.shard_map(
        body,
        mesh=mesh,
        in_specs=(P(None, "gy", "gz"), P(None, None, "gy", "gz"), P(None, "gy", "gz")),
        out_specs=(P(None, "gy", "gz"), P(None, None, "gy", "gz"), P(None, "gy", "gz")),
        check_vma=False,
    )
```
